32 devices in a mesh: groups: 2 (over x), gx: 16 (over z, y, core).
Axes of the slice: x: 2, y: 2, z: 4, core: 2. Of those that a mesh axis runs over, the one named last changes fastest.
Arguments:
- charge: float32 [16, 1048576], P(None, ('groups', 'gx')), parts along dimension 1, may hold values from -6 to 6
- jitter: float32 [3, 1048576], P(None, ('groups', 'gx')), parts along dimension 1, may hold values from -1.5 to 1.5
- basis: float32 [32, 1048576], P(None, ('groups', 'gx')), parts along dimension 1, may hold values from -0.75 to 0.75
- near: int32 [16384, 16], P(('groups', 'gx')), parts along dimension 0, may hold values from 0 to 8191, as said below
- trans0: float32 [16384, 1024], P(('groups', 'gx')), parts along dimension 0, may hold values from -1 to 1
- trans1: float32 [4096, 1024], P(('groups', 'gx')), parts along dimension 0, may hold values from -1 to 1
- trans2: float32 [1024, 1024], P(('groups', 'gx')), parts along dimension 0, may hold values from -1 to 1
- trans3: float32 [256, 1024], P(('groups', 'gx')), parts along dimension 0, may hold values from -1 to 1
- prox1: float32 [4096, 96], P(('groups', 'gx')), parts along dimension 0, may hold values from -0.5 to 0.5
- prox2: float32 [1024, 96], P(('groups', 'gx')), parts along dimension 0, may hold values from -0.5 to 0.5
- prox3: float32 [256, 96], P(('groups', 'gx')), parts along dimension 0, may hold values from -0.5 to 0.5
- prox_top: float32 [64, 96], P('groups'), parts along dimension 0, may hold values from -0.5 to 0.5
- list1: int32 [4096, 3], P(('groups', 'gx')), parts along dimension 0, may hold values from 0 to 2047, as said below
- list2: int32 [1024, 3], P(('groups', 'gx')), parts along dimension 0, may hold values from 0 to 511, as said below
- list3: int32 [256, 3], P(('groups', 'gx')), parts along dimension 0, may hold values from 0 to 127, as said below
- top_of: int32 [256], P('groups'), parts along dimension 0, may hold values from 0 to 31, never falling along the last dimension, each value on 1 to 8 neighbouring positions
Outputs:
- potential: float32 [16, 1048576], P(None, ('groups', 'gx')), parts along dimension 1
The draws below stay inside these ranges and needn't reach their ends.
There are 2 independent parts, one for each index of `groups`. The reference program is written for one: setup_inputs(seed, part) draws one part's arguments, and reference() takes and returns one part's arrays. A program takes and returns all parts, laid end to end along the dimension named above; each array names one. Nothing has to cross between parts.
Inputs may be any that keep to these rules, and one draw needn't show every extreme that they name: `near`: row g starts with g itself; its other entries are distinct leaves at distances 1 to 16 from g. `list1`: row c holds 3 distinct level-1 clusters at distances 2 to 4 from c. `list2`: row c holds 3 distinct level-2 clusters at distances 2 to 4 from c. `list3`: row c holds 3 distinct level-3 clusters at distances 2 to 4 from c. `top_of`: never falls; every top cluster owns 1 to 8 consecutive level-3 clusters, and some top cluster exactly 8.
All inputs are finite; a program needn't handle non-finite values.
Results may differ from the reference program's by a relative error of at most 0.0003.
Values sent between devices are 32-bit elements; how exact they have to be, the bound alone decides.
No kernel may reach another device: no remote copies, remote signals or barrier semaphores. Data moves between devices by JAX's collectives and lax.ppermute only.
A program may use at most 192 MiB of HBM per device.

```python
import math
import jax
import jax.numpy as jnp
import numpy as np
from jax import lax

LEAF = 64
K = 32
R = 16
NB = 16
NREACH = 16
NC = 3
REACH = 4
LEAVES = 8192
PANELS = 524288
C1 = 2048
C2 = 512
C3 = 128
TOP = 32


def nearby_ids(key, row_count, pick_count, nearest, farthest):
    steps_up = jnp.arange(nearest, farthest + 1, dtype=jnp.int32)
    offsets = jnp.concatenate([-steps_up, steps_up])
    candidates = offsets.shape[0]
    anchor = jnp.arange(row_count, dtype=jnp.int32)[:, None]
    targets = anchor + offsets[None, :]
    inside = (targets >= 0) & (targets < row_count)
    column_ids = jnp.arange(candidates, dtype=jnp.int32)[None, :]
    random_part = jax.random.randint(key, (row_count, candidates), 0, 1 << 20, dtype=jnp.int32)
    scores = jnp.where(inside, random_part * candidates + column_ids, -1 - column_ids)
    chosen = lax.top_k(scores, pick_count)[1]
    return jnp.take_along_axis(targets, chosen, axis=1)


def draw_near(key, part):
    key = jax.random.fold_in(key, 11)
    others = nearby_ids(key, LEAVES, NB - 1, 1, NREACH)
    itself = jnp.arange(LEAVES, dtype=jnp.int32)[:, None]
    return jnp.concatenate([itself, others], axis=1)


def draw_list1(key, part):
    key = jax.random.fold_in(key, 12)
    return nearby_ids(key, C1, NC, 2, REACH)


def draw_list2(key, part):
    key = jax.random.fold_in(key, 13)
    return nearby_ids(key, C2, NC, 2, REACH)


def draw_list3(key, part):
    key = jax.random.fold_in(key, 14)
    return nearby_ids(key, C3, NC, 2, REACH)


def level_of(stream_key, shape, pieces, least, high):
    level = 1.0
    for dim, shards_of in pieces:
        draws = jax.random.uniform(jax.random.fold_in(jax.random.fold_in(stream_key, 6), dim), (shards_of,), jnp.float32, least / len(pieces), high / len(pieces))
        level = level * jnp.repeat(jnp.exp(draws), shape[dim] // shards_of).reshape((-1,) + (1,) * (len(shape) - 1 - dim))
    return level


def length_profile(count, total, most, slope):
    weights = [(1 << 20) // math.isqrt(grade ** slope) + 1 for grade in range(2, count + 1)]
    surplus, holding = total - most - (count - 1), [1] * (count - 1)
    while surplus > 0:
        free = [i for i in range(count - 1) if holding[i] < most]
        mass, remaining = sum([weights[i] for i in free]), surplus
        for i in free:
            extra = min(most - holding[i], max(1, remaining * weights[i] // mass), surplus)
            holding[i] = holding[i] + extra
            surplus = surplus - extra
    return np.array([most] + holding)


def uneven(stream_key, number_of, total, limit, slope):
    if number_of == 2:
        one = jax.random.randint(stream_key, (), max(1, total - limit), min(limit, total - 1) + 1)
        return jnp.stack([one, total - one])
    lengths = jnp.asarray(length_profile(number_of, total, limit, slope), jnp.int32)
    couples = (number_of - 1) // 2
    source_of, receiver = lengths[1:1 + 2 * couples:2], lengths[2:2 + 2 * couples:2]
    slack = jnp.minimum(source_of - 1, limit - receiver)
    moved = jax.random.randint(jax.random.fold_in(stream_key, 1), (couples,), 0, 1 << 20) % (slack + 1)
    lengths = lengths.at[1:1 + 2 * couples:2].set(source_of - moved).at[2:2 + 2 * couples:2].set(receiver + moved)
    return lengths[jax.random.permutation(jax.random.fold_in(stream_key, 2), number_of)]


def gaussian(rng, shape, scale, limit, pieces=(), kind=jnp.bfloat16):
    factor_of = level_of(rng, shape, pieces, -0.22, 0.18) if pieces else 1.0
    values = jax.random.normal(rng, shape, jnp.float32) * scale * factor_of
    return jnp.minimum(jnp.maximum(values, -limit), limit).astype(kind)


def setup_inputs(seed: int = 0, part: int = 0) -> dict:
    key_of = jax.random.split(jax.random.key(seed), 17)
    own_keys = jax.random.split(jax.random.fold_in(key_of[16], part), 17)
    charge = gaussian(own_keys[0], (R, PANELS), 1.0, 6.0, ((1, 16),), jnp.float32)
    jitter = jnp.clip(jax.random.uniform(own_keys[1], (3, PANELS), jnp.float32, -1.5, 1.5) * level_of(own_keys[1], (3, PANELS), ((1, 16),), -0.4, 0.0), -1.5, 1.5)
    basis = gaussian(own_keys[2], (K, PANELS), LEAF ** -0.5, 0.75, ((1, 16),), jnp.float32)
    near = draw_near(jax.random.fold_in(jax.random.fold_in(key_of[16], part), 71), part)
    trans0 = gaussian(own_keys[4], (LEAVES, K * K), K ** -0.5, 1.0, ((0, 16),), jnp.float32)
    trans1 = gaussian(own_keys[5], (C1, K * K), K ** -0.5, 1.0, ((0, 16),), jnp.float32)
    trans2 = gaussian(own_keys[6], (C2, K * K), K ** -0.5, 1.0, ((0, 16),), jnp.float32)
    trans3 = gaussian(own_keys[7], (C3, K * K), K ** -0.5, 1.0, ((0, 16),), jnp.float32)
    prox1 = jnp.clip(jax.random.uniform(own_keys[8], (C1, 3 * K), jnp.float32, -0.5, 0.5) * level_of(own_keys[8], (C1, 3 * K), ((0, 16),), -0.4, 0.0), -0.5, 0.5)
    prox2 = jnp.clip(jax.random.uniform(own_keys[9], (C2, 3 * K), jnp.float32, -0.5, 0.5) * level_of(own_keys[9], (C2, 3 * K), ((0, 16),), -0.4, 0.0), -0.5, 0.5)
    prox3 = jnp.clip(jax.random.uniform(own_keys[10], (C3, 3 * K), jnp.float32, -0.5, 0.5) * level_of(own_keys[10], (C3, 3 * K), ((0, 16),), -0.4, 0.0), -0.5, 0.5)
    prox_top = jnp.clip(jax.random.uniform(own_keys[11], (TOP, 3 * K), jnp.float32, -0.5, 0.5), -0.5, 0.5)
    list1 = draw_list1(jax.random.fold_in(jax.random.fold_in(key_of[16], part), 71), part)
    list2 = draw_list2(jax.random.fold_in(jax.random.fold_in(key_of[16], part), 71), part)
    list3 = draw_list3(jax.random.fold_in(jax.random.fold_in(key_of[16], part), 71), part)
    top_of = jnp.searchsorted(jnp.cumsum(uneven(own_keys[15], TOP, C3, 8, 0)), jnp.arange(C3), side="right").astype(jnp.int32)
    return dict(charge=charge, jitter=jitter, basis=basis, near=near, trans0=trans0, trans1=trans1, trans2=trans2, trans3=trans3, prox1=prox1, prox2=prox2, prox3=prox3, prox_top=prox_top, list1=list1, list2=list2, list3=list3, top_of=top_of)


inv_four_pi = 0.07957747154594767
soft_square = 0.01
row_columns = 64
highest = lax.Precision.HIGHEST

def green(targets, sources):
    square = None
    for axis_id in range(3):
        spread = targets[..., axis_id, :, None] - sources[..., axis_id, None, :]
        square = spread * spread if square is None else square + spread * spread
    return inv_four_pi * lax.rsqrt(square + soft_square)

def cluster_centre(cluster_ids, level_width):
    first_column = cluster_ids * level_width
    row_number = first_column // row_columns
    row_offset = first_column % row_columns
    middle = row_offset.astype(jnp.float32) + 0.5 * (level_width - 1)
    flipped = row_columns - 1 - middle
    across = jnp.where(row_number % 2 == 0, middle, flipped)
    beside = 4.0 * row_number.astype(jnp.float32) + 1.5
    return (across, beside)

def panel_points(jitter, first_leaf):
    panel_count = jitter.shape[1]
    leaf_ids = first_leaf + jnp.arange(panel_count, dtype=jnp.int32) // LEAF
    across, beside = cluster_centre(leaf_ids // 4, 1)
    beside = beside - 1.5 + (leaf_ids % 4).astype(jnp.float32)
    return jnp.stack([across, beside, jnp.zeros_like(across)]) + jitter

def proxy_points(offsets, level, first_cluster):
    cluster_count = offsets.shape[0]
    level_width = 4 ** (level - 1)
    cluster_ids = first_cluster + jnp.arange(cluster_count, dtype=jnp.int32)
    across, beside = cluster_centre(cluster_ids, level_width)
    centre = jnp.stack([across, beside, jnp.zeros_like(across)], axis=1)
    extent = jnp.array([float(level_width), 4.0, 1.0], jnp.float32)
    return centre[:, :, None] + extent[None, :, None] * offsets.reshape(cluster_count, 3, -1)

def leaf_moments(basis, charge):
    leaf_count = basis.shape[1] // LEAF
    shaped_basis = basis.reshape(basis.shape[0], leaf_count, LEAF)
    shaped_charge = charge.reshape(charge.shape[0], leaf_count, LEAF)
    return jnp.einsum('klp,rlp->lkr', shaped_basis, shaped_charge, precision=highest)

def lift(trans, moments):
    return jnp.einsum('cab,cbr->car', trans.reshape(-1, K, K), moments, precision=highest)

def upward(trans, moments):
    return lift(trans, moments).reshape(-1, 4, K, R).sum(axis=1)

def descend(trans, parent_local):
    return jnp.einsum('cab,car->cbr', trans.reshape(-1, K, K), parent_local, precision=highest)

def couple(targets, sources, moments):
    return jnp.einsum('cjab,cjbr->car', green(targets[:, None], sources), moments, precision=highest)

def near_potential(source_points, source_charge, near_ids, target_points, group):
    leaf_count = near_ids.shape[0]
    block_count = leaf_count // group
    shaped_points = source_points.reshape(3, -1, LEAF)
    shaped_charge = source_charge.reshape(source_charge.shape[0], -1, LEAF)
    target_blocks = target_points.reshape(3, block_count, group, LEAF).transpose(1, 0, 2, 3)
    id_blocks = near_ids.reshape(block_count, group, near_ids.shape[1])

    def block_term(inputs):
        target_block, id_block = inputs
        source_place = jnp.take(shaped_points, id_block, axis=1)
        source_values = jnp.take(shaped_charge, id_block, axis=1)
        square = None
        for axis_id in range(3):
            spread = target_block[axis_id][:, :, None, None] - source_place[axis_id][:, None, :, :]
            square = spread * spread if square is None else square + spread * spread
        kernel = inv_four_pi * lax.rsqrt(square + soft_square)
        return jnp.einsum('gpjq,rgjq->rgp', kernel, source_values, precision=highest)
    blocks = lax.map(block_term, (target_blocks, id_blocks))
    return blocks.transpose(1, 0, 2, 3).reshape(source_charge.shape[0], leaf_count * LEAF)

def far_potential(basis, local_leaf):
    leaf_count = local_leaf.shape[0]
    shaped = basis.reshape(K, leaf_count, LEAF)
    return jnp.einsum('klp,lkr->rlp', shaped, local_leaf, precision=highest).reshape(R, leaf_count * LEAF)

def reference(charge, jitter, basis, near, trans0, trans1, trans2, trans3, prox1, prox2, prox3, prox_top, list1, list2, list3, top_of):
    points = panel_points(jitter, 0)
    near_field = near_potential(points, charge, near, points, 256)
    coef0 = leaf_moments(basis, charge)
    coef1 = upward(trans0, coef0)
    coef2 = upward(trans1, coef1)
    coef3 = upward(trans2, coef2)
    lifted = lift(trans3, coef3)
    top_count = prox_top.shape[0]
    top_ids = jnp.arange(top_count, dtype=jnp.int32)
    member = (top_of[:, None] == top_ids[None, :]).astype(jnp.float32)
    coef_top = jnp.einsum('ct,cab->tab', member, lifted, precision=highest)
    place_top = proxy_points(prox_top, 4, 0)
    separated = (jnp.abs(top_ids[:, None] - top_ids[None, :]) >= 2).astype(jnp.float32)
    kernel_top = green(place_top[:, None], place_top[None, :]) * separated[:, :, None, None]
    local_top = jnp.einsum('tuab,ubr->tar', kernel_top, coef_top, precision=highest)
    place3 = proxy_points(prox3, 3, 0)
    local3 = couple(place3, place3[list3], coef3[list3]) + descend(trans3, local_top[top_of])
    place2 = proxy_points(prox2, 2, 0)
    local2 = couple(place2, place2[list2], coef2[list2]) + descend(trans2, jnp.repeat(local3, 4, axis=0))
    place1 = proxy_points(prox1, 1, 0)
    local1 = couple(place1, place1[list1], coef1[list1]) + descend(trans1, jnp.repeat(local2, 4, axis=0))
    local_leaf = descend(trans0, jnp.repeat(local1, 4, axis=0))
    return near_field + far_potential(basis, local_leaf)
```

```python
import jax
import jax.numpy as jnp
from jax import lax
from jax.experimental import pallas as pl
from jax.experimental.pallas import tpu as pltpu
from jax.sharding import PartitionSpec as P

LEAF = 64
K = 32
R = 16
NREACH = 16
REACH = 4


inv_four_pi = 0.07957747154594767
soft_square = 0.01
row_columns = 64
highest = lax.Precision.HIGHEST


def padded(block, sides, width):
    for axis, dim in sides:
        count = lax.axis_size(axis)
        forward = [(i, i + 1) for i in range(count - 1)]
        backward = [(target, source) for source, target in forward]
        low = lax.ppermute(
            lax.slice_in_dim(block, block.shape[dim] - width, None, axis=dim), axis, forward
        )
        high = lax.ppermute(lax.slice_in_dim(block, 0, width, axis=dim), axis, backward)
        block = jnp.concatenate([low, block, high], axis=dim)
    return block


def leaf_halos(points, charge):
    count = lax.axis_size("gx")
    forward = [(i, i + 1) for i in range(count - 1)]
    backward = [(target, source) for source, target in forward]
    width = NREACH * LEAF
    last = jnp.concatenate([points[:, -width:], charge[:, -width:]], axis=0)
    first = jnp.concatenate([points[:, :width], charge[:, :width]], axis=0)
    return lax.ppermute(last, "gx", forward), lax.ppermute(first, "gx", backward)


def green(targets, sources):
    square = None
    for axis_id in range(3):
        spread = targets[..., axis_id, :, None] - sources[..., axis_id, None, :]
        square = spread * spread if square is None else square + spread * spread
    return inv_four_pi * lax.rsqrt(square + soft_square)


def cluster_centre(cluster_ids, level_width):
    first_column = cluster_ids * level_width
    row_number = first_column // row_columns
    row_offset = first_column % row_columns
    middle = row_offset.astype(jnp.float32) + 0.5 * (level_width - 1)
    flipped = row_columns - 1 - middle
    across = jnp.where(row_number % 2 == 0, middle, flipped)
    beside = 4.0 * row_number.astype(jnp.float32) + 1.5
    return (across, beside)


def panel_points(jitter, first_leaf):
    panel_count = jitter.shape[1]
    leaf_ids = first_leaf + jnp.arange(panel_count, dtype=jnp.int32) // LEAF
    across, beside = cluster_centre(leaf_ids // 4, 1)
    beside = beside - 1.5 + (leaf_ids % 4).astype(jnp.float32)
    return jnp.stack([across, beside, jnp.zeros_like(across)]) + jitter


def proxy_points(offsets, level, first_cluster):
    cluster_count = offsets.shape[0]
    level_width = 4 ** (level - 1)
    cluster_ids = first_cluster + jnp.arange(cluster_count, dtype=jnp.int32)
    across, beside = cluster_centre(cluster_ids, level_width)
    centre = jnp.stack([across, beside, jnp.zeros_like(across)], axis=1)
    extent = jnp.array([float(level_width), 4.0, 1.0], jnp.float32)
    return centre[:, :, None] + extent[None, :, None] * offsets.reshape(cluster_count, 3, -1)


def leaf_moments(basis, charge):
    leaf_count = basis.shape[1] // LEAF
    shaped_basis = basis.reshape(basis.shape[0], leaf_count, LEAF)
    shaped_charge = charge.reshape(charge.shape[0], leaf_count, LEAF)
    return jnp.einsum("klp,rlp->lkr", shaped_basis, shaped_charge, precision=highest)


def lift(trans, moments):
    return jnp.einsum("cab,cbr->car", trans.reshape(-1, K, K), moments, precision=highest)


def upward(trans, moments):
    return lift(trans, moments).reshape(-1, 4, K, R).sum(axis=1)


def descend(trans, parent_local):
    return jnp.einsum("cab,car->cbr", trans.reshape(-1, K, K), parent_local, precision=highest)


def couple(targets, sources, moments):
    return jnp.einsum(
        "cjab,cjbr->car", green(targets[:, None], sources), moments, precision=highest
    )


GROUP = 16
BATCH = 8
bf16 = jnp.bfloat16
f32 = jnp.float32


def split_two(value):
    high = value.astype(bf16)
    return high, (value - high.astype(f32)).astype(bf16)


def split_three(value):
    first = value.astype(bf16).astype(f32)
    rest = value - first
    second = rest.astype(bf16).astype(f32)
    return first, second, rest - second


def lanes_of(tile):
    return pl.ds(pl.multiple_of(tile * 128, 128), 128)


def near_kernel(
    ids, origin, own_points, own_charge, low_halo, high_halo, out, points, feats, charges, targets, kernels, weights
):
    halo_tiles = low_halo.shape[1] // 128
    own_tiles = own_points.shape[1] // 128
    left_half = lax.broadcasted_iota(jnp.int32, (32, 128), 1).astype(bf16) < 64
    row = lax.broadcasted_iota(jnp.int32, (8, 128), 0)
    is_three = row == 3
    is_four = row == 4
    below_five = row < 5
    one_three = jnp.where(is_three, 1.0, 0.0)
    one_four = jnp.where(is_four, 1.0, 0.0)

    def stage(tile, place, charge):
        points[:, lanes_of(tile)] = jnp.concatenate([place, jnp.zeros((5, 128), f32)], 0)
        charge = charge * inv_four_pi
        charges[2 * tile] = jnp.concatenate(split_two(charge), 0)
        charges[2 * tile + 1] = jnp.concatenate(split_two(pltpu.roll(charge, 64, 1)), 0)

    def stage_halo(halo, first):
        def step(i, carry):
            stage(first + i, halo[0:3, lanes_of(i)], halo[3:19, lanes_of(i)])
            return carry

        lax.fori_loop(0, halo_tiles, step, 0, unroll=2)

    def stage_own(i, carry):
        stage(halo_tiles + i, own_points[:, lanes_of(i)], own_charge[:, lanes_of(i)])
        return carry

    stage_halo(low_halo, 0)
    stage_halo(high_halo, halo_tiles + own_tiles)
    lax.fori_loop(0, own_tiles, stage_own, 0, unroll=4)

    def back(slot):
        total = lax.dot_general(
            kernels[slot], weights[slot], (((1,), (1,)), ((), ())), preferred_element_type=f32
        )
        total = jnp.transpose(total[:LEAF] + total[LEAF:])
        return total[:R] + total[R:]

    def emit(first):
        parts = [back(slot) for slot in range(BATCH)]
        first = jnp.maximum(first, 0)
        for half in range(BATCH // 2):
            place = pl.ds(pl.multiple_of((first + 2 * half) * LEAF, 128), 128)
            out[:, place] = jnp.concatenate([parts[2 * half], parts[2 * half + 1]], 1)

    def do_group(group, carry):
        base = group * GROUP
        shift = jnp.where(row == 0, origin[2 * group], jnp.where(row == 1, origin[2 * group + 1], 0.0))

        def local(tile):
            place = points[:, lanes_of(tile)] - shift
            square = place * place
            return place, jnp.broadcast_to(square[0:1] + square[1:2] + square[2:3], (8, 128))

        def source_rows(i, carry):
            place, square = local(base // 2 + i)
            rows = place * (-2.0) + jnp.where(is_three, square + soft_square, one_four)

            def put(entry, value):
                first, second, third = split_three(value)
                one = jnp.where(below_five, first, pltpu.roll(second, 5, 0))
                two = jnp.where(is_three, second, one)
                three = jnp.where(below_five, third + one_four, pltpu.roll(first, 5, 0))
                feats[entry] = jnp.concatenate([one, two, three, jnp.zeros_like(one)], 0).astype(bf16)

            put(2 * i, rows)
            put(2 * i + 1, pltpu.roll(rows, 64, 1))
            return carry

        def target_rows(i, carry):
            place, square = local(base // 2 + NREACH // 2 + i)
            first, second, third = split_three(place + jnp.where(is_four, square, one_three))
            one = jnp.where(below_five, first, pltpu.roll(first, 5, 0))
            two = jnp.where(below_five, second + one_three, pltpu.roll(second, 5, 0))
            three = jnp.where(below_five, jnp.where(is_four, third, first), pltpu.roll(third, 5, 0))
            rows = jnp.concatenate([one, two, three, jnp.zeros_like(one)], 0)
            targets[lanes_of(i), :] = jnp.transpose(rows).astype(bf16)
            return carry

        lax.fori_loop(0, (GROUP + 2 * NREACH) // 2, source_rows, 0, unroll=True)
        lax.fori_loop(0, GROUP // 2, target_rows, 0, unroll=True)

        def front(leaf, slot):
            target = targets[pl.ds(pl.multiple_of(leaf * LEAF, LEAF), LEAF), :]
            entry = (base + leaf) * 16
            for j in range(4):
                sides = []
                for h in range(2):
                    one = ids[entry + 4 * j + 2 * h]
                    two = ids[entry + 4 * j + 2 * h + 1] ^ 1
                    sides.append(jnp.where(left_half, feats[one - base], feats[two - base]))
                    weights[slot, :, (2 * j + h) * 128 : (2 * j + h + 1) * 128] = jnp.where(
                        left_half, charges[one], charges[two]
                    )
                square = jnp.dot(target, jnp.concatenate(sides, 1), preferred_element_type=f32)
                high, low = split_two(lax.rsqrt(square))
                kernels[slot, 0:LEAF, j * 256 : (j + 1) * 256] = high
                kernels[slot, LEAF : 2 * LEAF, j * 256 : (j + 1) * 256] = low

        def step(i, carry):
            emit(base + BATCH * i - BATCH)
            for slot in range(BATCH):
                front(BATCH * i + slot, slot)
            return carry

        lax.fori_loop(0, GROUP // BATCH, step, 0)
        return carry

    kernels[...] = jnp.zeros_like(kernels)
    weights[...] = jnp.zeros_like(weights)
    lax.fori_loop(0, own_tiles * 2 // GROUP, do_group, 0)
    emit(own_tiles * 2 - BATCH)


def near_potential(ids, origin, own_points, own_charge, low_halo, high_halo):
    panels = own_points.shape[1]
    leaves = (panels + 2 * low_halo.shape[1]) // LEAF
    pairs = panels * 16 * LEAF
    vmem = pl.BlockSpec(memory_space=pltpu.VMEM)
    smem = pl.BlockSpec(memory_space=pltpu.SMEM)
    return pl.pallas_call(
        near_kernel,
        out_shape=jax.ShapeDtypeStruct((R, panels), f32),
        in_specs=[smem, smem, vmem, vmem, vmem, vmem],
        out_specs=vmem,
        scratch_shapes=[
            pltpu.VMEM((8, leaves * LEAF), f32),
            pltpu.VMEM((GROUP + 2 * NREACH, 32, 128), bf16),
            pltpu.VMEM((leaves, 2 * R, 128), bf16),
            pltpu.VMEM((GROUP * LEAF, 32), bf16),
            pltpu.VMEM((BATCH, 2 * LEAF, 16 * LEAF), bf16),
            pltpu.VMEM((BATCH, 2 * R, 16 * LEAF), bf16),
        ],
        compiler_params=pltpu.CompilerParams(vmem_limit_bytes=40 * 2**20),
        cost_estimate=pl.CostEstimate(
            flops=pairs * 192, bytes_accessed=panels * 160, transcendentals=pairs
        ),
        name="near_potential",
    )(ids, origin, own_points, own_charge, low_halo, high_halo)


def far_potential(basis, local_leaf):
    leaf_count = local_leaf.shape[0]
    shaped = basis.reshape(K, leaf_count, LEAF)
    return jnp.einsum("klp,lkr->rlp", shaped, local_leaf, precision=highest).reshape(
        R, leaf_count * LEAF
    )


def make_payload(moments, places):
    cluster_count = moments.shape[0]
    return jnp.concatenate(
        [moments.reshape(cluster_count, K * R), places.reshape(cluster_count, 3 * K)], axis=1
    )


def couple_level(extended, payload, partners, first_cluster):
    cluster_count = payload.shape[0]
    row_ids = partners - (first_cluster - REACH)
    picked = extended[row_ids]
    moments = picked[..., : K * R].reshape(cluster_count, partners.shape[1], K, R)
    sources = picked[..., K * R :].reshape(cluster_count, partners.shape[1], 3, K)
    targets = payload[:, K * R :].reshape(cluster_count, 3, K)
    return couple(targets, sources, moments)


def body(
    charge,
    jitter,
    basis,
    near,
    trans0,
    trans1,
    trans2,
    trans3,
    prox1,
    prox2,
    prox3,
    prox_top,
    list1,
    list2,
    list3,
    top_of,
):
    here = lax.axis_index("gx")
    leaf_count = near.shape[0]
    count_one = prox1.shape[0]
    count_two = prox2.shape[0]
    count_three = prox3.shape[0]
    points = panel_points(jitter, here * leaf_count)
    low_halo, high_halo = leaf_halos(points, charge)
    coef0 = leaf_moments(basis, charge)
    coef1 = upward(trans0, coef0)
    coef2 = upward(trans1, coef1)
    coef3 = upward(trans2, coef2)
    lifted_flat = lift(trans3, coef3).reshape(count_three, K * R)
    payload_one = make_payload(coef1, proxy_points(prox1, 1, here * count_one))
    payload_two = make_payload(coef2, proxy_points(prox2, 2, here * count_two))
    payload_three = make_payload(coef3, proxy_points(prox3, 3, here * count_three))
    extended_one = padded(payload_one, (("gx", 0),), REACH)
    extended_two = padded(payload_two, (("gx", 0),), REACH)
    extended_three = padded(payload_three, (("gx", 0),), REACH)
    top_count = prox_top.shape[0]
    top_ids = jnp.arange(top_count, dtype=jnp.int32)
    my_tops = lax.dynamic_slice_in_dim(top_of, here * count_three, count_three)
    place_top = proxy_points(prox_top, 4, 0)
    member = (my_tops[:, None] == top_ids[None, :]).astype(jnp.float32)
    terms = jnp.einsum("ct,cq->tq", member, lifted_flat, precision=highest)
    coef_top = lax.psum(terms, "gx")
    separated = (jnp.abs(my_tops[:, None] - top_ids[None, :]) >= 2).astype(jnp.float32)
    kernel_top = (
        green(place_top[my_tops][:, None], place_top[None, :]) * separated[:, :, None, None]
    )
    local_top = jnp.einsum(
        "cuab,ubr->car", kernel_top, coef_top.reshape(top_count, K, R), precision=highest
    )
    local3 = couple_level(extended_three, payload_three, list3, here * count_three) + descend(
        trans3, local_top
    )
    local2 = couple_level(extended_two, payload_two, list2, here * count_two) + descend(
        trans2, jnp.repeat(local3, 4, axis=0)
    )
    local1 = couple_level(extended_one, payload_one, list1, here * count_one) + descend(
        trans1, jnp.repeat(local2, 4, axis=0)
    )
    local_leaf = descend(trans0, jnp.repeat(local1, 4, axis=0))
    far_field = far_potential(basis, local_leaf)
    near_ids = (near - (here * leaf_count - NREACH)).reshape(-1)
    group_count = leaf_count // GROUP
    group_ids = here * group_count + jnp.arange(group_count, dtype=jnp.int32)
    origin = jnp.stack(cluster_centre(group_ids, GROUP // 4), axis=1).reshape(-1)
    near_field = near_potential(near_ids, origin, points, charge, low_halo, high_halo)
    return near_field + far_field


def solution(mesh):
    placed = (
        P(None, ("groups", "gx")),
        P(None, ("groups", "gx")),
        P(None, ("groups", "gx")),
        P(("groups", "gx"), None),
        P(("groups", "gx"), None),
        P(("groups", "gx"), None),
        P(("groups", "gx"), None),
        P(("groups", "gx"), None),
        P(("groups", "gx"), None),
        P(("groups", "gx"), None),
        P(("groups", "gx"), None),
        P("groups", None),
        P(("groups", "gx"), None),
        P(("groups", "gx"), None),
        P(("groups", "gx"), None),
        P("groups"),
    )
    return jax.shard_map(
        body, mesh=mesh, in_specs=placed, out_specs=P(None, ("groups", "gx")), check_vma=False
    )
```

```python
import jax
import jax.numpy as jnp
from jax import lax
from jax.experimental import pallas as pl
from jax.experimental.pallas import tpu as pltpu
from jax.sharding import PartitionSpec as P

LEAF = 64
K = 32
R = 16
NREACH = 16


inv_four_pi = 0.07957747154594767
soft_square = 0.01
row_columns = 64


def leaf_halos(jitter, charge):
    count = lax.axis_size("gx")
    forward = [(i, i + 1) for i in range(count - 1)]
    backward = [(target, source) for source, target in forward]
    width = NREACH * LEAF
    last = jnp.concatenate([jitter[:, -width:], charge[:, -width:]], axis=0)
    first = jnp.concatenate([jitter[:, :width], charge[:, :width]], axis=0)
    return lax.ppermute(last, "gx", forward), lax.ppermute(first, "gx", backward)


def column_place(column):
    row_number = column >> 6
    middle = column & (row_columns - 1)
    across = jnp.where((row_number & 1) == 0, middle, row_columns - 1 - middle)
    return across.astype(jnp.float32), (4 * row_number).astype(jnp.float32)


GROUP = 16
BATCH = 8
bf16 = jnp.bfloat16
f32 = jnp.float32


def split_two(value):
    high = value.astype(bf16)
    return high, (value - high.astype(f32)).astype(bf16)


def split_three(value):
    first = value.astype(bf16).astype(f32)
    rest = value - first
    second = rest.astype(bf16).astype(f32)
    return first, second, rest - second


def lanes_of(tile):
    return pl.ds(pl.multiple_of(tile * 128, 128), 128)


def near_kernel(
    ids, own_jitter, own_charge, low_halo, high_halo, out, points, feats, charges, targets, kernels, weights
):
    halo_tiles = low_halo.shape[1] // 128
    own_tiles = own_jitter.shape[1] // 128
    here = lax.axis_index("gx")
    first_id = here * (2 * own_tiles) - NREACH
    high_side = jnp.where(lax.broadcasted_iota(jnp.int32, (1, 128), 1) < LEAF, 0.0, 1.0)
    left_half = lax.broadcasted_iota(jnp.int32, (32, 128), 1).astype(bf16) < 64
    row = lax.broadcasted_iota(jnp.int32, (8, 128), 0)
    is_three = row == 3
    is_four = row == 4
    below_five = row < 5
    one_three = jnp.where(is_three, 1.0, 0.0)
    one_four = jnp.where(is_four, 1.0, 0.0)

    def stage(tile, place, charge):
        number = tile + (here * own_tiles - halo_tiles)
        across, beside = column_place(number >> 1)
        beside = beside + (2 * (number & 1)).astype(f32)
        points[0:1, lanes_of(tile)] = across + place[0:1]
        points[1:2, lanes_of(tile)] = (beside + high_side) + place[1:2]
        points[2:3, lanes_of(tile)] = place[2:3]
        points[3:8, lanes_of(tile)] = jnp.zeros((5, 128), f32)
        charge = charge * inv_four_pi
        charges[2 * tile] = jnp.concatenate(split_two(charge), 0)
        charges[2 * tile + 1] = jnp.concatenate(split_two(pltpu.roll(charge, 64, 1)), 0)

    def stage_halo(halo, first):
        def step(i, carry):
            stage(first + i, halo[0:3, lanes_of(i)], halo[3:19, lanes_of(i)])
            return carry

        lax.fori_loop(0, halo_tiles, step, 0, unroll=2)

    def stage_own(i, carry):
        stage(halo_tiles + i, own_jitter[:, lanes_of(i)], own_charge[:, lanes_of(i)])
        return carry

    stage_halo(low_halo, 0)
    stage_halo(high_halo, halo_tiles + own_tiles)
    lax.fori_loop(0, own_tiles, stage_own, 0, unroll=4)

    def back(slot):
        total = lax.dot_general(
            kernels[slot], weights[slot], (((1,), (1,)), ((), ())), preferred_element_type=f32
        )
        total = jnp.transpose(total[:LEAF] + total[LEAF:])
        return total[:R] + total[R:]

    def emit(first):
        parts = [back(slot) for slot in range(BATCH)]
        first = jnp.maximum(first, 0)
        for half in range(BATCH // 2):
            place = pl.ds(pl.multiple_of((first + 2 * half) * LEAF, 128), 128)
            out[:, place] = jnp.concatenate([parts[2 * half], parts[2 * half + 1]], 1)

    def do_group(group, carry):
        base = group * GROUP
        across, beside = column_place(((first_id + NREACH) >> 2) + group * (GROUP // 4))
        row_sign = jnp.where(((first_id + NREACH + base) >> 8) % 2 == 0, 1.5, -1.5)
        shift = jnp.where(row == 0, across + row_sign, jnp.where(row == 1, beside + 1.5, 0.0))

        def local(tile):
            place = points[:, lanes_of(tile)] - shift
            square = place * place
            return place, jnp.broadcast_to(square[0:1] + square[1:2] + square[2:3], (8, 128))

        def source_rows(i, carry):
            place, square = local(base // 2 + i)
            rows = place * (-2.0) + jnp.where(is_three, square + soft_square, one_four)

            def put(entry, value):
                first, second, third = split_three(value)
                one = jnp.where(below_five, first, pltpu.roll(second, 5, 0))
                two = jnp.where(is_three, second, one)
                three = jnp.where(below_five, third + one_four, pltpu.roll(first, 5, 0))
                feats[entry] = jnp.concatenate([one, two, three, jnp.zeros_like(one)], 0).astype(bf16)

            put(2 * i, rows)
            put(2 * i + 1, pltpu.roll(rows, 64, 1))
            return carry

        def target_rows(i, carry):
            place, square = local(base // 2 + NREACH // 2 + i)
            first, second, third = split_three(place + jnp.where(is_four, square, one_three))
            one = jnp.where(below_five, first, pltpu.roll(first, 5, 0))
            two = jnp.where(below_five, second + one_three, pltpu.roll(second, 5, 0))
            three = jnp.where(below_five, jnp.where(is_four, third, first), pltpu.roll(third, 5, 0))
            rows = jnp.concatenate([one, two, three, jnp.zeros_like(one)], 0)
            targets[lanes_of(i), :] = jnp.transpose(rows).astype(bf16)
            return carry

        lax.fori_loop(0, (GROUP + 2 * NREACH) // 2, source_rows, 0, unroll=True)
        lax.fori_loop(0, GROUP // 2, target_rows, 0, unroll=True)

        def front(leaf, slot):
            target = targets[pl.ds(pl.multiple_of(leaf * LEAF, LEAF), LEAF), :]
            entry = base + leaf
            for j in range(4):
                sides = []
                for h in range(2):
                    one = ids[4 * j + 2 * h, entry] - first_id
                    two = (ids[4 * j + 2 * h + 1, entry] - first_id) ^ 1
                    sides.append(jnp.where(left_half, feats[one - base], feats[two - base]))
                    weights[slot, :, (2 * j + h) * 128 : (2 * j + h + 1) * 128] = jnp.where(
                        left_half, charges[one], charges[two]
                    )
                square = jnp.dot(target, jnp.concatenate(sides, 1), preferred_element_type=f32)
                high, low = split_two(lax.rsqrt(square))
                kernels[slot, 0:LEAF, j * 256 : (j + 1) * 256] = high
                kernels[slot, LEAF : 2 * LEAF, j * 256 : (j + 1) * 256] = low

        def step(i, carry):
            emit(base + BATCH * i - BATCH)
            for slot in range(BATCH):
                front(BATCH * i + slot, slot)
            return carry

        lax.fori_loop(0, GROUP // BATCH, step, 0)
        return carry

    kernels[...] = jnp.zeros_like(kernels)
    weights[...] = jnp.zeros_like(weights)
    lax.fori_loop(0, own_tiles * 2 // GROUP, do_group, 0)
    emit(own_tiles * 2 - BATCH)


def near_potential(ids, own_jitter, own_charge, low_halo, high_halo):
    panels = own_jitter.shape[1]
    leaves = (panels + 2 * low_halo.shape[1]) // LEAF
    pairs = panels * 16 * LEAF
    vmem = pl.BlockSpec(memory_space=pltpu.VMEM)
    smem = pl.BlockSpec(memory_space=pltpu.SMEM)
    return pl.pallas_call(
        near_kernel,
        out_shape=jax.ShapeDtypeStruct((R, panels), f32),
        in_specs=[smem, vmem, vmem, vmem, vmem],
        out_specs=vmem,
        scratch_shapes=[
            pltpu.VMEM((8, leaves * LEAF), f32),
            pltpu.VMEM((GROUP + 2 * NREACH, 32, 128), bf16),
            pltpu.VMEM((leaves, 2 * R, 128), bf16),
            pltpu.VMEM((GROUP * LEAF, 32), bf16),
            pltpu.VMEM((BATCH, 2 * LEAF, 16 * LEAF), bf16),
            pltpu.VMEM((BATCH, 2 * R, 16 * LEAF), bf16),
        ],
        compiler_params=pltpu.CompilerParams(vmem_limit_bytes=40 * 2**20),
        cost_estimate=pl.CostEstimate(
            flops=pairs * 192, bytes_accessed=panels * 160, transcendentals=pairs
        ),
        name="near_potential",
    )(ids, own_jitter, own_charge, low_halo, high_halo)


EDGE = 16
ROWS = R * K
WIDE = ROWS + 3 * K


def lane_digits(shape, dim):
    index = lax.broadcasted_iota(jnp.int32, shape, dim)
    return index >> 5, (index >> 3) & 3, index & 7


def matvec(matrix, vector, out, add):
    for_rows = 4

    def step(block, carry):
        start = pl.multiple_of(block * for_rows * K, for_rows * K)
        sums = [jnp.zeros((K, 128), f32) for _ in range(for_rows)]
        for column in range(K):
            values = matrix(column)
            for i in range(for_rows):
                sums[i] = sums[i] + values * vector[pl.ds(start + i * K + column, 1), :]
        for i in range(for_rows):
            place = pl.ds(start + i * K, K)
            out[place, :] = out[place, :] + sums[i] if add else sums[i]
        return carry

    lax.fori_loop(0, R // for_rows, step, 0)


def fold(ref, shifts):
    def step(i, carry):
        place = pl.ds(pl.multiple_of(i * 64, 64), 64)
        value = ref[place, :]
        for shift in shifts:
            value = value + pltpu.roll(value, shift, 1)
        ref[place, :] = value
        return carry

    lax.fori_loop(0, ROWS // 64, step, 0)


def centre_lanes(ids, level_width):
    first = ids * level_width
    row_number = first >> 6
    middle = (first & (row_columns - 1)).astype(f32) + 0.5 * (level_width - 1)
    across = jnp.where((row_number & 1) == 0, middle, row_columns - 1 - middle)
    return across, 4.0 * row_number.astype(f32) + 1.5


def up_kernel(
    tops, basis, charge, trans0, trans1, trans2, trans3, prox1, prox2, prox3,
    et, payload, last_out, first_out, terms, leaf_rows, coef0, coef, flipped, columns,
):
    here = lax.axis_index("gx")
    quarter = lax.broadcasted_iota(jnp.int32, (R, 256), 1).astype(f32)

    def moments(tile, carry):
        lanes = pl.ds(pl.multiple_of(tile * 256, 256), 256)
        high, low = split_two(basis[:, lanes])
        right = jnp.concatenate([high, low, high], 1)
        value = charge[:, lanes]
        pieces = [
            split_two(jnp.where((quarter >= 64.0 * i) & (quarter < 64.0 * (i + 1)), value, 0.0))
            for i in range(4)
        ]
        highs = jnp.concatenate([p[0] for p in pieces], 0)
        lows = jnp.concatenate([p[1] for p in pieces], 0)
        left = jnp.concatenate([highs, highs, lows], 1)
        leaf_rows[pl.ds(pl.multiple_of(tile * 64, 64), 64), 0:K] = lax.dot_general(
            left, right, (((1,), (1,)), ((), ())), preferred_element_type=f32
        )
        return carry

    lax.fori_loop(0, basis.shape[1] // 256, moments, 0, unroll=4)

    def leaf_coefs(r, carry):
        place = pl.ds(pl.multiple_of(r * K, K), K)
        for j0 in range(4):
            parts = [
                leaf_rows[pl.ds((j2 * 16 + j1 * 4 + j0) * R + r, 8, stride=64 * R), :]
                for j1 in range(4)
                for j2 in range(4)
            ]
            coef0[j0, place, :] = jnp.transpose(jnp.concatenate(parts, 0))[0:K]
        return carry

    lax.fori_loop(0, R, leaf_coefs, 0, unroll=2)

    def digits_first(q, rows):
        parts = [
            columns[q, pl.ds(rows[0] * a + rows[1] * b + rows[2], 8, stride=rows[3]), :]
            for a in range(4)
            for b in range(4)
        ]
        return jnp.transpose(jnp.concatenate(parts, 0))

    def flip(source, entries):
        for q in range(8):
            columns[q, 0 : source.shape[0], :] = source[:, q * 128 : (q + 1) * 128]
        for q in range(8):
            for entry, rows in entries:
                et[entry, q * 128 : (q + 1) * 128, :] = digits_first(q, rows)

    flip(trans0, [(j0, (4, 16, j0, 64)) for j0 in range(4)])
    flip(trans1, [(4, (1, 4, 0, 16))])
    flip(trans2, [(5, (0, 1, 0, 4))])
    flip(trans3, [(6, (0, 0, 0, 1))])

    def lift_from(entry, vector, out, add):
        matvec(lambda b: et[entry, pl.ds(b, K, stride=K), :], vector, out, add)

    for j0 in range(4):
        lift_from(j0, coef0.at[j0], coef.at[0], j0 > 0)
    lift_from(4, coef.at[0], coef.at[1], False)
    fold(coef.at[1], (32, 64))
    lift_from(5, coef.at[1], coef.at[2], False)
    fold(coef.at[2], (8, 16))
    lift_from(6, coef.at[2], coef.at[3], False)

    j1, j2, c3 = lane_digits((1, 128), 1)
    for level, (prox, ids, rows) in enumerate(
        (
            (prox1, c3 * 16 + j2 * 4 + j1 + here * 128, (1, 4, 0, 16)),
            (prox2, c3 * 4 + j2 + here * 32, (0, 1, 0, 4)),
            (prox3, c3 + here * 8, (0, 0, 0, 1)),
        )
    ):
        if level == 0:
            columns[level, 0:128, :] = jnp.transpose(
                jnp.concatenate([prox[...], jnp.zeros((128 - 3 * K, 128), f32)], 0)
            )
        else:
            columns[level, 0 : prox.shape[0], :] = jnp.concatenate(
                [prox[...], jnp.zeros((prox.shape[0], 128 - 3 * K), f32)], 1
            )
        offsets = digits_first(level, rows)
        across, beside = centre_lanes(ids, 4**level)
        payload[level, 0:ROWS, :] = coef[level]
        payload[level, ROWS : ROWS + K, :] = across + float(4**level) * offsets[0:K]
        payload[level, ROWS + K : ROWS + 2 * K, :] = beside + 4.0 * offsets[K : 2 * K]
        payload[level, ROWS + 2 * K : WIDE, :] = offsets[2 * K : 3 * K]

    def flip_payload(source, width):
        for q in range(0, width, 128):
            size = min(128, width - q)
            block = source[q : q + size, :]
            if size < 128:
                block = jnp.concatenate([block, jnp.zeros((128 - size, 128), f32)], 0)
            flipped[:, q : q + 128] = jnp.transpose(block)

    last_rows = ([31, 63, 95, 127], [7, 15, 23, 31], [4, 5, 6, 7])
    first_rows = ([0, 32, 64, 96], [0, 8, 16, 24], [0, 1, 2, 3])
    last_out[...] = jnp.zeros_like(last_out)
    first_out[...] = jnp.zeros_like(first_out)
    for level in range(3):
        flip_payload(payload.at[level], WIDE)
        for i in range(4):
            target = level * 4 + i
            last_out[target : target + 1, :] = flipped[last_rows[level][i] : last_rows[level][i] + 1, 0:WIDE]
            first_out[target : target + 1, :] = flipped[first_rows[level][i] : first_rows[level][i] + 1, 0:WIDE]
    flip_payload(coef.at[3], ROWS)
    top_ids = lax.broadcasted_iota(jnp.int32, (terms.shape[0], ROWS), 0)
    total = jnp.zeros(terms.shape, f32)
    for c in range(8):
        total = total + jnp.where(top_ids == tops[here * 8 + c], flipped[c : c + 1, 0:ROWS], 0.0)
    terms[...] = total


def upward_pass(tops, basis, charge, trans0, trans1, trans2, trans3, prox1, prox2, prox3, top_count):
    vmem = pl.BlockSpec(memory_space=pltpu.VMEM)
    smem = pl.BlockSpec(memory_space=pltpu.SMEM)
    leaves = trans0.shape[0]
    return pl.pallas_call(
        up_kernel,
        out_shape=[
            jax.ShapeDtypeStruct((7, K * K, 128), f32),
            jax.ShapeDtypeStruct((3, WIDE, 128), f32),
            jax.ShapeDtypeStruct((EDGE, WIDE), f32),
            jax.ShapeDtypeStruct((EDGE, WIDE), f32),
            jax.ShapeDtypeStruct((top_count, ROWS), f32),
        ],
        in_specs=[smem] + [vmem] * 9,
        out_specs=[vmem] * 5,
        scratch_shapes=[
            pltpu.VMEM((leaves * R, 128), f32),
            pltpu.VMEM((4, ROWS, 128), f32),
            pltpu.VMEM((4, ROWS, 128), f32),
            pltpu.VMEM((128, 640), f32),
            pltpu.VMEM((8, leaves, 128), f32),
        ],
        compiler_params=pltpu.CompilerParams(vmem_limit_bytes=40 * 2**20),
        cost_estimate=pl.CostEstimate(
            flops=leaves * 200000, bytes_accessed=leaves * 20000, transcendentals=0
        ),
        name="upward_pass",
    )(tops, basis, charge, trans0, trans1, trans2, trans3, prox1, prox2, prox3)


def down_kernel(
    tops, et, payload, low_halo, high_halo, coef_top, prox_top, list1, list2, list3, basis, near_field,
    out, split_rows, split_top, gathered, green_rows, local, leaf_local, leaf_rows, columns,
):
    here = lax.axis_index("gx")
    top_count = coef_top.shape[0]
    j1, j2, c3 = lane_digits((1, 128), 1)

    def split_to(ref, columns, value):
        parts = split_three(value)
        for i in range(3):
            ref[i, :, columns] = parts[i].astype(bf16)

    def pick(ref, hot):
        hot = hot.astype(f32).astype(bf16)
        total = jnp.dot(ref[0], hot, preferred_element_type=f32)
        total = total + jnp.dot(ref[1], hot, preferred_element_type=f32)
        return total + jnp.dot(ref[2], hot, preferred_element_type=f32)

    def couple_picked(target, out_ref, add):
        def step(b, carry):
            square = None
            for axis_id in range(3):
                spread = target(axis_id) - gathered[pl.ds(ROWS + axis_id * K + b, 1), :]
                square = spread * spread if square is None else square + spread * spread
            green_rows[pl.ds(pl.multiple_of(b * K, K), K), :] = inv_four_pi * lax.rsqrt(square + soft_square)
            return carry

        lax.fori_loop(0, K, step, 0, unroll=4)
        matvec(lambda b: green_rows[b * K : (b + 1) * K, :], gathered, out_ref, add)

    def descend_from(entry, vector, out_ref, add):
        matvec(lambda a: et[entry, a * K : (a + 1) * K, :], vector, out_ref, add)

    my_top = jnp.zeros((1, 128), jnp.int32)
    for c in range(8):
        my_top = jnp.where(c3 == c, tops[here * 8 + c], my_top)
    for q in range(0, split_top.shape[2], 128):
        rows = min(128, top_count - q)

        def flip_top(block):
            if block.shape[1] < 128:
                block = jnp.concatenate([block, jnp.zeros((rows, 128 - block.shape[1]), f32)], 1)
            if rows < 128:
                block = jnp.concatenate([block, jnp.zeros((128 - rows, 128), f32)], 0)
            return jnp.transpose(block)

        def keep_top(first, value):
            parts = split_three(value)
            for i in range(3):
                split_top[i, first : first + value.shape[0], q : q + 128] = parts[i].astype(bf16)

        for w in range(0, ROWS, 128):
            keep_top(w, flip_top(coef_top[q : q + rows, w : w + 128]))
        offsets = flip_top(prox_top[q : q + rows, :])
        across, beside = centre_lanes(lax.broadcasted_iota(jnp.int32, (1, 128), 1) + q, 64)
        keep_top(ROWS, across + 64.0 * offsets[0:K])
        keep_top(ROWS + K, beside + 4.0 * offsets[K : 2 * K])
        keep_top(ROWS + 2 * K, offsets[2 * K : 3 * K])
    top_rows = lax.broadcasted_iota(jnp.int32, (split_top.shape[2], 128), 0)
    targets = pick(split_top.at[:, ROWS:WIDE, :], top_rows == my_top)
    leaf_local[0, 0 : 3 * K, :] = targets
    lane_block = lax.broadcasted_iota(jnp.int32, (1, 128), 1) >> 3
    local[0] = jnp.zeros((ROWS, 128), f32)

    def top_block(block, carry):
        source = block * 16 + lane_block
        far = jnp.abs(source - my_top) >= 2
        gathered[...] = pick(split_top, (top_rows == jnp.where(far, source, -1)))
        couple_picked(lambda axis_id: leaf_local[0, axis_id * K : (axis_id + 1) * K, :], local.at[0], True)
        return carry

    lax.fori_loop(0, (top_count + 15) // 16, top_block, 0)
    fold(local.at[0], (8, 16, 32, 64))

    halo = jnp.concatenate([low_halo[...], high_halo[...], jnp.zeros((128 - 2 * EDGE, WIDE), f32)], 0)
    for w in range(0, WIDE, 128):
        size = min(128, WIDE - w)
        block = halo[:, w : w + size]
        if size < 128:
            block = jnp.concatenate([block, jnp.zeros((128, 128 - size), f32)], 1)
        parts = split_three(jnp.transpose(block))
        for i in range(3):
            split_rows[i, w : w + size, 128:256] = parts[i][0:size].astype(bf16)

    def lane_list(ref, rows, base):
        count = ref.shape[1]
        values = jnp.concatenate([(ref[...] - base).astype(f32), jnp.zeros((125, count), f32)], 0)
        if count < 128:
            values = jnp.concatenate([values, jnp.zeros((128, 128 - count), f32)], 1)
        columns[...] = jnp.transpose(values)
        parts = [
            columns[pl.ds(rows[0] * a + rows[1] * b, 8, stride=rows[2]), :] for a in range(4) for b in range(4)
        ]
        return jnp.transpose(jnp.concatenate(parts, 0)).astype(jnp.int32)

    source = lax.broadcasted_iota(jnp.int32, (256, 128), 0)
    edge = source - 128
    s1, s2, s3 = (source >> 5) & 3, (source >> 3) & 3, source & 7

    def source_ids(level, own, own_count, count):
        low = edge - 4 * level
        high = edge - EDGE - 4 * level
        ids = jnp.where(source < own_count, own, -1000)
        ids = jnp.where((low >= 0) & (low < 4), low - 4, ids)
        return jnp.where((high >= 0) & (high < 4), high + count, ids)

    def place_of(level):
        return lambda axis_id: payload[level, ROWS + axis_id * K : ROWS + (axis_id + 1) * K, :]

    picked = lane_list(list3, (0, 0, 1), here * 8)
    wanted = jnp.where(j2 == 0, picked[0:1], jnp.where(j2 == 1, picked[1:2], jnp.where(j2 == 2, picked[2:3], -5000)))
    split_to(split_rows, slice(0, 128), payload[2])
    gathered[...] = pick(split_rows, source_ids(2, s3, 8, 8) == wanted)
    couple_picked(place_of(2), local.at[1], False)
    fold(local.at[1], (8, 16))
    descend_from(6, local.at[0], local.at[1], True)

    picked = lane_list(list2, (0, 1, 4), here * 32)
    wanted = jnp.where(j1 == 0, picked[0:1], jnp.where(j1 == 1, picked[1:2], jnp.where(j1 == 2, picked[2:3], -5000)))
    split_to(split_rows, slice(0, 128), payload[1])
    gathered[...] = pick(split_rows, source_ids(1, s3 * 4 + s2, 32, 32) == wanted)
    couple_picked(place_of(1), local.at[0], False)
    fold(local.at[0], (32, 64))
    descend_from(5, local.at[1], local.at[0], True)

    picked = lane_list(list1, (1, 4, 16), here * 128)
    split_to(split_rows, slice(0, 128), payload[0])
    ids = source_ids(0, s3 * 16 + s2 * 4 + s1, 128, 128)
    for j in range(3):
        gathered[...] = pick(split_rows, ids == picked[j : j + 1])
        couple_picked(place_of(0), local.at[1], j > 0)
    descend_from(4, local.at[0], local.at[1], True)
    for j0 in range(4):
        descend_from(j0, local.at[1], leaf_local.at[j0], False)

    def leaf_terms(r, carry):
        place = pl.ds(pl.multiple_of(r * K, K), K)
        for j0 in range(4):
            value = jnp.transpose(
                jnp.concatenate([leaf_local[j0, place, :], jnp.zeros((128 - K, 128), f32)], 0)
            )
            for a in range(4):
                for b in range(4):
                    leaf_rows[pl.ds((b * 16 + a * 4 + j0) * R + r, 8, stride=64 * R), :] = value[
                        a * 32 + b * 8 : a * 32 + b * 8 + 8
                    ]
        return carry

    lax.fori_loop(0, R, leaf_terms, 0, unroll=2)
    half = lax.broadcasted_iota(jnp.int32, (R, 128), 1) < 64

    def potential(tile, carry):
        lanes = pl.ds(pl.multiple_of(tile * 256, 256), 256)
        high, low = split_two(basis[:, lanes])
        left, left_low = split_two(leaf_rows[pl.ds(pl.multiple_of(tile * 64, 64), 64), 0:K])
        total = jnp.dot(left, high, preferred_element_type=f32)
        total = total + jnp.dot(left, low, preferred_element_type=f32)
        total = total + jnp.dot(left_low, high, preferred_element_type=f32)
        one = jnp.where(half, total[0:16, 0:128], total[16:32, 0:128])
        two = jnp.where(half, total[32:48, 128:256], total[48:64, 128:256])
        out[:, lanes] = near_field[:, lanes] + jnp.concatenate([one, two], 1)
        return carry

    lax.fori_loop(0, basis.shape[1] // 256, potential, 0, unroll=4)


def downward_pass(
    tops, et, payload, low_halo, high_halo, coef_top, prox_top, list1, list2, list3, basis, near_field
):
    vmem = pl.BlockSpec(memory_space=pltpu.VMEM)
    smem = pl.BlockSpec(memory_space=pltpu.SMEM)
    panels = basis.shape[1]
    top_count = coef_top.shape[0]
    top_lanes = (top_count + 127) // 128 * 128
    return pl.pallas_call(
        down_kernel,
        out_shape=jax.ShapeDtypeStruct((R, panels), f32),
        in_specs=[smem] + [vmem] * 11,
        out_specs=vmem,
        scratch_shapes=[
            pltpu.VMEM((3, WIDE, 256), bf16),
            pltpu.VMEM((3, WIDE, top_lanes), bf16),
            pltpu.VMEM((WIDE, 128), f32),
            pltpu.VMEM((K * K, 128), f32),
            pltpu.VMEM((2, ROWS, 128), f32),
            pltpu.VMEM((4, ROWS, 128), f32),
            pltpu.VMEM((panels // LEAF * R, 128), f32),
            pltpu.VMEM((128, 128), f32),
        ],
        compiler_params=pltpu.CompilerParams(vmem_limit_bytes=40 * 2**20),
        cost_estimate=pl.CostEstimate(
            flops=panels * 4000, bytes_accessed=panels * 400, transcendentals=panels * 20
        ),
        name="downward_pass",
    )(tops, et, payload, low_halo, high_halo, coef_top, prox_top, list1, list2, list3, basis, near_field)


def body(
    charge, jitter, basis, near, trans0, trans1, trans2, trans3,
    prox1, prox2, prox3, prox_top, list1, list2, list3, top_of,
):
    count = lax.axis_size("gx")
    forward = [(i, i + 1) for i in range(count - 1)]
    backward = [(target, source) for source, target in forward]
    low_leaves, high_leaves = leaf_halos(jitter, charge)
    et, payload, last, first, terms = upward_pass(
        top_of, basis, charge, trans0, trans1, trans2, trans3, prox1.T, prox2, prox3, prox_top.shape[0]
    )
    low_halo = lax.ppermute(last, "gx", forward)
    high_halo = lax.ppermute(first, "gx", backward)
    coef_top = lax.psum(terms, "gx")
    near_field = near_potential(near.T, jitter, charge, low_leaves, high_leaves)
    near_field, coef_top = lax.optimization_barrier((near_field, coef_top))
    return downward_pass(
        top_of, et, payload, low_halo, high_halo, coef_top, prox_top, list1.T, list2.T, list3.T, basis, near_field
    )


def solution(mesh):
    placed = (
        P(None, ("groups", "gx")),
        P(None, ("groups", "gx")),
        P(None, ("groups", "gx")),
        P(("groups", "gx"), None),
        P(("groups", "gx"), None),
        P(("groups", "gx"), None),
        P(("groups", "gx"), None),
        P(("groups", "gx"), None),
        P(("groups", "gx"), None),
        P(("groups", "gx"), None),
        P(("groups", "gx"), None),
        P("groups", None),
        P(("groups", "gx"), None),
        P(("groups", "gx"), None),
        P(("groups", "gx"), None),
        P("groups"),
    )
    return jax.shard_map(
        body, mesh=mesh, in_specs=placed, out_specs=P(None, ("groups", "gx")), check_vma=False
    )
```

```python
import jax
import jax.numpy as jnp
from jax import lax
from jax.experimental import pallas as pl
from jax.experimental.pallas import tpu as pltpu
from jax.sharding import PartitionSpec as P

LEAF = 64
K = 32
R = 16
NREACH = 16


inv_four_pi = 0.07957747154594767
soft_square = 0.01
row_columns = 64


def leaf_halos(jitter, charge):
    count = lax.axis_size("gx")
    forward = [(i, i + 1) for i in range(count - 1)]
    backward = [(target, source) for source, target in forward]
    width = NREACH * LEAF
    last = jnp.concatenate([jitter[:, -width:], charge[:, -width:]], axis=0)
    first = jnp.concatenate([jitter[:, :width], charge[:, :width]], axis=0)
    return lax.ppermute(last, "gx", forward), lax.ppermute(first, "gx", backward)


def column_place(column):
    row_number = column >> 6
    middle = column & (row_columns - 1)
    across = jnp.where((row_number & 1) == 0, middle, row_columns - 1 - middle)
    return across.astype(jnp.float32), (4 * row_number).astype(jnp.float32)


GROUP = 16
BATCH = 8
bf16 = jnp.bfloat16
f32 = jnp.float32


def split_two(value):
    high = value.astype(bf16)
    return high, (value - high.astype(f32)).astype(bf16)


def split_three(value):
    first = value.astype(bf16).astype(f32)
    rest = value - first
    second = rest.astype(bf16).astype(f32)
    return first, second, rest - second


def lanes_of(tile):
    return pl.ds(pl.multiple_of(tile * 128, 128), 128)


def near_kernel(
    ids, own_jitter, own_charge, low_halo, high_halo, out, points, feats0, feats1, charges, targets0, targets1, kernels, weights
):
    halo_tiles = low_halo.shape[1] // 128
    own_tiles = own_jitter.shape[1] // 128
    here = lax.axis_index("gx")
    first_id = here * (2 * own_tiles) - NREACH
    high_side = jnp.where(lax.broadcasted_iota(jnp.int32, (1, 128), 1) < LEAF, 0.0, 1.0)
    left_half = lax.broadcasted_iota(jnp.int32, (32, 128), 1).astype(bf16) < 64
    row = lax.broadcasted_iota(jnp.int32, (8, 128), 0)
    is_three = row == 3
    is_four = row == 4
    below_five = row < 5
    one_three = jnp.where(is_three, 1.0, 0.0)
    one_four = jnp.where(is_four, 1.0, 0.0)

    def stage(tile, place, charge):
        number = tile + (here * own_tiles - halo_tiles)
        across, beside = column_place(number >> 1)
        beside = beside + (2 * (number & 1)).astype(f32)
        centre = jnp.where(row == 0, across, jnp.where(row == 1, beside + high_side, 0.0))
        points[:, lanes_of(tile)] = centre + jnp.concatenate([place, jnp.zeros((5, 128), f32)], 0)
        charge = charge * inv_four_pi
        charges[2 * tile] = jnp.concatenate(split_two(charge), 0)
        charges[2 * tile + 1] = jnp.concatenate(split_two(pltpu.roll(charge, 64, 1)), 0)

    def stage_halo(halo, first):
        def step(i, carry):
            stage(first + i, halo[0:3, lanes_of(i)], halo[3:19, lanes_of(i)])
            return carry

        lax.fori_loop(0, halo_tiles, step, 0, unroll=2)

    def stage_own(i, carry):
        stage(halo_tiles + i, own_jitter[:, lanes_of(i)], own_charge[:, lanes_of(i)])
        return carry

    stage_halo(low_halo, 0)
    stage_halo(high_halo, halo_tiles + own_tiles)
    lax.fori_loop(0, own_tiles, stage_own, 0, unroll=4)

    def back(slot):
        total = lax.dot_general(
            kernels[slot], weights[slot], (((1,), (1,)), ((), ())), preferred_element_type=f32
        )
        total = jnp.transpose(total[:LEAF] + total[LEAF:])
        return total[:R] + total[R:]

    def emit(first):
        parts = [back(slot) for slot in range(BATCH)]
        first = jnp.maximum(first, 0)
        for half in range(BATCH // 2):
            place = pl.ds(pl.multiple_of((first + 2 * half) * LEAF, 128), 128)
            out[:, place] = jnp.concatenate([parts[2 * half], parts[2 * half + 1]], 1)

    def fill(group, feats, targets, part, part_count):
        base = group * GROUP
        across, beside = column_place(((first_id + NREACH) >> 2) + group * (GROUP // 4))
        row_sign = jnp.where((((first_id + NREACH + base) >> 8) & 1) == 0, 1.5, -1.5)
        shift = jnp.where(row == 0, across + row_sign, jnp.where(row == 1, beside + 1.5, 0.0))

        def local(tile):
            place = points[:, lanes_of(tile)] - shift
            square = place * place
            return place, jnp.broadcast_to(square[0:1] + square[1:2] + square[2:3], (8, 128))

        def source_rows(i):
            place, square = local(base // 2 + i)
            rows = place * (-2.0) + jnp.where(is_three, square + soft_square, one_four)

            def put(entry, value):
                first, second, third = split_three(value)
                one = jnp.where(below_five, first, pltpu.roll(second, 5, 0))
                two = jnp.where(is_three, second, one)
                three = jnp.where(below_five, third + one_four, pltpu.roll(first, 5, 0))
                feats[entry] = jnp.concatenate([one, two, three, jnp.zeros_like(one)], 0).astype(bf16)

            put(2 * i, rows)
            put(2 * i + 1, pltpu.roll(rows, 64, 1))

        def target_rows(i):
            place, square = local(base // 2 + NREACH // 2 + i)
            first, second, third = split_three(place + jnp.where(is_four, square, one_three))
            one = jnp.where(below_five, first, pltpu.roll(first, 5, 0))
            two = jnp.where(below_five, second + one_three, pltpu.roll(second, 5, 0))
            three = jnp.where(below_five, jnp.where(is_four, third, first), pltpu.roll(third, 5, 0))
            rows = jnp.concatenate([one, two, three, jnp.zeros_like(one)], 0)
            targets[lanes_of(i), :] = jnp.transpose(rows).astype(bf16)

        sources = (GROUP + 2 * NREACH) // 2 // part_count
        for i in range(sources):
            source_rows(part * sources + i)
        own = GROUP // 2 // part_count
        for i in range(own):
            target_rows(part * own + i)

    def front(base, leaf, slot, feats, targets):
        target = targets[pl.ds(pl.multiple_of(leaf * LEAF, LEAF), LEAF), :]
        entry = base + leaf
        for j in range(4):
            sides = []
            for h in range(2):
                one = ids[4 * j + 2 * h, entry] - first_id
                two = (ids[4 * j + 2 * h + 1, entry] - first_id) ^ 1
                sides.append(jnp.where(left_half, feats[one - base], feats[two - base]))
                weights[slot, :, (2 * j + h) * 128 : (2 * j + h + 1) * 128] = jnp.where(
                    left_half, charges[one], charges[two]
                )
            square = jnp.dot(target, jnp.concatenate(sides, 1), preferred_element_type=f32)
            high, low = split_two(lax.rsqrt(square))
            kernels[slot, 0:LEAF, j * 256 : (j + 1) * 256] = high
            kernels[slot, LEAF : 2 * LEAF, j * 256 : (j + 1) * 256] = low

    group_count = own_tiles * 2 // GROUP

    def do_two_groups(i, carry):
        for half in range(2):
            now = (feats0, targets0) if half == 0 else (feats1, targets1)
            later = (feats1, targets1) if half == 0 else (feats0, targets0)
            group = 2 * i + half
            following = jnp.minimum(group + 1, group_count - 1)

            def step(part, inner):
                emit(group * GROUP + BATCH * part - BATCH)
                for slot in range(BATCH):
                    front(group * GROUP, BATCH * part + slot, slot, *now)
                fill(following, *later, part, GROUP // BATCH)
                return inner

            lax.fori_loop(0, GROUP // BATCH, step, 0)
        return carry

    kernels[...] = jnp.zeros_like(kernels)
    weights[...] = jnp.zeros_like(weights)
    fill(0, feats0, targets0, 0, 1)
    lax.fori_loop(0, group_count // 2, do_two_groups, 0)
    emit(own_tiles * 2 - BATCH)


def near_potential(ids, own_jitter, own_charge, low_halo, high_halo):
    panels = own_jitter.shape[1]
    leaves = (panels + 2 * low_halo.shape[1]) // LEAF
    pairs = panels * 16 * LEAF
    vmem = pl.BlockSpec(memory_space=pltpu.VMEM)
    smem = pl.BlockSpec(memory_space=pltpu.SMEM)
    return pl.pallas_call(
        near_kernel,
        out_shape=jax.ShapeDtypeStruct((R, panels), f32),
        in_specs=[smem, vmem, vmem, vmem, vmem],
        out_specs=vmem,
        scratch_shapes=[
            pltpu.VMEM((8, leaves * LEAF), f32),
            pltpu.VMEM((GROUP + 2 * NREACH, 32, 128), bf16),
            pltpu.VMEM((GROUP + 2 * NREACH, 32, 128), bf16),
            pltpu.VMEM((leaves, 2 * R, 128), bf16),
            pltpu.VMEM((GROUP * LEAF, 32), bf16),
            pltpu.VMEM((GROUP * LEAF, 32), bf16),
            pltpu.VMEM((BATCH, 2 * LEAF, 16 * LEAF), bf16),
            pltpu.VMEM((BATCH, 2 * R, 16 * LEAF), bf16),
        ],
        compiler_params=pltpu.CompilerParams(vmem_limit_bytes=16 * 2**20),
        cost_estimate=pl.CostEstimate(
            flops=pairs * 192, bytes_accessed=panels * 160, transcendentals=pairs
        ),
        name="near_potential",
    )(ids, own_jitter, own_charge, low_halo, high_halo)


EDGE = 16
CHUNKS = 4
ROWS = R * K
WIDE = ROWS + 3 * K


def lane_digits(shape, dim):
    index = lax.broadcasted_iota(jnp.int32, shape, dim)
    return index >> 5, (index >> 3) & 3, index & 7


def lane_of_tile(tile):
    return (tile & 3) * 32 + ((tile >> 2) & 3) * 8 + (tile >> 4)


def matvec(matrix, vector, out, add, for_rows=4):

    def step(block, carry):
        start = pl.multiple_of(block * for_rows * K, for_rows * K)
        sums = [jnp.zeros((K, 128), f32) for _ in range(for_rows)]
        for column in range(K):
            values = matrix(column)
            for i in range(for_rows):
                sums[i] = sums[i] + values * vector[pl.ds(start + i * K + column, 1), :]
        for i in range(for_rows):
            place = pl.ds(start + i * K, K)
            out[place, :] = out[place, :] + sums[i] if add else sums[i]
        return carry

    lax.fori_loop(0, R // for_rows, step, 0)


def fold(ref, shifts):
    def step(i, carry):
        place = pl.ds(pl.multiple_of(i * 64, 64), 64)
        value = ref[place, :]
        for shift in shifts:
            value = value + pltpu.roll(value, shift, 1)
        ref[place, :] = value
        return carry

    lax.fori_loop(0, ROWS // 64, step, 0)


def centre_lanes(ids, level_width):
    first = ids * level_width
    row_number = first >> 6
    middle = (first & (row_columns - 1)).astype(f32) + 0.5 * (level_width - 1)
    across = jnp.where((row_number & 1) == 0, middle, row_columns - 1 - middle)
    return across, 4.0 * row_number.astype(f32) + 1.5


def up_kernel(
    tops, basis_hbm, charge_hbm, trans0_hbm, trans1, trans2, trans3, prox1, prox2, prox3,
    et, payload, last_out, first_out, terms, leaf_rows, coef0, coef, flipped, columns, by_column, basis, charge, trans0, sems,
):
    here = lax.axis_index("gx")
    quarter = lax.broadcasted_iota(jnp.int32, (R, 256), 1).astype(f32)

    def moments(tile, carry):
        lanes = pl.ds(pl.multiple_of(tile * 256, 256), 256)
        high, low = split_two(basis[:, lanes])
        right = jnp.concatenate([high, low, high], 1)
        value = charge[:, lanes]
        pieces = [
            split_two(jnp.where((quarter >= 64.0 * i) & (quarter < 64.0 * (i + 1)), value, 0.0))
            for i in range(4)
        ]
        highs = jnp.concatenate([p[0] for p in pieces], 0)
        lows = jnp.concatenate([p[1] for p in pieces], 0)
        left = jnp.concatenate([highs, highs, lows], 1)
        total = lax.dot_general(left, right, (((1,), (1,)), ((), ())), preferred_element_type=f32)
        total = jnp.concatenate([total, jnp.zeros((64, 128 - K), f32)], 1)
        leaf_rows[pl.ds(lane_of_tile(tile), 64, stride=128), :] = total
        return carry

    tiles = basis.shape[1] // 256
    chunk = basis.shape[1] // CHUNKS
    copies = []
    for i in range(CHUNKS):
        lanes = pl.ds(i * chunk, chunk)
        copies.append(pltpu.make_async_copy(basis_hbm.at[:, lanes], basis.at[:, lanes], sems.at[2 * i]))
        copies.append(pltpu.make_async_copy(charge_hbm.at[:, lanes], charge.at[:, lanes], sems.at[2 * i + 1]))
    copies.append(pltpu.make_async_copy(trans0_hbm, trans0, sems.at[2 * CHUNKS]))
    for copy in copies:
        copy.start()
    for i in range(CHUNKS):
        copies[2 * i].wait()
        copies[2 * i + 1].wait()
        lax.fori_loop(i * tiles // CHUNKS, (i + 1) * tiles // CHUNKS, moments, 0, unroll=4)
    copies[2 * CHUNKS].wait()

    def leaf_coefs(r, carry):
        place = pl.ds(pl.multiple_of(r * K, K), K)
        for j0 in range(4):
            rows = leaf_rows[pl.ds(pl.multiple_of((j0 * R + r) * 128, 128), 128), :]
            coef0[j0, place, :] = jnp.transpose(rows)[0:K]
        return carry

    lax.fori_loop(0, R, leaf_coefs, 0, unroll=2)

    def digits_first(q, rows):
        parts = [
            columns[q, pl.ds(rows[0] * a + rows[1] * b + rows[2], 8, stride=rows[3]), :]
            for a in range(4)
            for b in range(4)
        ]
        return jnp.transpose(jnp.concatenate(parts, 0))

    def flip(source, entries):
        for q in range(8):
            columns[q, 0 : source.shape[0], :] = source[:, q * 128 : (q + 1) * 128]
        for q in range(8):
            for entry, rows in entries:
                et[entry, q * 128 : (q + 1) * 128, :] = digits_first(q, rows)

    flip(trans0, [(j0, (4, 16, j0, 64)) for j0 in range(4)])
    flip(trans1, [(4, (1, 4, 0, 16))])
    flip(trans2, [(5, (0, 1, 0, 4))])
    flip(trans3, [(6, (0, 0, 0, 1))])

    def lift_from(entry, vector, out, add):
        for b in range(K):
            by_column[b * K : (b + 1) * K, :] = et[entry, pl.ds(b, K, stride=K), :]
        matvec(lambda b: by_column[b * K : (b + 1) * K, :], vector, out, add)

    for j0 in range(4):
        lift_from(j0, coef0.at[j0], coef.at[0], j0 > 0)
    lift_from(4, coef.at[0], coef.at[1], False)
    fold(coef.at[1], (32, 64))
    lift_from(5, coef.at[1], coef.at[2], False)
    fold(coef.at[2], (8, 16))
    lift_from(6, coef.at[2], coef.at[3], False)

    j1, j2, c3 = lane_digits((1, 128), 1)
    for level, (prox, ids, rows) in enumerate(
        (
            (prox1, c3 * 16 + j2 * 4 + j1 + here * 128, (1, 4, 0, 16)),
            (prox2, c3 * 4 + j2 + here * 32, (0, 1, 0, 4)),
            (prox3, c3 + here * 8, (0, 0, 0, 1)),
        )
    ):
        if level == 0:
            columns[level, 0:128, :] = jnp.transpose(
                jnp.concatenate([prox[...], jnp.zeros((128 - 3 * K, 128), f32)], 0)
            )
        else:
            columns[level, 0 : prox.shape[0], :] = jnp.concatenate(
                [prox[...], jnp.zeros((prox.shape[0], 128 - 3 * K), f32)], 1
            )
        offsets = digits_first(level, rows)
        across, beside = centre_lanes(ids, 4**level)
        payload[level, 0:ROWS, :] = coef[level]
        payload[level, ROWS : ROWS + K, :] = across + float(4**level) * offsets[0:K]
        payload[level, ROWS + K : ROWS + 2 * K, :] = beside + 4.0 * offsets[K : 2 * K]
        payload[level, ROWS + 2 * K : WIDE, :] = offsets[2 * K : 3 * K]

    def flip_payload(source, width):
        for q in range(0, width, 128):
            size = min(128, width - q)
            block = source[q : q + size, :]
            if size < 128:
                block = jnp.concatenate([block, jnp.zeros((128 - size, 128), f32)], 0)
            flipped[:, q : q + 128] = jnp.transpose(block)

    last_rows = ([31, 63, 95, 127], [7, 15, 23, 31], [4, 5, 6, 7])
    first_rows = ([0, 32, 64, 96], [0, 8, 16, 24], [0, 1, 2, 3])
    last_out[...] = jnp.zeros_like(last_out)
    first_out[...] = jnp.zeros_like(first_out)
    for level in range(3):
        flip_payload(payload.at[level], WIDE)
        for i in range(4):
            target = level * 4 + i
            last_out[target : target + 1, :] = flipped[last_rows[level][i] : last_rows[level][i] + 1, 0:WIDE]
            first_out[target : target + 1, :] = flipped[first_rows[level][i] : first_rows[level][i] + 1, 0:WIDE]
    flip_payload(coef.at[3], ROWS)
    top_ids = lax.broadcasted_iota(jnp.int32, (terms.shape[0], ROWS), 0)
    total = jnp.zeros(terms.shape, f32)
    for c in range(8):
        total = total + jnp.where(top_ids == tops[here * 8 + c], flipped[c : c + 1, 0:ROWS], 0.0)
    terms[...] = total


def upward_pass(tops, basis, charge, trans0, trans1, trans2, trans3, prox1, prox2, prox3, top_count):
    vmem = pl.BlockSpec(memory_space=pltpu.VMEM)
    smem = pl.BlockSpec(memory_space=pltpu.SMEM)
    leaves = trans0.shape[0]
    return pl.pallas_call(
        up_kernel,
        out_shape=[
            jax.ShapeDtypeStruct((7, K * K, 128), f32),
            jax.ShapeDtypeStruct((3, WIDE, 128), f32),
            jax.ShapeDtypeStruct((EDGE, WIDE), f32),
            jax.ShapeDtypeStruct((EDGE, WIDE), f32),
            jax.ShapeDtypeStruct((top_count, ROWS), f32),
        ],
        in_specs=[smem] + [pl.BlockSpec(memory_space=pltpu.HBM)] * 3 + [vmem] * 6,
        out_specs=[vmem] * 5,
        scratch_shapes=[
            pltpu.VMEM((leaves * R, 128), f32),
            pltpu.VMEM((4, ROWS, 128), f32),
            pltpu.VMEM((4, ROWS, 128), f32),
            pltpu.VMEM((128, 640), f32),
            pltpu.VMEM((8, leaves, 128), f32),
            pltpu.VMEM((K * K, 128), f32),
            pltpu.VMEM(basis.shape, f32),
            pltpu.VMEM(charge.shape, f32),
            pltpu.VMEM(trans0.shape, f32),
            pltpu.SemaphoreType.DMA((2 * CHUNKS + 1,)),
        ],
        compiler_params=pltpu.CompilerParams(vmem_limit_bytes=54 * 2**20),
        cost_estimate=pl.CostEstimate(
            flops=leaves * 200000, bytes_accessed=leaves * 20000, transcendentals=0
        ),
        name="upward_pass",
    )(tops, basis, charge, trans0, trans1, trans2, trans3, prox1, prox2, prox3)


def down_kernel(
    tops, et, payload, low_halo, high_halo, coef_top, prox_top, list1, list2, list3, basis, near_field,
    out, split_rows, split_top, gathered, green_rows, local, leaf_local, leaf_rows, columns,
):
    here = lax.axis_index("gx")
    top_count = coef_top.shape[0]
    j1, j2, c3 = lane_digits((1, 128), 1)

    def split_to(ref, columns, value):
        parts = split_three(value)
        for i in range(3):
            ref[i, :, columns] = parts[i].astype(bf16)

    def pick(ref, hot):
        hot = hot.astype(f32).astype(bf16)
        total = jnp.dot(ref[0], hot, preferred_element_type=f32)
        total = total + jnp.dot(ref[1], hot, preferred_element_type=f32)
        return total + jnp.dot(ref[2], hot, preferred_element_type=f32)

    def couple_picked(target, out_ref, add):
        def step(b, carry):
            square = None
            for axis_id in range(3):
                spread = target(axis_id) - gathered[pl.ds(ROWS + axis_id * K + b, 1), :]
                square = spread * spread if square is None else square + spread * spread
            green_rows[pl.ds(pl.multiple_of(b * K, K), K), :] = inv_four_pi * lax.rsqrt(square + soft_square)
            return carry

        lax.fori_loop(0, K, step, 0, unroll=4)
        matvec(lambda b: green_rows[b * K : (b + 1) * K, :], gathered, out_ref, add)

    def descend_from(entry, vector, out_ref, add):
        matvec(lambda a: et[entry, a * K : (a + 1) * K, :], vector, out_ref, add)

    my_top = jnp.zeros((1, 128), jnp.int32)
    for c in range(8):
        my_top = jnp.where(c3 == c, tops[here * 8 + c], my_top)
    for q in range(0, split_top.shape[2], 128):
        rows = min(128, top_count - q)

        def flip_top(block):
            if block.shape[1] < 128:
                block = jnp.concatenate([block, jnp.zeros((rows, 128 - block.shape[1]), f32)], 1)
            if rows < 128:
                block = jnp.concatenate([block, jnp.zeros((128 - rows, 128), f32)], 0)
            return jnp.transpose(block)

        def keep_top(first, value):
            parts = split_three(value)
            for i in range(3):
                split_top[i, first : first + value.shape[0], q : q + 128] = parts[i].astype(bf16)

        for w in range(0, ROWS, 128):
            keep_top(w, flip_top(coef_top[q : q + rows, w : w + 128]))
        offsets = flip_top(prox_top[q : q + rows, :])
        across, beside = centre_lanes(lax.broadcasted_iota(jnp.int32, (1, 128), 1) + q, 64)
        keep_top(ROWS, across + 64.0 * offsets[0:K])
        keep_top(ROWS + K, beside + 4.0 * offsets[K : 2 * K])
        keep_top(ROWS + 2 * K, offsets[2 * K : 3 * K])
    top_rows = lax.broadcasted_iota(jnp.int32, (split_top.shape[2], 128), 0)
    targets = pick(split_top.at[:, ROWS:WIDE, :], top_rows == my_top)
    leaf_local[0, 0 : 3 * K, :] = targets
    lane_block = lax.broadcasted_iota(jnp.int32, (1, 128), 1) >> 3
    local[0] = jnp.zeros((ROWS, 128), f32)

    def top_block(block, carry):
        source = block * 16 + lane_block
        far = jnp.abs(source - my_top) >= 2
        gathered[...] = pick(split_top, (top_rows == jnp.where(far, source, -1)))
        couple_picked(lambda axis_id: leaf_local[0, axis_id * K : (axis_id + 1) * K, :], local.at[0], True)
        return carry

    lax.fori_loop(0, (top_count + 15) // 16, top_block, 0)
    fold(local.at[0], (8, 16, 32, 64))

    halo = jnp.concatenate([low_halo[...], high_halo[...], jnp.zeros((128 - 2 * EDGE, WIDE), f32)], 0)
    for w in range(0, WIDE, 128):
        size = min(128, WIDE - w)
        block = halo[:, w : w + size]
        if size < 128:
            block = jnp.concatenate([block, jnp.zeros((128, 128 - size), f32)], 1)
        parts = split_three(jnp.transpose(block))
        for i in range(3):
            split_rows[i, w : w + size, 128:256] = parts[i][0:size].astype(bf16)

    def lane_list(ref, rows, base):
        count = ref.shape[1]
        values = jnp.concatenate([(ref[...] - base).astype(f32), jnp.zeros((125, count), f32)], 0)
        if count < 128:
            values = jnp.concatenate([values, jnp.zeros((128, 128 - count), f32)], 1)
        columns[...] = jnp.transpose(values)
        parts = [
            columns[pl.ds(rows[0] * a + rows[1] * b, 8, stride=rows[2]), :] for a in range(4) for b in range(4)
        ]
        return jnp.transpose(jnp.concatenate(parts, 0)).astype(jnp.int32)

    source = lax.broadcasted_iota(jnp.int32, (256, 128), 0)
    edge = source - 128
    s1, s2, s3 = (source >> 5) & 3, (source >> 3) & 3, source & 7

    def source_ids(level, own, own_count, count):
        low = edge - 4 * level
        high = edge - EDGE - 4 * level
        ids = jnp.where(source < own_count, own, -1000)
        ids = jnp.where((low >= 0) & (low < 4), low - 4, ids)
        return jnp.where((high >= 0) & (high < 4), high + count, ids)

    def place_of(level):
        return lambda axis_id: payload[level, ROWS + axis_id * K : ROWS + (axis_id + 1) * K, :]

    picked = lane_list(list3, (0, 0, 1), here * 8)
    wanted = jnp.where(j2 == 0, picked[0:1], jnp.where(j2 == 1, picked[1:2], jnp.where(j2 == 2, picked[2:3], -5000)))
    split_to(split_rows, slice(0, 128), payload[2])
    gathered[...] = pick(split_rows, source_ids(2, s3, 8, 8) == wanted)
    couple_picked(place_of(2), local.at[1], False)
    fold(local.at[1], (8, 16))
    descend_from(6, local.at[0], local.at[1], True)

    picked = lane_list(list2, (0, 1, 4), here * 32)
    wanted = jnp.where(j1 == 0, picked[0:1], jnp.where(j1 == 1, picked[1:2], jnp.where(j1 == 2, picked[2:3], -5000)))
    split_to(split_rows, slice(0, 128), payload[1])
    gathered[...] = pick(split_rows, source_ids(1, s3 * 4 + s2, 32, 32) == wanted)
    couple_picked(place_of(1), local.at[0], False)
    fold(local.at[0], (32, 64))
    descend_from(5, local.at[1], local.at[0], True)

    picked = lane_list(list1, (1, 4, 16), here * 128)
    split_to(split_rows, slice(0, 128), payload[0])
    ids = source_ids(0, s3 * 16 + s2 * 4 + s1, 128, 128)
    for j in range(3):
        gathered[...] = pick(split_rows, ids == picked[j : j + 1])
        couple_picked(place_of(0), local.at[1], j > 0)
    descend_from(4, local.at[0], local.at[1], True)
    for j0 in range(4):
        descend_from(j0, local.at[1], leaf_local.at[j0], False)

    def leaf_terms(r, carry):
        place = pl.ds(pl.multiple_of(r * K, K), K)
        for j0 in range(4):
            value = jnp.transpose(
                jnp.concatenate([leaf_local[j0, place, :], jnp.zeros((128 - K, 128), f32)], 0)
            )
            for a in range(4):
                for b in range(4):
                    leaf_rows[pl.ds((b * 16 + a * 4 + j0) * R + r, 8, stride=64 * R), :] = value[
                        a * 32 + b * 8 : a * 32 + b * 8 + 8
                    ]
        return carry

    lax.fori_loop(0, R, leaf_terms, 0, unroll=2)
    half = lax.broadcasted_iota(jnp.int32, (R, 128), 1) < 64

    def potential(tile, carry):
        lanes = pl.ds(pl.multiple_of(tile * 256, 256), 256)
        high, low = split_two(basis[:, lanes])
        left, left_low = split_two(leaf_rows[pl.ds(pl.multiple_of(tile * 64, 64), 64), 0:K])
        total = jnp.dot(left, high, preferred_element_type=f32)
        total = total + jnp.dot(left, low, preferred_element_type=f32)
        total = total + jnp.dot(left_low, high, preferred_element_type=f32)
        one = jnp.where(half, total[0:16, 0:128], total[16:32, 0:128])
        two = jnp.where(half, total[32:48, 128:256], total[48:64, 128:256])
        out[:, lanes] = near_field[:, lanes] + jnp.concatenate([one, two], 1)
        return carry

    lax.fori_loop(0, basis.shape[1] // 256, potential, 0, unroll=4)


def downward_pass(
    tops, et, payload, low_halo, high_halo, coef_top, prox_top, list1, list2, list3, basis, near_field
):
    vmem = pl.BlockSpec(memory_space=pltpu.VMEM)
    smem = pl.BlockSpec(memory_space=pltpu.SMEM)
    panels = basis.shape[1]
    top_count = coef_top.shape[0]
    top_lanes = (top_count + 127) // 128 * 128
    return pl.pallas_call(
        down_kernel,
        out_shape=jax.ShapeDtypeStruct((R, panels), f32),
        in_specs=[smem] + [vmem] * 11,
        out_specs=vmem,
        scratch_shapes=[
            pltpu.VMEM((3, WIDE, 256), bf16),
            pltpu.VMEM((3, WIDE, top_lanes), bf16),
            pltpu.VMEM((WIDE, 128), f32),
            pltpu.VMEM((K * K, 128), f32),
            pltpu.VMEM((2, ROWS, 128), f32),
            pltpu.VMEM((4, ROWS, 128), f32),
            pltpu.VMEM((panels // LEAF * R, 128), f32),
            pltpu.VMEM((128, 128), f32),
        ],
        compiler_params=pltpu.CompilerParams(vmem_limit_bytes=16 * 2**20),
        cost_estimate=pl.CostEstimate(
            flops=panels * 4000, bytes_accessed=panels * 400, transcendentals=panels * 20
        ),
        name="downward_pass",
    )(tops, et, payload, low_halo, high_halo, coef_top, prox_top, list1, list2, list3, basis, near_field)


def body(
    charge, jitter, basis, near, trans0, trans1, trans2, trans3,
    prox1, prox2, prox3, prox_top, list1, list2, list3, top_of,
):
    count = lax.axis_size("gx")
    forward = [(i, i + 1) for i in range(count - 1)]
    backward = [(target, source) for source, target in forward]
    low_leaves, high_leaves = leaf_halos(jitter, charge)
    et, payload, last, first, terms = upward_pass(
        top_of, basis, charge, trans0, trans1, trans2, trans3, prox1.T, prox2, prox3, prox_top.shape[0]
    )
    low_halo = lax.ppermute(last, "gx", forward)
    high_halo = lax.ppermute(first, "gx", backward)
    coef_top = lax.psum(terms, "gx")
    near_field = near_potential(near.T, jitter, charge, low_leaves, high_leaves)
    near_field, coef_top = lax.optimization_barrier((near_field, coef_top))
    return downward_pass(
        top_of, et, payload, low_halo, high_halo, coef_top, prox_top, list1.T, list2.T, list3.T, basis, near_field
    )


def solution(mesh):
    placed = (
        P(None, ("groups", "gx")),
        P(None, ("groups", "gx")),
        P(None, ("groups", "gx")),
        P(("groups", "gx"), None),
        P(("groups", "gx"), None),
        P(("groups", "gx"), None),
        P(("groups", "gx"), None),
        P(("groups", "gx"), None),
        P(("groups", "gx"), None),
        P(("groups", "gx"), None),
        P(("groups", "gx"), None),
        P("groups", None),
        P(("groups", "gx"), None),
        P(("groups", "gx"), None),
        P(("groups", "gx"), None),
        P("groups"),
    )
    return jax.shard_map(
        body, mesh=mesh, in_specs=placed, out_specs=P(None, ("groups", "gx")), check_vma=False
    )
```

```python
import jax
import jax.numpy as jnp
from jax import lax
from jax.experimental import pallas as pl
from jax.experimental.pallas import tpu as pltpu
from jax.sharding import PartitionSpec as P

LEAF = 64
K = 32
R = 16
NREACH = 16


inv_four_pi = 0.07957747154594767
soft_square = 0.01
row_columns = 64


def leaf_halos(jitter, charge):
    count = lax.axis_size("gx")
    forward = [(i, i + 1) for i in range(count - 1)]
    backward = [(target, source) for source, target in forward]
    width = NREACH * LEAF
    last = jnp.concatenate([jitter[:, -width:], charge[:, -width:]], axis=0)
    first = jnp.concatenate([jitter[:, :width], charge[:, :width]], axis=0)
    return lax.ppermute(last, "gx", forward), lax.ppermute(first, "gx", backward)


def column_place(column):
    row_number = column >> 6
    middle = column & (row_columns - 1)
    across = jnp.where((row_number & 1) == 0, middle, row_columns - 1 - middle)
    return across.astype(jnp.float32), (4 * row_number).astype(jnp.float32)


GROUP = 16
BATCH = 8
bf16 = jnp.bfloat16
f32 = jnp.float32


def split_two(value):
    high = value.astype(bf16)
    return high, (value - high.astype(f32)).astype(bf16)


def split_three(value):
    first = value.astype(bf16).astype(f32)
    rest = value - first
    second = rest.astype(bf16).astype(f32)
    return first, second, rest - second


def lanes_of(tile):
    return pl.ds(pl.multiple_of(tile * 128, 128), 128)


def near_kernel(
    ids, own_jitter, own_charge, low_halo, high_halo, out, points, feats0, feats1, charges, targets0, targets1, kernels, weights
):
    halo_tiles = low_halo.shape[1] // 128
    own_tiles = own_jitter.shape[1] // 128
    here = lax.axis_index("gx")
    first_id = here * (2 * own_tiles) - NREACH
    high_side = jnp.where(lax.broadcasted_iota(jnp.int32, (1, 128), 1) < LEAF, 0.0, 1.0)
    left_half = lax.broadcasted_iota(jnp.int32, (32, 128), 1).astype(bf16) < 64
    row = lax.broadcasted_iota(jnp.int32, (8, 128), 0)
    is_three = row == 3
    is_four = row == 4
    below_five = row < 5
    one_three = jnp.where(is_three, 1.0, 0.0)
    one_four = jnp.where(is_four, 1.0, 0.0)

    def stage(tile, place, charge):
        number = tile + (here * own_tiles - halo_tiles)
        across, beside = column_place(number >> 1)
        beside = beside + (2 * (number & 1)).astype(f32)
        centre = jnp.where(row == 0, across, jnp.where(row == 1, beside + high_side, 0.0))
        points[:, lanes_of(tile)] = centre + jnp.concatenate([place, jnp.zeros((5, 128), f32)], 0)
        charge = charge * inv_four_pi
        charges[2 * tile] = jnp.concatenate(split_two(charge), 0)
        charges[2 * tile + 1] = jnp.concatenate(split_two(pltpu.roll(charge, 64, 1)), 0)

    def stage_halo(halo, first):
        def step(i, carry):
            stage(first + i, halo[0:3, lanes_of(i)], halo[3:19, lanes_of(i)])
            return carry

        lax.fori_loop(0, halo_tiles, step, 0, unroll=2)

    def stage_own(i, carry):
        stage(halo_tiles + i, own_jitter[:, lanes_of(i)], own_charge[:, lanes_of(i)])
        return carry

    stage_halo(low_halo, 0)
    stage_halo(high_halo, halo_tiles + own_tiles)
    lax.fori_loop(0, own_tiles, stage_own, 0, unroll=4)

    def back(slot):
        total = lax.dot_general(
            kernels[slot], weights[slot], (((1,), (1,)), ((), ())), preferred_element_type=f32
        )
        total = jnp.transpose(total[:LEAF] + total[LEAF:])
        return total[:R] + total[R:]

    def emit(first):
        parts = [back(slot) for slot in range(BATCH)]
        first = jnp.maximum(first, 0)
        for half in range(BATCH // 2):
            place = pl.ds(pl.multiple_of((first + 2 * half) * LEAF, 128), 128)
            out[:, place] = jnp.concatenate([parts[2 * half], parts[2 * half + 1]], 1)

    def fill(group, feats, targets, part, part_count):
        base = group * GROUP
        across, beside = column_place(((first_id + NREACH) >> 2) + group * (GROUP // 4))
        row_sign = jnp.where((((first_id + NREACH + base) >> 8) & 1) == 0, 1.5, -1.5)
        shift = jnp.where(row == 0, across + row_sign, jnp.where(row == 1, beside + 1.5, 0.0))

        def local(tile):
            place = points[:, lanes_of(tile)] - shift
            square = place * place
            return place, jnp.broadcast_to(square[0:1] + square[1:2] + square[2:3], (8, 128))

        def source_rows(i):
            place, square = local(base // 2 + i)
            rows = place * (-2.0) + jnp.where(is_three, square + soft_square, one_four)

            def put(entry, value):
                first, second, third = split_three(value)
                one = jnp.where(below_five, first, pltpu.roll(second, 5, 0))
                two = jnp.where(is_three, second, one)
                three = jnp.where(below_five, third + one_four, pltpu.roll(first, 5, 0))
                feats[entry] = jnp.concatenate([one, two, three, jnp.zeros_like(one)], 0).astype(bf16)

            put(2 * i, rows)
            put(2 * i + 1, pltpu.roll(rows, 64, 1))

        def target_rows(i):
            place, square = local(base // 2 + NREACH // 2 + i)
            first, second, third = split_three(place + jnp.where(is_four, square, one_three))
            one = jnp.where(below_five, first, pltpu.roll(first, 5, 0))
            two = jnp.where(below_five, second + one_three, pltpu.roll(second, 5, 0))
            three = jnp.where(below_five, jnp.where(is_four, third, first), pltpu.roll(third, 5, 0))
            rows = jnp.concatenate([one, two, three, jnp.zeros_like(one)], 0)
            targets[lanes_of(i), :] = jnp.transpose(rows).astype(bf16)

        sources = (GROUP + 2 * NREACH) // 2 // part_count
        for i in range(sources):
            source_rows(part * sources + i)
        own = GROUP // 2 // part_count
        for i in range(own):
            target_rows(part * own + i)

    def front(base, leaf, slot, feats, targets):
        target = targets[pl.ds(pl.multiple_of(leaf * LEAF, LEAF), LEAF), :]
        entry = base + leaf
        for j in range(4):
            sides = []
            for h in range(2):
                one = ids[4 * j + 2 * h, entry] - first_id
                two = (ids[4 * j + 2 * h + 1, entry] - first_id) ^ 1
                sides.append(jnp.where(left_half, feats[one - base], feats[two - base]))
                weights[slot, :, (2 * j + h) * 128 : (2 * j + h + 1) * 128] = jnp.where(
                    left_half, charges[one], charges[two]
                )
            square = jnp.dot(target, jnp.concatenate(sides, 1), preferred_element_type=f32)
            high, low = split_two(lax.rsqrt(square))
            kernels[slot, 0:LEAF, j * 256 : (j + 1) * 256] = high
            kernels[slot, LEAF : 2 * LEAF, j * 256 : (j + 1) * 256] = low

    group_count = own_tiles * 2 // GROUP

    def do_two_groups(i, carry):
        for half in range(2):
            now = (feats0, targets0) if half == 0 else (feats1, targets1)
            later = (feats1, targets1) if half == 0 else (feats0, targets0)
            group = 2 * i + half
            following = jnp.minimum(group + 1, group_count - 1)

            def step(part, inner):
                emit(group * GROUP + BATCH * part - BATCH)
                for slot in range(BATCH):
                    front(group * GROUP, BATCH * part + slot, slot, *now)
                fill(following, *later, part, GROUP // BATCH)
                return inner

            lax.fori_loop(0, GROUP // BATCH, step, 0)
        return carry

    kernels[...] = jnp.zeros_like(kernels)
    weights[...] = jnp.zeros_like(weights)
    fill(0, feats0, targets0, 0, 1)
    lax.fori_loop(0, group_count // 2, do_two_groups, 0)
    emit(own_tiles * 2 - BATCH)


def near_potential(ids, own_jitter, own_charge, low_halo, high_halo):
    panels = own_jitter.shape[1]
    leaves = (panels + 2 * low_halo.shape[1]) // LEAF
    pairs = panels * 16 * LEAF
    vmem = pl.BlockSpec(memory_space=pltpu.VMEM)
    smem = pl.BlockSpec(memory_space=pltpu.SMEM)
    return pl.pallas_call(
        near_kernel,
        out_shape=jax.ShapeDtypeStruct((R, panels), f32),
        in_specs=[smem, vmem, vmem, vmem, vmem],
        out_specs=vmem,
        scratch_shapes=[
            pltpu.VMEM((8, leaves * LEAF), f32),
            pltpu.VMEM((GROUP + 2 * NREACH, 32, 128), bf16),
            pltpu.VMEM((GROUP + 2 * NREACH, 32, 128), bf16),
            pltpu.VMEM((leaves, 2 * R, 128), bf16),
            pltpu.VMEM((GROUP * LEAF, 32), bf16),
            pltpu.VMEM((GROUP * LEAF, 32), bf16),
            pltpu.VMEM((BATCH, 2 * LEAF, 16 * LEAF), bf16),
            pltpu.VMEM((BATCH, 2 * R, 16 * LEAF), bf16),
        ],
        compiler_params=pltpu.CompilerParams(vmem_limit_bytes=16 * 2**20),
        cost_estimate=pl.CostEstimate(
            flops=pairs * 192, bytes_accessed=panels * 160, transcendentals=pairs
        ),
        name="near_potential",
    )(ids, own_jitter, own_charge, low_halo, high_halo)


EDGE = 16
CHUNKS = 4
ROWS = R * K
WIDE = ROWS + 3 * K


def lane_digits(shape, dim):
    index = lax.broadcasted_iota(jnp.int32, shape, dim)
    return index >> 5, (index >> 3) & 3, index & 7


def lane_of_tile(tile):
    return (tile & 3) * 32 + ((tile >> 2) & 3) * 8 + (tile >> 4)


def matvec(matrix, vector, out, add, for_rows=4):

    def step(block, carry):
        start = pl.multiple_of(block * for_rows * K, for_rows * K)
        sums = [jnp.zeros((K, 128), f32) for _ in range(for_rows)]
        for column in range(K):
            values = matrix(column)
            for i in range(for_rows):
                sums[i] = sums[i] + values * vector[pl.ds(start + i * K + column, 1), :]
        for i in range(for_rows):
            place = pl.ds(start + i * K, K)
            out[place, :] = out[place, :] + sums[i] if add else sums[i]
        return carry

    lax.fori_loop(0, R // for_rows, step, 0)


def fold(ref, shifts):
    def step(i, carry):
        place = pl.ds(pl.multiple_of(i * 64, 64), 64)
        value = ref[place, :]
        for shift in shifts:
            value = value + pltpu.roll(value, shift, 1)
        ref[place, :] = value
        return carry

    lax.fori_loop(0, ROWS // 64, step, 0)


def centre_lanes(ids, level_width):
    first = ids * level_width
    row_number = first >> 6
    middle = (first & (row_columns - 1)).astype(f32) + 0.5 * (level_width - 1)
    across = jnp.where((row_number & 1) == 0, middle, row_columns - 1 - middle)
    return across, 4.0 * row_number.astype(f32) + 1.5


def up_kernel(
    basis_hbm, charge_hbm, trans0_hbm, trans1, trans2, trans3, prox1, prox2, prox3,
    et, payload, last_out, first_out, lifted, leaf_rows, coef0, coef, flipped, columns, by_column, basis, charge, trans0, sems,
):
    here = lax.axis_index("gx")
    quarter = lax.broadcasted_iota(jnp.int32, (R, 256), 1).astype(f32)

    def moments(tile, carry):
        lanes = pl.ds(pl.multiple_of(tile * 256, 256), 256)
        high, low = split_two(basis[:, lanes])
        right = jnp.concatenate([high, low, high], 1)
        value = charge[:, lanes]
        pieces = [
            split_two(jnp.where((quarter >= 64.0 * i) & (quarter < 64.0 * (i + 1)), value, 0.0))
            for i in range(4)
        ]
        highs = jnp.concatenate([p[0] for p in pieces], 0)
        lows = jnp.concatenate([p[1] for p in pieces], 0)
        left = jnp.concatenate([highs, highs, lows], 1)
        total = lax.dot_general(left, right, (((1,), (1,)), ((), ())), preferred_element_type=f32)
        total = jnp.concatenate([total, jnp.zeros((64, 128 - K), f32)], 1)
        leaf_rows[pl.ds(lane_of_tile(tile), 64, stride=128), :] = total
        return carry

    tiles = basis.shape[1] // 256
    chunk = basis.shape[1] // CHUNKS
    copies = []
    for i in range(CHUNKS):
        lanes = pl.ds(i * chunk, chunk)
        copies.append(pltpu.make_async_copy(basis_hbm.at[:, lanes], basis.at[:, lanes], sems.at[2 * i]))
        copies.append(pltpu.make_async_copy(charge_hbm.at[:, lanes], charge.at[:, lanes], sems.at[2 * i + 1]))
    copies.append(pltpu.make_async_copy(trans0_hbm, trans0, sems.at[2 * CHUNKS]))
    for copy in copies:
        copy.start()
    for i in range(CHUNKS):
        copies[2 * i].wait()
        copies[2 * i + 1].wait()
        lax.fori_loop(i * tiles // CHUNKS, (i + 1) * tiles // CHUNKS, moments, 0, unroll=8)
    copies[2 * CHUNKS].wait()

    def leaf_coefs(r, carry):
        place = pl.ds(pl.multiple_of(r * K, K), K)
        for j0 in range(4):
            rows = leaf_rows[pl.ds(pl.multiple_of((j0 * R + r) * 128, 128), 128), :]
            coef0[j0, place, :] = jnp.transpose(rows)[0:K]
        return carry

    lax.fori_loop(0, R, leaf_coefs, 0, unroll=2)

    def digits_first(q, rows):
        parts = [
            columns[q, pl.ds(rows[0] * a + rows[1] * b + rows[2], 8, stride=rows[3]), :]
            for a in range(4)
            for b in range(4)
        ]
        return jnp.transpose(jnp.concatenate(parts, 0))

    def flip(source, entries):
        for q in range(8):
            columns[q, 0 : source.shape[0], :] = source[:, q * 128 : (q + 1) * 128]
        for q in range(8):
            for entry, rows in entries:
                et[entry, q * 128 : (q + 1) * 128, :] = digits_first(q, rows)

    flip(trans0, [(j0, (4, 16, j0, 64)) for j0 in range(4)])
    flip(trans1, [(4, (1, 4, 0, 16))])
    flip(trans2, [(5, (0, 1, 0, 4))])
    flip(trans3, [(6, (0, 0, 0, 1))])

    def lift_from(entry, vector, out, add):
        for b in range(K):
            by_column[b * K : (b + 1) * K, :] = et[entry, pl.ds(b, K, stride=K), :]
        matvec(lambda b: by_column[b * K : (b + 1) * K, :], vector, out, add)

    for j0 in range(4):
        lift_from(j0, coef0.at[j0], coef.at[0], j0 > 0)
    lift_from(4, coef.at[0], coef.at[1], False)
    fold(coef.at[1], (32, 64))
    lift_from(5, coef.at[1], coef.at[2], False)
    fold(coef.at[2], (8, 16))
    lift_from(6, coef.at[2], coef.at[3], False)

    j1, j2, c3 = lane_digits((1, 128), 1)
    for level, (prox, ids, rows) in enumerate(
        (
            (prox1, c3 * 16 + j2 * 4 + j1 + here * 128, (1, 4, 0, 16)),
            (prox2, c3 * 4 + j2 + here * 32, (0, 1, 0, 4)),
            (prox3, c3 + here * 8, (0, 0, 0, 1)),
        )
    ):
        if level == 0:
            columns[level, 0:128, :] = jnp.transpose(
                jnp.concatenate([prox[...], jnp.zeros((128 - 3 * K, 128), f32)], 0)
            )
        else:
            columns[level, 0 : prox.shape[0], :] = jnp.concatenate(
                [prox[...], jnp.zeros((prox.shape[0], 128 - 3 * K), f32)], 1
            )
        offsets = digits_first(level, rows)
        across, beside = centre_lanes(ids, 4**level)
        payload[level, 0:ROWS, :] = coef[level]
        payload[level, ROWS : ROWS + K, :] = across + float(4**level) * offsets[0:K]
        payload[level, ROWS + K : ROWS + 2 * K, :] = beside + 4.0 * offsets[K : 2 * K]
        payload[level, ROWS + 2 * K : WIDE, :] = offsets[2 * K : 3 * K]

    def flip_payload(source, width):
        for q in range(0, width, 128):
            size = min(128, width - q)
            block = source[q : q + size, :]
            if size < 128:
                block = jnp.concatenate([block, jnp.zeros((128 - size, 128), f32)], 0)
            flipped[:, q : q + 128] = jnp.transpose(block)

    last_rows = ([31, 63, 95, 127], [7, 15, 23, 31], [4, 5, 6, 7])
    first_rows = ([0, 32, 64, 96], [0, 8, 16, 24], [0, 1, 2, 3])
    last_out[...] = jnp.zeros_like(last_out)
    first_out[...] = jnp.zeros_like(first_out)
    for level in range(3):
        flip_payload(payload.at[level], WIDE)
        for i in range(4):
            target = level * 4 + i
            last_out[target : target + 1, :] = flipped[last_rows[level][i] : last_rows[level][i] + 1, 0:WIDE]
            first_out[target : target + 1, :] = flipped[first_rows[level][i] : first_rows[level][i] + 1, 0:WIDE]
    flip_payload(coef.at[3], ROWS)
    lifted[...] = flipped[0:8, 0:ROWS]


def upward_pass(basis, charge, trans0, trans1, trans2, trans3, prox1, prox2, prox3):
    vmem = pl.BlockSpec(memory_space=pltpu.VMEM)
    leaves = trans0.shape[0]
    return pl.pallas_call(
        up_kernel,
        out_shape=[
            jax.ShapeDtypeStruct((7, K * K, 128), f32),
            jax.ShapeDtypeStruct((3, WIDE, 128), f32),
            jax.ShapeDtypeStruct((EDGE, WIDE), f32),
            jax.ShapeDtypeStruct((EDGE, WIDE), f32),
            jax.ShapeDtypeStruct((8, ROWS), f32),
        ],
        in_specs=[pl.BlockSpec(memory_space=pltpu.HBM)] * 3 + [vmem] * 6,
        out_specs=[vmem] * 5,
        scratch_shapes=[
            pltpu.VMEM((leaves * R, 128), f32),
            pltpu.VMEM((4, ROWS, 128), f32),
            pltpu.VMEM((4, ROWS, 128), f32),
            pltpu.VMEM((128, 640), f32),
            pltpu.VMEM((8, leaves, 128), f32),
            pltpu.VMEM((K * K, 128), f32),
            pltpu.VMEM(basis.shape, f32),
            pltpu.VMEM(charge.shape, f32),
            pltpu.VMEM(trans0.shape, f32),
            pltpu.SemaphoreType.DMA((2 * CHUNKS + 1,)),
        ],
        compiler_params=pltpu.CompilerParams(vmem_limit_bytes=54 * 2**20),
        cost_estimate=pl.CostEstimate(
            flops=leaves * 200000, bytes_accessed=leaves * 20000, transcendentals=0
        ),
        name="upward_pass",
    )(basis, charge, trans0, trans1, trans2, trans3, prox1, prox2, prox3)


def down_kernel(
    tops, et_hbm, payload, low_halo, high_halo, lifted, top_row, prox_top, list1, list2, list3, basis_hbm, near_hbm,
    out, split_rows, split_top, split_place, top_column, gathered, green_rows, local, leaf_local, leaf_rows, columns,
    et, basis, near_field, sems,
):
    copies = [
        pltpu.make_async_copy(et_hbm, et, sems.at[0]),
        pltpu.make_async_copy(basis_hbm, basis, sems.at[1]),
        pltpu.make_async_copy(near_hbm, near_field, sems.at[2]),
    ]
    for copy in copies:
        copy.start()
    here = lax.axis_index("gx")
    top_count = prox_top.shape[0]
    j1, j2, c3 = lane_digits((1, 128), 1)

    def split_to(ref, columns, value):
        parts = split_three(value)
        for i in range(3):
            ref[i, :, columns] = parts[i].astype(bf16)

    def pick(ref, hot):
        hot = hot.astype(f32).astype(bf16)
        total = jnp.dot(ref[0], hot, preferred_element_type=f32)
        total = total + jnp.dot(ref[1], hot, preferred_element_type=f32)
        return total + jnp.dot(ref[2], hot, preferred_element_type=f32)

    def couple_picked(target, out_ref, add):
        def step(b, carry):
            square = None
            for axis_id in range(3):
                spread = target(axis_id) - gathered[pl.ds(ROWS + axis_id * K + b, 1), :]
                square = spread * spread if square is None else square + spread * spread
            green_rows[pl.ds(pl.multiple_of(b * K, K), K), :] = inv_four_pi * lax.rsqrt(square + soft_square)
            return carry

        lax.fori_loop(0, K, step, 0, unroll=4)
        matvec(lambda b: green_rows[b * K : (b + 1) * K, :], gathered, out_ref, add)

    def descend_from(entry, vector, out_ref, add):
        matvec(lambda a: et[entry, a * K : (a + 1) * K, :], vector, out_ref, add)

    my_top = jnp.zeros((1, 128), jnp.int32)
    for c in range(8):
        my_top = jnp.where(c3 == c, tops[here * 8 + c], my_top)
    def flip_top(block):
        rows, width = block.shape
        if width < 128:
            block = jnp.concatenate([block, jnp.zeros((rows, 128 - width), f32)], 1)
        if rows < 128:
            block = jnp.concatenate([block, jnp.zeros((128 - rows, 128), f32)], 0)
        return jnp.transpose(block)

    def keep(ref, first, q, value):
        parts = split_three(value)
        for i in range(3):
            ref[i, first : first + value.shape[0], q : q + 128] = parts[i].astype(bf16)

    cluster_count = lifted.shape[0]
    for q in range(0, split_top.shape[2], 128):
        rows = min(128, cluster_count - q)
        for w in range(0, ROWS, 128):
            keep(split_top, w, q, flip_top(lifted[q : q + rows, w : w + 128]))
        owners = top_row[:, q : q + rows].astype(f32)
        if rows < 128:
            owners = jnp.concatenate([owners, jnp.full((1, 128 - rows), -9.0, f32)], 1)
        top_column[q : q + 128, :] = jnp.transpose(jnp.broadcast_to(owners, (128, 128))).astype(jnp.int32)
    for q in range(0, split_place.shape[2], 128):
        offsets = flip_top(prox_top[q : q + min(128, top_count - q), :])
        across, beside = centre_lanes(lax.broadcasted_iota(jnp.int32, (1, 128), 1) + q, 64)
        keep(split_place, 0, q, across + 64.0 * offsets[0:K])
        keep(split_place, K, q, beside + 4.0 * offsets[K : 2 * K])
        keep(split_place, 2 * K, q, offsets[2 * K : 3 * K])
    top_rows = lax.broadcasted_iota(jnp.int32, (split_place.shape[2], 128), 0)
    leaf_local[0, 0 : 3 * K, :] = pick(split_place, top_rows == my_top)
    lane_block = lax.broadcasted_iota(jnp.int32, (1, 128), 1) >> 3
    local[0] = jnp.zeros((ROWS, 128), f32)

    def top_block(block, carry):
        source = block * 16 + lane_block
        wanted = jnp.where(jnp.abs(source - my_top) >= 2, source, -1)
        gathered[0:ROWS, :] = pick(split_top, top_column[...] == wanted)
        gathered[ROWS:WIDE, :] = pick(split_place, top_rows == wanted)
        couple_picked(lambda axis_id: leaf_local[0, axis_id * K : (axis_id + 1) * K, :], local.at[0], True)
        return carry

    lax.fori_loop(0, (top_count + 15) // 16, top_block, 0)
    fold(local.at[0], (8, 16, 32, 64))

    halo = jnp.concatenate([low_halo[...], high_halo[...], jnp.zeros((128 - 2 * EDGE, WIDE), f32)], 0)
    for w in range(0, WIDE, 128):
        size = min(128, WIDE - w)
        block = halo[:, w : w + size]
        if size < 128:
            block = jnp.concatenate([block, jnp.zeros((128, 128 - size), f32)], 1)
        parts = split_three(jnp.transpose(block))
        for i in range(3):
            split_rows[i, w : w + size, 128:256] = parts[i][0:size].astype(bf16)

    def lane_list(ref, rows, base):
        count = ref.shape[1]
        values = jnp.concatenate([(ref[...] - base).astype(f32), jnp.zeros((125, count), f32)], 0)
        if count < 128:
            values = jnp.concatenate([values, jnp.zeros((128, 128 - count), f32)], 1)
        columns[...] = jnp.transpose(values)
        parts = [
            columns[pl.ds(rows[0] * a + rows[1] * b, 8, stride=rows[2]), :] for a in range(4) for b in range(4)
        ]
        return jnp.transpose(jnp.concatenate(parts, 0)).astype(jnp.int32)

    source = lax.broadcasted_iota(jnp.int32, (256, 128), 0)
    edge = source - 128
    s1, s2, s3 = (source >> 5) & 3, (source >> 3) & 3, source & 7

    def source_ids(level, own, own_count, count):
        low = edge - 4 * level
        high = edge - EDGE - 4 * level
        ids = jnp.where(source < own_count, own, -1000)
        ids = jnp.where((low >= 0) & (low < 4), low - 4, ids)
        return jnp.where((high >= 0) & (high < 4), high + count, ids)

    def place_of(level):
        return lambda axis_id: payload[level, ROWS + axis_id * K : ROWS + (axis_id + 1) * K, :]

    picked = lane_list(list3, (0, 0, 1), here * 8)
    wanted = jnp.where(j2 == 0, picked[0:1], jnp.where(j2 == 1, picked[1:2], jnp.where(j2 == 2, picked[2:3], -5000)))
    split_to(split_rows, slice(0, 128), payload[2])
    gathered[...] = pick(split_rows, source_ids(2, s3, 8, 8) == wanted)
    couple_picked(place_of(2), local.at[1], False)
    fold(local.at[1], (8, 16))
    copies[0].wait()
    descend_from(6, local.at[0], local.at[1], True)

    picked = lane_list(list2, (0, 1, 4), here * 32)
    wanted = jnp.where(j1 == 0, picked[0:1], jnp.where(j1 == 1, picked[1:2], jnp.where(j1 == 2, picked[2:3], -5000)))
    split_to(split_rows, slice(0, 128), payload[1])
    gathered[...] = pick(split_rows, source_ids(1, s3 * 4 + s2, 32, 32) == wanted)
    couple_picked(place_of(1), local.at[0], False)
    fold(local.at[0], (32, 64))
    descend_from(5, local.at[1], local.at[0], True)

    picked = lane_list(list1, (1, 4, 16), here * 128)
    split_to(split_rows, slice(0, 128), payload[0])
    ids = source_ids(0, s3 * 16 + s2 * 4 + s1, 128, 128)
    for j in range(3):
        gathered[...] = pick(split_rows, ids == picked[j : j + 1])
        couple_picked(place_of(0), local.at[1], j > 0)
    descend_from(4, local.at[0], local.at[1], True)
    for j0 in range(4):
        descend_from(j0, local.at[1], leaf_local.at[j0], False)

    def leaf_terms(r, carry):
        place = pl.ds(pl.multiple_of(r * K, K), K)
        for j0 in range(4):
            high, low = split_two(leaf_local[j0, place, :])
            high, low = high.astype(f32), low.astype(f32)
            value = jnp.transpose(jnp.concatenate([high, high, low, jnp.zeros_like(low)], 0))
            for a in range(4):
                for b in range(4):
                    leaf_rows[pl.ds((b * 16 + a * 4 + j0) * R + r, 8, stride=64 * R), :] = value[
                        a * 32 + b * 8 : a * 32 + b * 8 + 8
                    ]
        return carry

    lax.fori_loop(0, R, leaf_terms, 0, unroll=2)
    half = lax.broadcasted_iota(jnp.int32, (R, 128), 1) < 64
    copies[1].wait()
    copies[2].wait()

    def potential(tile, carry):
        lanes = pl.ds(pl.multiple_of(tile * 256, 256), 256)
        high, low = split_two(basis[:, lanes])
        left = leaf_rows[pl.ds(pl.multiple_of(tile * 64, 64), 64), 0 : 3 * K].astype(bf16)
        total = jnp.dot(left, jnp.concatenate([high, low, high], 0), preferred_element_type=f32)
        one = jnp.where(half, total[0:16, 0:128], total[16:32, 0:128])
        two = jnp.where(half, total[32:48, 128:256], total[48:64, 128:256])
        out[:, lanes] = near_field[:, lanes] + jnp.concatenate([one, two], 1)
        return carry

    lax.fori_loop(0, basis.shape[1] // 256, potential, 0, unroll=8)


def downward_pass(
    tops, et, payload, low_halo, high_halo, lifted, prox_top, list1, list2, list3, basis, near_field
):
    vmem = pl.BlockSpec(memory_space=pltpu.VMEM)
    smem = pl.BlockSpec(memory_space=pltpu.SMEM)
    panels = basis.shape[1]
    hbm = pl.BlockSpec(memory_space=pltpu.HBM)
    cluster_lanes = (lifted.shape[0] + 127) // 128 * 128
    top_lanes = (prox_top.shape[0] + 127) // 128 * 128
    return pl.pallas_call(
        down_kernel,
        out_shape=jax.ShapeDtypeStruct((R, panels), f32),
        in_specs=[smem, hbm] + [vmem] * 9 + [hbm] * 2,
        out_specs=vmem,
        scratch_shapes=[
            pltpu.VMEM((3, WIDE, 256), bf16),
            pltpu.VMEM((3, ROWS, cluster_lanes), bf16),
            pltpu.VMEM((3, 3 * K, top_lanes), bf16),
            pltpu.VMEM((cluster_lanes, 128), jnp.int32),
            pltpu.VMEM((WIDE, 128), f32),
            pltpu.VMEM((K * K, 128), f32),
            pltpu.VMEM((2, ROWS, 128), f32),
            pltpu.VMEM((4, ROWS, 128), f32),
            pltpu.VMEM((panels // LEAF * R, 128), f32),
            pltpu.VMEM((128, 128), f32),
            pltpu.VMEM(et.shape, f32),
            pltpu.VMEM(basis.shape, f32),
            pltpu.VMEM(near_field.shape, f32),
            pltpu.SemaphoreType.DMA((3,)),
        ],
        compiler_params=pltpu.CompilerParams(vmem_limit_bytes=54 * 2**20),
        cost_estimate=pl.CostEstimate(
            flops=panels * 4000, bytes_accessed=panels * 400, transcendentals=panels * 20
        ),
        name="downward_pass",
    )(
        tops, et, payload, low_halo, high_halo, lifted, tops.reshape(1, -1), prox_top,
        list1, list2, list3, basis, near_field,
    )


def body(
    charge, jitter, basis, near, trans0, trans1, trans2, trans3,
    prox1, prox2, prox3, prox_top, list1, list2, list3, top_of,
):
    count = lax.axis_size("gx")
    forward = [(i, i + 1) for i in range(count - 1)]
    backward = [(target, source) for source, target in forward]
    low_leaves, high_leaves = leaf_halos(jitter, charge)
    et, payload, last, first, lifted = upward_pass(
        basis, charge, trans0, trans1, trans2, trans3, prox1.T, prox2, prox3
    )
    low_halo = lax.ppermute(last, "gx", forward)
    high_halo = lax.ppermute(first, "gx", backward)
    lifted = lax.all_gather(lifted, "gx", tiled=True)
    near_field = near_potential(near.T, jitter, charge, low_leaves, high_leaves)
    near_field, lifted = lax.optimization_barrier((near_field, lifted))
    return downward_pass(
        top_of, et, payload, low_halo, high_halo, lifted, prox_top, list1.T, list2.T, list3.T, basis, near_field
    )


def solution(mesh):
    placed = (
        P(None, ("groups", "gx")),
        P(None, ("groups", "gx")),
        P(None, ("groups", "gx")),
        P(("groups", "gx"), None),
        P(("groups", "gx"), None),
        P(("groups", "gx"), None),
        P(("groups", "gx"), None),
        P(("groups", "gx"), None),
        P(("groups", "gx"), None),
        P(("groups", "gx"), None),
        P(("groups", "gx"), None),
        P("groups", None),
        P(("groups", "gx"), None),
        P(("groups", "gx"), None),
        P(("groups", "gx"), None),
        P("groups"),
    )
    return jax.shard_map(
        body, mesh=mesh, in_specs=placed, out_specs=P(None, ("groups", "gx")), check_vma=False
    )
```

```python
import jax
import jax.numpy as jnp
from jax import lax
from jax.experimental import pallas as pl
from jax.experimental.pallas import tpu as pltpu
from jax.sharding import PartitionSpec as P

LEAF = 64
K = 32
R = 16
NREACH = 16


inv_four_pi = 0.07957747154594767
soft_square = 0.01
row_columns = 64


def leaf_halos(jitter, charge):
    count = lax.axis_size("gx")
    forward = [(i, i + 1) for i in range(count - 1)]
    backward = [(target, source) for source, target in forward]
    width = NREACH * LEAF
    last = jnp.concatenate([jitter[:, -width:], charge[:, -width:]], axis=0)
    first = jnp.concatenate([jitter[:, :width], charge[:, :width]], axis=0)
    return lax.ppermute(last, "gx", forward), lax.ppermute(first, "gx", backward)


def column_place(column):
    row_number = column >> 6
    middle = column & (row_columns - 1)
    across = jnp.where((row_number & 1) == 0, middle, row_columns - 1 - middle)
    return across.astype(jnp.float32), (4 * row_number).astype(jnp.float32)


GROUP = 16
BATCH = 8
bf16 = jnp.bfloat16
f32 = jnp.float32


def split_two(value):
    high = value.astype(bf16)
    return high, (value - high.astype(f32)).astype(bf16)


def split_three(value):
    first = value.astype(bf16).astype(f32)
    rest = value - first
    second = rest.astype(bf16).astype(f32)
    return first, second, rest - second


def lanes_of(tile):
    return pl.ds(pl.multiple_of(tile * 128, 128), 128)


def near_kernel(
    ids, own_jitter, own_charge, low_halo, high_halo, out, points, feats0, feats1, charges, targets0, targets1, kernels, weights
):
    halo_tiles = low_halo.shape[1] // 128
    own_tiles = own_jitter.shape[1] // 128
    here = lax.axis_index("gx")
    first_id = here * (2 * own_tiles) - NREACH
    high_side = jnp.where(lax.broadcasted_iota(jnp.int32, (1, 128), 1) < LEAF, 0.0, 1.0)
    left_half = lax.broadcasted_iota(jnp.int32, (32, 128), 1).astype(bf16) < 64
    row = lax.broadcasted_iota(jnp.int32, (8, 128), 0)
    is_three = row == 3
    is_four = row == 4
    below_five = row < 5
    one_three = jnp.where(is_three, 1.0, 0.0)
    one_four = jnp.where(is_four, 1.0, 0.0)

    def stage(tile, place, charge):
        number = tile + (here * own_tiles - halo_tiles)
        across, beside = column_place(number >> 1)
        beside = beside + (2 * (number & 1)).astype(f32)
        centre = jnp.where(row == 0, across, jnp.where(row == 1, beside + high_side, 0.0))
        points[:, lanes_of(tile)] = centre + jnp.concatenate([place, jnp.zeros((5, 128), f32)], 0)
        charge = charge * inv_four_pi
        charges[2 * tile] = jnp.concatenate(split_two(charge), 0)
        charges[2 * tile + 1] = jnp.concatenate(split_two(pltpu.roll(charge, 64, 1)), 0)

    def stage_halo(halo, first):
        def step(i, carry):
            stage(first + i, halo[0:3, lanes_of(i)], halo[3:19, lanes_of(i)])
            return carry

        lax.fori_loop(0, halo_tiles, step, 0, unroll=2)

    def stage_own(i, carry):
        stage(halo_tiles + i, own_jitter[:, lanes_of(i)], own_charge[:, lanes_of(i)])
        return carry

    stage_halo(low_halo, 0)
    stage_halo(high_halo, halo_tiles + own_tiles)
    lax.fori_loop(0, own_tiles, stage_own, 0, unroll=4)

    def back(slot):
        total = lax.dot_general(
            kernels[slot], weights[slot], (((1,), (1,)), ((), ())), preferred_element_type=f32
        )
        total = jnp.transpose(total[:LEAF] + total[LEAF:])
        return total[:R] + total[R:]

    def emit(first):
        parts = [back(slot) for slot in range(BATCH)]
        first = jnp.maximum(first, 0)
        for half in range(BATCH // 2):
            place = pl.ds(pl.multiple_of((first + 2 * half) * LEAF, 128), 128)
            out[:, place] = jnp.concatenate([parts[2 * half], parts[2 * half + 1]], 1)

    def fill(group, feats, targets, part, part_count):
        base = group * GROUP
        across, beside = column_place(((first_id + NREACH) >> 2) + group * (GROUP // 4))
        row_sign = jnp.where((((first_id + NREACH + base) >> 8) & 1) == 0, 1.5, -1.5)
        shift = jnp.where(row == 0, across + row_sign, jnp.where(row == 1, beside + 1.5, 0.0))

        def local(tile):
            place = points[:, lanes_of(tile)] - shift
            square = place * place
            return place, jnp.broadcast_to(square[0:1] + square[1:2] + square[2:3], (8, 128))

        def source_rows(i):
            place, square = local(base // 2 + i)
            rows = place * (-2.0) + jnp.where(is_three, square + soft_square, one_four)

            def put(entry, value):
                first, second, third = split_three(value)
                one = jnp.where(below_five, first, pltpu.roll(second, 5, 0))
                two = jnp.where(is_three, second, one)
                three = jnp.where(below_five, third + one_four, pltpu.roll(first, 5, 0))
                feats[entry] = jnp.concatenate([one, two, three, jnp.zeros_like(one)], 0).astype(bf16)

            put(2 * i, rows)
            put(2 * i + 1, pltpu.roll(rows, 64, 1))

        def target_rows(i):
            place, square = local(base // 2 + NREACH // 2 + i)
            first, second, third = split_three(place + jnp.where(is_four, square, one_three))
            one = jnp.where(below_five, first, pltpu.roll(first, 5, 0))
            two = jnp.where(below_five, second + one_three, pltpu.roll(second, 5, 0))
            three = jnp.where(below_five, jnp.where(is_four, third, first), pltpu.roll(third, 5, 0))
            rows = jnp.concatenate([one, two, three, jnp.zeros_like(one)], 0)
            targets[lanes_of(i), :] = jnp.transpose(rows).astype(bf16)

        sources = (GROUP + 2 * NREACH) // 2 // part_count
        for i in range(sources):
            source_rows(part * sources + i)
        own = GROUP // 2 // part_count
        for i in range(own):
            target_rows(part * own + i)

    def front(base, leaf, slot, feats, targets):
        target = targets[pl.ds(pl.multiple_of(leaf * LEAF, LEAF), LEAF), :]
        entry = base + leaf
        for j in range(4):
            sides = []
            for h in range(2):
                one = ids[4 * j + 2 * h, entry] - first_id
                two = (ids[4 * j + 2 * h + 1, entry] - first_id) ^ 1
                sides.append(jnp.where(left_half, feats[one - base], feats[two - base]))
                weights[slot, :, (2 * j + h) * 128 : (2 * j + h + 1) * 128] = jnp.where(
                    left_half, charges[one], charges[two]
                )
            square = jnp.dot(target, jnp.concatenate(sides, 1), preferred_element_type=f32)
            high, low = split_two(lax.rsqrt(square))
            kernels[slot, 0:LEAF, j * 256 : (j + 1) * 256] = high
            kernels[slot, LEAF : 2 * LEAF, j * 256 : (j + 1) * 256] = low

    group_count = own_tiles * 2 // GROUP

    def do_two_groups(i, carry):
        for half in range(2):
            now = (feats0, targets0) if half == 0 else (feats1, targets1)
            later = (feats1, targets1) if half == 0 else (feats0, targets0)
            group = 2 * i + half
            following = jnp.minimum(group + 1, group_count - 1)

            def step(part, inner):
                emit(group * GROUP + BATCH * part - BATCH)
                for slot in range(BATCH):
                    front(group * GROUP, BATCH * part + slot, slot, *now)
                fill(following, *later, part, GROUP // BATCH)
                return inner

            lax.fori_loop(0, GROUP // BATCH, step, 0)
        return carry

    kernels[...] = jnp.zeros_like(kernels)
    weights[...] = jnp.zeros_like(weights)
    fill(0, feats0, targets0, 0, 1)
    lax.fori_loop(0, group_count // 2, do_two_groups, 0)
    emit(own_tiles * 2 - BATCH)


def near_potential(ids, own_jitter, own_charge, low_halo, high_halo):
    panels = own_jitter.shape[1]
    leaves = (panels + 2 * low_halo.shape[1]) // LEAF
    pairs = panels * 16 * LEAF
    vmem = pl.BlockSpec(memory_space=pltpu.VMEM)
    smem = pl.BlockSpec(memory_space=pltpu.SMEM)
    return pl.pallas_call(
        near_kernel,
        out_shape=jax.ShapeDtypeStruct((R, panels), f32),
        in_specs=[smem, vmem, vmem, vmem, vmem],
        out_specs=vmem,
        scratch_shapes=[
            pltpu.VMEM((8, leaves * LEAF), f32),
            pltpu.VMEM((GROUP + 2 * NREACH, 32, 128), bf16),
            pltpu.VMEM((GROUP + 2 * NREACH, 32, 128), bf16),
            pltpu.VMEM((leaves, 2 * R, 128), bf16),
            pltpu.VMEM((GROUP * LEAF, 32), bf16),
            pltpu.VMEM((GROUP * LEAF, 32), bf16),
            pltpu.VMEM((BATCH, 2 * LEAF, 16 * LEAF), bf16),
            pltpu.VMEM((BATCH, 2 * R, 16 * LEAF), bf16),
        ],
        compiler_params=pltpu.CompilerParams(vmem_limit_bytes=16 * 2**20),
        cost_estimate=pl.CostEstimate(
            flops=pairs * 192, bytes_accessed=panels * 160, transcendentals=pairs
        ),
        name="near_potential",
    )(ids, own_jitter, own_charge, low_halo, high_halo)


EDGE = 16
CHUNKS = 4
ROWS = R * K
WIDE = ROWS + 3 * K


def lane_digits(shape, dim):
    index = lax.broadcasted_iota(jnp.int32, shape, dim)
    return index >> 5, (index >> 3) & 3, index & 7


def lane_of_tile(tile):
    return (tile & 3) * 32 + ((tile >> 2) & 3) * 8 + (tile >> 4)


def matvec(matrix, vector, out, add, for_rows=4):

    def step(block, carry):
        start = pl.multiple_of(block * for_rows * K, for_rows * K)
        sums = [jnp.zeros((K, 128), f32) for _ in range(for_rows)]
        for column in range(K):
            values = matrix(column)
            for i in range(for_rows):
                sums[i] = sums[i] + values * vector[pl.ds(start + i * K + column, 1), :]
        for i in range(for_rows):
            place = pl.ds(start + i * K, K)
            out[place, :] = out[place, :] + sums[i] if add else sums[i]
        return carry

    lax.fori_loop(0, R // for_rows, step, 0)


def matvec_packed(matrix, vector, packed, out, add, shifts=()):
    block = lane_digits((1, 128), 1)[0]
    for i in range(4):
        value = vector[i * K : (i + 1) * K, :]
        for q in range(1, 4):
            value = jnp.where(block == q, vector[(4 * q + i) * K : (4 * q + i + 1) * K, :], value)
        packed[i * K : (i + 1) * K, :] = value
    sums = [jnp.zeros((K, 128), f32) for _ in range(4)]
    for column in range(K):
        values = matrix(column)
        for i in range(4):
            sums[i] = sums[i] + values * packed[i * K + column : i * K + column + 1, :]
    for i in range(4):
        for q in range(4):
            part = jnp.where(block == q, sums[i], 0.0)
            for shift in (32, 64) + tuple(shifts):
                part = part + pltpu.roll(part, shift, 1)
            place = slice((4 * q + i) * K, (4 * q + i + 1) * K)
            out[place, :] = out[place, :] + part if add else part


def fold(ref, shifts):
    def step(i, carry):
        place = pl.ds(pl.multiple_of(i * 64, 64), 64)
        value = ref[place, :]
        for shift in shifts:
            value = value + pltpu.roll(value, shift, 1)
        ref[place, :] = value
        return carry

    lax.fori_loop(0, ROWS // 64, step, 0)


def centre_lanes(ids, level_width):
    first = ids * level_width
    row_number = first >> 6
    middle = (first & (row_columns - 1)).astype(f32) + 0.5 * (level_width - 1)
    across = jnp.where((row_number & 1) == 0, middle, row_columns - 1 - middle)
    return across, 4.0 * row_number.astype(f32) + 1.5


def up_kernel(
    tops, basis_hbm, charge_hbm, trans0_hbm, trans1, trans2, trans3, prox1, prox2, prox3,
    et, payload, last_out, first_out, terms, leaf_rows, coef0, coef, flipped, columns, by_column, packed, basis, charge, trans0, sems,
):
    here = lax.axis_index("gx")
    quarter = lax.broadcasted_iota(jnp.int32, (R, 256), 1).astype(f32)

    def moments(tile, carry):
        lanes = pl.ds(pl.multiple_of(tile * 256, 256), 256)
        high, low = split_two(basis[:, lanes])
        right = jnp.concatenate([high, low, high], 1)
        value = charge[:, lanes]
        pieces = [
            split_two(jnp.where((quarter >= 64.0 * i) & (quarter < 64.0 * (i + 1)), value, 0.0))
            for i in range(4)
        ]
        highs = jnp.concatenate([p[0] for p in pieces], 0)
        lows = jnp.concatenate([p[1] for p in pieces], 0)
        left = jnp.concatenate([highs, highs, lows], 1)
        total = lax.dot_general(left, right, (((1,), (1,)), ((), ())), preferred_element_type=f32)
        total = jnp.concatenate([total, jnp.zeros((64, 128 - K), f32)], 1)
        leaf_rows[pl.ds(lane_of_tile(tile), 64, stride=128), :] = total
        return carry

    tiles = basis.shape[1] // 256
    chunk = basis.shape[1] // CHUNKS
    copies = []
    for i in range(CHUNKS):
        lanes = pl.ds(i * chunk, chunk)
        copies.append(pltpu.make_async_copy(basis_hbm.at[:, lanes], basis.at[:, lanes], sems.at[2 * i]))
        copies.append(pltpu.make_async_copy(charge_hbm.at[:, lanes], charge.at[:, lanes], sems.at[2 * i + 1]))
    copies.append(pltpu.make_async_copy(trans0_hbm, trans0, sems.at[2 * CHUNKS]))
    for copy in copies:
        copy.start()
    for i in range(CHUNKS):
        copies[2 * i].wait()
        copies[2 * i + 1].wait()
        lax.fori_loop(i * tiles // CHUNKS, (i + 1) * tiles // CHUNKS, moments, 0, unroll=8)
    copies[2 * CHUNKS].wait()

    def leaf_coefs(r, carry):
        place = pl.ds(pl.multiple_of(r * K, K), K)
        for j0 in range(4):
            rows = leaf_rows[pl.ds(pl.multiple_of((j0 * R + r) * 128, 128), 128), :]
            coef0[j0, place, :] = jnp.transpose(rows)[0:K]
        return carry

    lax.fori_loop(0, R, leaf_coefs, 0, unroll=2)

    def digits_first(q, rows):
        parts = [
            columns[q, pl.ds(rows[0] * a + rows[1] * b + rows[2], 8, stride=rows[3]), :]
            for a in range(4)
            for b in range(4)
        ]
        return jnp.transpose(jnp.concatenate(parts, 0))

    def flip(source, entries):
        for q in range(8):
            columns[q, 0 : source.shape[0], :] = source[:, q * 128 : (q + 1) * 128]
        for q in range(8):
            for entry, rows in entries:
                et[entry, q * 128 : (q + 1) * 128, :] = digits_first(q, rows)

    flip(trans0, [(j0, (4, 16, j0, 64)) for j0 in range(4)])
    flip(trans1, [(4, (1, 4, 0, 16))])
    flip(trans2, [(5, (0, 1, 0, 4))])
    flip(trans3, [(6, (0, 0, 0, 1))])

    def lift_from(entry, vector, out, add):
        for b in range(K):
            by_column[b * K : (b + 1) * K, :] = et[entry, pl.ds(b, K, stride=K), :]
        if entry < 5:
            matvec(lambda b: by_column[b * K : (b + 1) * K, :], vector, out, add)
        else:
            shifts = (8, 16) if entry == 5 else ()
            matvec_packed(lambda b: by_column[b * K : (b + 1) * K, :], vector, packed, out, add, shifts)

    for j0 in range(4):
        lift_from(j0, coef0.at[j0], coef.at[0], j0 > 0)
    lift_from(4, coef.at[0], coef.at[1], False)
    fold(coef.at[1], (32, 64))
    lift_from(5, coef.at[1], coef.at[2], False)
    lift_from(6, coef.at[2], coef.at[3], False)

    j1, j2, c3 = lane_digits((1, 128), 1)
    for level, (prox, ids, rows) in enumerate(
        (
            (prox1, c3 * 16 + j2 * 4 + j1 + here * 128, (1, 4, 0, 16)),
            (prox2, c3 * 4 + j2 + here * 32, (0, 1, 0, 4)),
            (prox3, c3 + here * 8, (0, 0, 0, 1)),
        )
    ):
        if level == 0:
            columns[level, 0:128, :] = jnp.transpose(
                jnp.concatenate([prox[...], jnp.zeros((128 - 3 * K, 128), f32)], 0)
            )
        else:
            columns[level, 0 : prox.shape[0], :] = jnp.concatenate(
                [prox[...], jnp.zeros((prox.shape[0], 128 - 3 * K), f32)], 1
            )
        offsets = digits_first(level, rows)
        across, beside = centre_lanes(ids, 4**level)
        payload[level, 0:ROWS, :] = coef[level]
        payload[level, ROWS : ROWS + K, :] = across + float(4**level) * offsets[0:K]
        payload[level, ROWS + K : ROWS + 2 * K, :] = beside + 4.0 * offsets[K : 2 * K]
        payload[level, ROWS + 2 * K : WIDE, :] = offsets[2 * K : 3 * K]

    def flip_payload(source, width):
        for q in range(0, width, 128):
            size = min(128, width - q)
            block = source[q : q + size, :]
            if size < 128:
                block = jnp.concatenate([block, jnp.zeros((128 - size, 128), f32)], 0)
            flipped[:, q : q + 128] = jnp.transpose(block)

    last_rows = ([31, 63, 95, 127], [7, 15, 23, 31], [4, 5, 6, 7])
    first_rows = ([0, 32, 64, 96], [0, 8, 16, 24], [0, 1, 2, 3])
    last_out[...] = jnp.zeros_like(last_out)
    first_out[...] = jnp.zeros_like(first_out)
    for level in range(3):
        flip_payload(payload.at[level], WIDE)
        for i in range(4):
            target = level * 4 + i
            last_out[target : target + 1, :] = flipped[last_rows[level][i] : last_rows[level][i] + 1, 0:WIDE]
            first_out[target : target + 1, :] = flipped[first_rows[level][i] : first_rows[level][i] + 1, 0:WIDE]
    flip_payload(coef.at[3], ROWS)
    top_ids = lax.broadcasted_iota(jnp.int32, terms.shape, 0)
    total = jnp.zeros(terms.shape, f32)
    for c in range(8):
        total = total + jnp.where(top_ids == tops[here * 8 + c], flipped[c : c + 1, 0:ROWS], 0.0)
    terms[...] = total


def upward_pass(tops, basis, charge, trans0, trans1, trans2, trans3, prox1, prox2, prox3, top_count):
    vmem = pl.BlockSpec(memory_space=pltpu.VMEM)
    leaves = trans0.shape[0]
    return pl.pallas_call(
        up_kernel,
        out_shape=[
            jax.ShapeDtypeStruct((7, K * K, 128), f32),
            jax.ShapeDtypeStruct((3, WIDE, 128), f32),
            jax.ShapeDtypeStruct((EDGE, WIDE), f32),
            jax.ShapeDtypeStruct((EDGE, WIDE), f32),
            jax.ShapeDtypeStruct((top_count, ROWS), f32),
        ],
        in_specs=[pl.BlockSpec(memory_space=pltpu.SMEM)] + [pl.BlockSpec(memory_space=pltpu.HBM)] * 3 + [vmem] * 6,
        out_specs=[vmem] * 5,
        scratch_shapes=[
            pltpu.VMEM((leaves * R, 128), f32),
            pltpu.VMEM((4, ROWS, 128), f32),
            pltpu.VMEM((4, ROWS, 128), f32),
            pltpu.VMEM((128, 640), f32),
            pltpu.VMEM((8, leaves, 128), f32),
            pltpu.VMEM((K * K, 128), f32),
            pltpu.VMEM((4 * K, 128), f32),
            pltpu.VMEM(basis.shape, f32),
            pltpu.VMEM(charge.shape, f32),
            pltpu.VMEM(trans0.shape, f32),
            pltpu.SemaphoreType.DMA((2 * CHUNKS + 1,)),
        ],
        compiler_params=pltpu.CompilerParams(vmem_limit_bytes=54 * 2**20),
        cost_estimate=pl.CostEstimate(
            flops=leaves * 200000, bytes_accessed=leaves * 20000, transcendentals=0
        ),
        name="upward_pass",
    )(tops, basis, charge, trans0, trans1, trans2, trans3, prox1, prox2, prox3)


def down_kernel(
    tops, et_hbm, payload, low_halo, high_halo, coef_top, prox_top, list1, list2, list3, basis_hbm, near_hbm,
    out, split_rows, split_top, split_place, gathered, green_rows, local, leaf_local, leaf_rows, columns, packed,
    et, basis, near_field, sems,
):
    copies = [
        pltpu.make_async_copy(et_hbm, et, sems.at[0]),
        pltpu.make_async_copy(basis_hbm, basis, sems.at[1]),
        pltpu.make_async_copy(near_hbm, near_field, sems.at[2]),
    ]
    for copy in copies:
        copy.start()
    here = lax.axis_index("gx")
    top_count = prox_top.shape[0]
    j1, j2, c3 = lane_digits((1, 128), 1)

    def split_to(ref, columns, value):
        parts = split_three(value)
        for i in range(3):
            ref[i, :, columns] = parts[i].astype(bf16)

    def pick(ref, hot):
        hot = hot.astype(f32).astype(bf16)
        total = jnp.dot(ref[0], hot, preferred_element_type=f32)
        total = total + jnp.dot(ref[1], hot, preferred_element_type=f32)
        return total + jnp.dot(ref[2], hot, preferred_element_type=f32)

    def couple_picked(target, out_ref, add, shifts=None):
        def step(b, carry):
            square = None
            for axis_id in range(3):
                spread = target(axis_id) - gathered[pl.ds(ROWS + axis_id * K + b, 1), :]
                square = spread * spread if square is None else square + spread * spread
            green_rows[pl.ds(pl.multiple_of(b * K, K), K), :] = inv_four_pi * lax.rsqrt(square + soft_square)
            return carry

        lax.fori_loop(0, K, step, 0, unroll=4)
        if shifts is None:
            matvec(lambda b: green_rows[b * K : (b + 1) * K, :], gathered, out_ref, add)
        else:
            matvec_packed(lambda b: green_rows[b * K : (b + 1) * K, :], gathered, packed, out_ref, add, shifts)

    def descend_from(entry, vector, out_ref, add):
        if entry < 5:
            matvec(lambda a: et[entry, a * K : (a + 1) * K, :], vector, out_ref, add)
        else:
            matvec_packed(lambda a: et[entry, a * K : (a + 1) * K, :], vector, packed, out_ref, add)

    my_top = jnp.zeros((1, 128), jnp.int32)
    for c in range(8):
        my_top = jnp.where(c3 == c, tops[here * 8 + c], my_top)
    def flip_top(block):
        rows, width = block.shape
        if width < 128:
            block = jnp.concatenate([block, jnp.zeros((rows, 128 - width), f32)], 1)
        if rows < 128:
            block = jnp.concatenate([block, jnp.zeros((128 - rows, 128), f32)], 0)
        return jnp.transpose(block)

    def keep(ref, first, q, value):
        parts = split_three(value)
        for i in range(3):
            ref[i, first : first + value.shape[0], q : q + 128] = parts[i].astype(bf16)

    for q in range(0, split_top.shape[2], 128):
        for w in range(0, ROWS, 128):
            keep(split_top, w, q, flip_top(coef_top[q : q + min(128, top_count - q), w : w + 128]))
        offsets = flip_top(prox_top[q : q + min(128, top_count - q), :])
        across, beside = centre_lanes(lax.broadcasted_iota(jnp.int32, (1, 128), 1) + q, 64)
        keep(split_place, 0, q, across + 64.0 * offsets[0:K])
        keep(split_place, K, q, beside + 4.0 * offsets[K : 2 * K])
        keep(split_place, 2 * K, q, offsets[2 * K : 3 * K])
    top_rows = lax.broadcasted_iota(jnp.int32, (split_place.shape[2], 128), 0)
    leaf_local[0, 0 : 3 * K, :] = pick(split_place, top_rows == my_top)
    lane_block = lax.broadcasted_iota(jnp.int32, (1, 128), 1) >> 3
    local[0] = jnp.zeros((ROWS, 128), f32)

    def top_block(block, carry):
        source = block * 16 + lane_block
        wanted = jnp.where(jnp.abs(source - my_top) >= 2, source, -1)
        gathered[0:ROWS, :] = pick(split_top, top_rows == wanted)
        gathered[ROWS:WIDE, :] = pick(split_place, top_rows == wanted)
        couple_picked(lambda axis_id: leaf_local[0, axis_id * K : (axis_id + 1) * K, :], local.at[0], True)
        return carry

    lax.fori_loop(0, (top_count + 15) // 16, top_block, 0)
    fold(local.at[0], (8, 16, 32, 64))

    halo = jnp.concatenate([low_halo[...], high_halo[...], jnp.zeros((128 - 2 * EDGE, WIDE), f32)], 0)
    for w in range(0, WIDE, 128):
        size = min(128, WIDE - w)
        block = halo[:, w : w + size]
        if size < 128:
            block = jnp.concatenate([block, jnp.zeros((128, 128 - size), f32)], 1)
        parts = split_three(jnp.transpose(block))
        for i in range(3):
            split_rows[i, w : w + size, 128:256] = parts[i][0:size].astype(bf16)

    def lane_list(ref, rows, base):
        count = ref.shape[1]
        values = jnp.concatenate([(ref[...] - base).astype(f32), jnp.zeros((125, count), f32)], 0)
        if count < 128:
            values = jnp.concatenate([values, jnp.zeros((128, 128 - count), f32)], 1)
        columns[...] = jnp.transpose(values)
        parts = [
            columns[pl.ds(rows[0] * a + rows[1] * b, 8, stride=rows[2]), :] for a in range(4) for b in range(4)
        ]
        return jnp.transpose(jnp.concatenate(parts, 0)).astype(jnp.int32)

    source = lax.broadcasted_iota(jnp.int32, (256, 128), 0)
    edge = source - 128
    s1, s2, s3 = (source >> 5) & 3, (source >> 3) & 3, source & 7

    def source_ids(level, own, own_count, count):
        low = edge - 4 * level
        high = edge - EDGE - 4 * level
        ids = jnp.where(source < own_count, own, -1000)
        ids = jnp.where((low >= 0) & (low < 4), low - 4, ids)
        return jnp.where((high >= 0) & (high < 4), high + count, ids)

    def place_of(level):
        return lambda axis_id: payload[level, ROWS + axis_id * K : ROWS + (axis_id + 1) * K, :]

    picked = lane_list(list3, (0, 0, 1), here * 8)
    wanted = jnp.where(j2 == 0, picked[0:1], jnp.where(j2 == 1, picked[1:2], jnp.where(j2 == 2, picked[2:3], -5000)))
    split_to(split_rows, slice(0, 128), payload[2])
    gathered[...] = pick(split_rows, source_ids(2, s3, 8, 8) == wanted)
    couple_picked(place_of(2), local.at[1], False, (8, 16))
    copies[0].wait()
    descend_from(6, local.at[0], local.at[1], True)

    picked = lane_list(list2, (0, 1, 4), here * 32)
    wanted = jnp.where(j1 == 0, picked[0:1], jnp.where(j1 == 1, picked[1:2], jnp.where(j1 == 2, picked[2:3], -5000)))
    split_to(split_rows, slice(0, 128), payload[1])
    gathered[...] = pick(split_rows, source_ids(1, s3 * 4 + s2, 32, 32) == wanted)
    couple_picked(place_of(1), local.at[0], False)
    fold(local.at[0], (32, 64))
    descend_from(5, local.at[1], local.at[0], True)

    picked = lane_list(list1, (1, 4, 16), here * 128)
    split_to(split_rows, slice(0, 128), payload[0])
    ids = source_ids(0, s3 * 16 + s2 * 4 + s1, 128, 128)
    for j in range(3):
        gathered[...] = pick(split_rows, ids == picked[j : j + 1])
        couple_picked(place_of(0), local.at[1], j > 0)
    descend_from(4, local.at[0], local.at[1], True)
    for j0 in range(4):
        descend_from(j0, local.at[1], leaf_local.at[j0], False)

    def leaf_terms(r, carry):
        place = pl.ds(pl.multiple_of(r * K, K), K)
        for j0 in range(4):
            high, low = split_two(leaf_local[j0, place, :])
            high, low = high.astype(f32), low.astype(f32)
            value = jnp.transpose(jnp.concatenate([high, high, low, jnp.zeros_like(low)], 0))
            for a in range(4):
                for b in range(4):
                    leaf_rows[pl.ds((b * 16 + a * 4 + j0) * R + r, 8, stride=64 * R), :] = value[
                        a * 32 + b * 8 : a * 32 + b * 8 + 8
                    ]
        return carry

    lax.fori_loop(0, R, leaf_terms, 0, unroll=2)
    half = lax.broadcasted_iota(jnp.int32, (R, 128), 1) < 64
    copies[1].wait()
    copies[2].wait()

    def potential(tile, carry):
        lanes = pl.ds(pl.multiple_of(tile * 256, 256), 256)
        high, low = split_two(basis[:, lanes])
        left = leaf_rows[pl.ds(pl.multiple_of(tile * 64, 64), 64), 0 : 3 * K].astype(bf16)
        total = jnp.dot(left, jnp.concatenate([high, low, high], 0), preferred_element_type=f32)
        one = jnp.where(half, total[0:16, 0:128], total[16:32, 0:128])
        two = jnp.where(half, total[32:48, 128:256], total[48:64, 128:256])
        out[:, lanes] = near_field[:, lanes] + jnp.concatenate([one, two], 1)
        return carry

    lax.fori_loop(0, basis.shape[1] // 256, potential, 0, unroll=8)


def downward_pass(
    tops, et, payload, low_halo, high_halo, coef_top, prox_top, list1, list2, list3, basis, near_field
):
    vmem = pl.BlockSpec(memory_space=pltpu.VMEM)
    smem = pl.BlockSpec(memory_space=pltpu.SMEM)
    panels = basis.shape[1]
    hbm = pl.BlockSpec(memory_space=pltpu.HBM)
    top_lanes = (prox_top.shape[0] + 127) // 128 * 128
    return pl.pallas_call(
        down_kernel,
        out_shape=jax.ShapeDtypeStruct((R, panels), f32),
        in_specs=[smem, hbm] + [vmem] * 8 + [hbm] * 2,
        out_specs=vmem,
        scratch_shapes=[
            pltpu.VMEM((3, WIDE, 256), bf16),
            pltpu.VMEM((3, ROWS, top_lanes), bf16),
            pltpu.VMEM((3, 3 * K, top_lanes), bf16),
            pltpu.VMEM((WIDE, 128), f32),
            pltpu.VMEM((K * K, 128), f32),
            pltpu.VMEM((2, ROWS, 128), f32),
            pltpu.VMEM((4, ROWS, 128), f32),
            pltpu.VMEM((panels // LEAF * R, 128), f32),
            pltpu.VMEM((128, 128), f32),
            pltpu.VMEM((4 * K, 128), f32),
            pltpu.VMEM(et.shape, f32),
            pltpu.VMEM(basis.shape, f32),
            pltpu.VMEM(near_field.shape, f32),
            pltpu.SemaphoreType.DMA((3,)),
        ],
        compiler_params=pltpu.CompilerParams(vmem_limit_bytes=54 * 2**20),
        cost_estimate=pl.CostEstimate(
            flops=panels * 4000, bytes_accessed=panels * 400, transcendentals=panels * 20
        ),
        name="downward_pass",
    )(
        tops, et, payload, low_halo, high_halo, coef_top, prox_top,
        list1, list2, list3, basis, near_field,
    )


def body(
    charge, jitter, basis, near, trans0, trans1, trans2, trans3,
    prox1, prox2, prox3, prox_top, list1, list2, list3, top_of,
):
    count = lax.axis_size("gx")
    forward = [(i, i + 1) for i in range(count - 1)]
    backward = [(target, source) for source, target in forward]
    low_leaves, high_leaves = leaf_halos(jitter, charge)
    et, payload, last, first, terms = upward_pass(
        top_of, basis, charge, trans0, trans1, trans2, trans3, prox1.T, prox2, prox3, prox_top.shape[0]
    )
    low_halo = lax.ppermute(last, "gx", forward)
    high_halo = lax.ppermute(first, "gx", backward)
    coef_top = lax.psum(terms, "gx")
    near_field = near_potential(near.T, jitter, charge, low_leaves, high_leaves)
    near_field, coef_top = lax.optimization_barrier((near_field, coef_top))
    return downward_pass(
        top_of, et, payload, low_halo, high_halo, coef_top, prox_top, list1.T, list2.T, list3.T, basis, near_field
    )


def solution(mesh):
    placed = (
        P(None, ("groups", "gx")),
        P(None, ("groups", "gx")),
        P(None, ("groups", "gx")),
        P(("groups", "gx"), None),
        P(("groups", "gx"), None),
        P(("groups", "gx"), None),
        P(("groups", "gx"), None),
        P(("groups", "gx"), None),
        P(("groups", "gx"), None),
        P(("groups", "gx"), None),
        P(("groups", "gx"), None),
        P("groups", None),
        P(("groups", "gx"), None),
        P(("groups", "gx"), None),
        P(("groups", "gx"), None),
        P("groups"),
    )
    return jax.shard_map(
        body, mesh=mesh, in_specs=placed, out_specs=P(None, ("groups", "gx")), check_vma=False
    )
```

```python
import jax
import jax.numpy as jnp
from jax import lax
from jax.experimental import pallas as pl
from jax.experimental.pallas import tpu as pltpu
from jax.sharding import PartitionSpec as P

LEAF = 64
K = 32
R = 16
NREACH = 16


inv_four_pi = 0.07957747154594767
soft_square = 0.01
row_columns = 64


def leaf_halos(jitter, charge):
    count = lax.axis_size("gx")
    forward = [(i, i + 1) for i in range(count - 1)]
    backward = [(target, source) for source, target in forward]
    width = NREACH * LEAF
    last = jnp.concatenate([jitter[:, -width:], charge[:, -width:]], axis=0)
    first = jnp.concatenate([jitter[:, :width], charge[:, :width]], axis=0)
    return lax.ppermute(last, "gx", forward), lax.ppermute(first, "gx", backward)


def column_place(column):
    row_number = column >> 6
    middle = column & (row_columns - 1)
    across = jnp.where((row_number & 1) == 0, middle, row_columns - 1 - middle)
    return across.astype(jnp.float32), (4 * row_number).astype(jnp.float32)


GROUP = 16
BATCH = 16
bf16 = jnp.bfloat16
f32 = jnp.float32


def split_two(value):
    high = value.astype(bf16)
    return high, (value - high.astype(f32)).astype(bf16)


def split_three(value):
    first = value.astype(bf16).astype(f32)
    rest = value - first
    second = rest.astype(bf16).astype(f32)
    return first, second, rest - second


def lanes_of(tile):
    return pl.ds(pl.multiple_of(tile * 128, 128), 128)


def near_kernel(
    ids, own_jitter, own_charge, low_halo, high_halo, out, points, feats0, feats1, charges, targets0, targets1, kernels, weights
):
    halo_tiles = low_halo.shape[1] // 128
    own_tiles = own_jitter.shape[1] // 128
    here = lax.axis_index("gx")
    first_id = here * (2 * own_tiles) - NREACH
    high_side = jnp.where(lax.broadcasted_iota(jnp.int32, (1, 128), 1) < LEAF, 0.0, 1.0)
    left_half = lax.broadcasted_iota(jnp.int32, (32, 128), 1).astype(bf16) < 64
    row = lax.broadcasted_iota(jnp.int32, (8, 128), 0)
    is_three = row == 3
    is_four = row == 4
    below_five = row < 5
    one_three = jnp.where(is_three, 1.0, 0.0)
    one_four = jnp.where(is_four, 1.0, 0.0)

    def stage(tile, place, charge):
        number = tile + (here * own_tiles - halo_tiles)
        across, beside = column_place(number >> 1)
        beside = beside + (2 * (number & 1)).astype(f32)
        centre = jnp.where(row == 0, across, jnp.where(row == 1, beside + high_side, 0.0))
        points[:, lanes_of(tile)] = centre + jnp.concatenate([place, jnp.zeros((5, 128), f32)], 0)
        charge = charge * inv_four_pi
        charges[2 * tile] = jnp.concatenate(split_two(charge), 0)
        charges[2 * tile + 1] = jnp.concatenate(split_two(pltpu.roll(charge, 64, 1)), 0)

    def stage_halo(halo, first):
        def step(i, carry):
            stage(first + i, halo[0:3, lanes_of(i)], halo[3:19, lanes_of(i)])
            return carry

        lax.fori_loop(0, halo_tiles, step, 0, unroll=2)

    def stage_own(i, carry):
        stage(halo_tiles + i, own_jitter[:, lanes_of(i)], own_charge[:, lanes_of(i)])
        return carry

    stage_halo(low_halo, 0)
    stage_halo(high_halo, halo_tiles + own_tiles)
    lax.fori_loop(0, own_tiles, stage_own, 0, unroll=4)

    def back(slot):
        total = lax.dot_general(
            kernels[slot], weights[slot], (((1,), (1,)), ((), ())), preferred_element_type=f32
        )
        total = jnp.transpose(total[:LEAF] + total[LEAF:])
        return total[:R] + total[R:]

    def emit(first):
        parts = [back(slot) for slot in range(BATCH)]
        first = jnp.maximum(first, 0)
        for half in range(BATCH // 2):
            place = pl.ds(pl.multiple_of((first + 2 * half) * LEAF, 128), 128)
            out[:, place] = jnp.concatenate([parts[2 * half], parts[2 * half + 1]], 1)

    def fill(group, feats, targets, part, part_count):
        base = group * GROUP
        across, beside = column_place(((first_id + NREACH) >> 2) + group * (GROUP // 4))
        row_sign = jnp.where((((first_id + NREACH + base) >> 8) & 1) == 0, 1.5, -1.5)
        shift = jnp.where(row == 0, across + row_sign, jnp.where(row == 1, beside + 1.5, 0.0))

        def local(tile):
            place = points[:, lanes_of(tile)] - shift
            square = place * place
            return place, jnp.broadcast_to(square[0:1] + square[1:2] + square[2:3], (8, 128))

        def source_rows(i):
            place, square = local(base // 2 + i)
            rows = place * (-2.0) + jnp.where(is_three, square + soft_square, one_four)

            def put(entry, value):
                first, second, third = split_three(value)
                one = jnp.where(below_five, first, pltpu.roll(second, 5, 0))
                two = jnp.where(is_three, second, one)
                three = jnp.where(below_five, third + one_four, pltpu.roll(first, 5, 0))
                feats[entry] = jnp.concatenate([one, two, three, jnp.zeros_like(one)], 0).astype(bf16)

            put(2 * i, rows)
            put(2 * i + 1, pltpu.roll(rows, 64, 1))

        def target_rows(i):
            place, square = local(base // 2 + NREACH // 2 + i)
            first, second, third = split_three(place + jnp.where(is_four, square, one_three))
            one = jnp.where(below_five, first, pltpu.roll(first, 5, 0))
            two = jnp.where(below_five, second + one_three, pltpu.roll(second, 5, 0))
            three = jnp.where(below_five, jnp.where(is_four, third, first), pltpu.roll(third, 5, 0))
            rows = jnp.concatenate([one, two, three, jnp.zeros_like(one)], 0)
            targets[lanes_of(i), :] = jnp.transpose(rows).astype(bf16)

        sources = (GROUP + 2 * NREACH) // 2 // part_count
        for i in range(sources):
            source_rows(part * sources + i)
        own = GROUP // 2 // part_count
        for i in range(own):
            target_rows(part * own + i)

    def front(base, leaf, slot, feats, targets):
        target = targets[pl.ds(pl.multiple_of(leaf * LEAF, LEAF), LEAF), :]
        entry = base + leaf
        for j in range(4):
            sides = []
            for h in range(2):
                one = ids[4 * j + 2 * h, entry] - first_id
                two = (ids[4 * j + 2 * h + 1, entry] - first_id) ^ 1
                sides.append(jnp.where(left_half, feats[one - base], feats[two - base]))
                weights[slot, :, (2 * j + h) * 128 : (2 * j + h + 1) * 128] = jnp.where(
                    left_half, charges[one], charges[two]
                )
            square = jnp.dot(target, jnp.concatenate(sides, 1), preferred_element_type=f32)
            high, low = split_two(lax.rsqrt(square))
            kernels[slot, 0:LEAF, j * 256 : (j + 1) * 256] = high
            kernels[slot, LEAF : 2 * LEAF, j * 256 : (j + 1) * 256] = low

    group_count = own_tiles * 2 // GROUP

    def do_two_groups(i, carry):
        for half in range(2):
            now = (feats0, targets0) if half == 0 else (feats1, targets1)
            later = (feats1, targets1) if half == 0 else (feats0, targets0)
            group = 2 * i + half
            following = jnp.minimum(group + 1, group_count - 1)

            def step(part, inner):
                emit(group * GROUP + BATCH * part - BATCH)
                for slot in range(BATCH):
                    front(group * GROUP, BATCH * part + slot, slot, *now)
                fill(following, *later, part, GROUP // BATCH)
                return inner

            lax.fori_loop(0, GROUP // BATCH, step, 0)
        return carry

    kernels[...] = jnp.zeros_like(kernels)
    weights[...] = jnp.zeros_like(weights)
    fill(0, feats0, targets0, 0, 1)
    lax.fori_loop(0, group_count // 2, do_two_groups, 0)
    emit(own_tiles * 2 - BATCH)


def near_potential(ids, own_jitter, own_charge, low_halo, high_halo):
    panels = own_jitter.shape[1]
    leaves = (panels + 2 * low_halo.shape[1]) // LEAF
    pairs = panels * 16 * LEAF
    vmem = pl.BlockSpec(memory_space=pltpu.VMEM)
    smem = pl.BlockSpec(memory_space=pltpu.SMEM)
    return pl.pallas_call(
        near_kernel,
        out_shape=jax.ShapeDtypeStruct((R, panels), f32),
        in_specs=[smem, vmem, vmem, vmem, vmem],
        out_specs=vmem,
        scratch_shapes=[
            pltpu.VMEM((8, leaves * LEAF), f32),
            pltpu.VMEM((GROUP + 2 * NREACH, 32, 128), bf16),
            pltpu.VMEM((GROUP + 2 * NREACH, 32, 128), bf16),
            pltpu.VMEM((leaves, 2 * R, 128), bf16),
            pltpu.VMEM((GROUP * LEAF, 32), bf16),
            pltpu.VMEM((GROUP * LEAF, 32), bf16),
            pltpu.VMEM((BATCH, 2 * LEAF, 16 * LEAF), bf16),
            pltpu.VMEM((BATCH, 2 * R, 16 * LEAF), bf16),
        ],
        compiler_params=pltpu.CompilerParams(vmem_limit_bytes=16 * 2**20),
        cost_estimate=pl.CostEstimate(
            flops=pairs * 192, bytes_accessed=panels * 160, transcendentals=pairs
        ),
        name="near_potential",
    )(ids, own_jitter, own_charge, low_halo, high_halo)


EDGE = 16
CHUNKS = 4
ROWS = R * K
WIDE = ROWS + 3 * K


def lane_digits(shape, dim):
    index = lax.broadcasted_iota(jnp.int32, shape, dim)
    return index >> 5, (index >> 3) & 3, index & 7


def lane_of_tile(tile):
    return (tile & 3) * 32 + ((tile >> 2) & 3) * 8 + (tile >> 4)


def matvec(matrix, vector, out, add, for_rows=4):

    def step(block, carry):
        start = pl.multiple_of(block * for_rows * K, for_rows * K)
        sums = [jnp.zeros((K, 128), f32) for _ in range(for_rows)]
        for column in range(K):
            values = matrix(column)
            for i in range(for_rows):
                sums[i] = sums[i] + values * vector[pl.ds(start + i * K + column, 1), :]
        for i in range(for_rows):
            place = pl.ds(start + i * K, K)
            out[place, :] = out[place, :] + sums[i] if add else sums[i]
        return carry

    lax.fori_loop(0, R // for_rows, step, 0)


def matvec_packed(matrix, vector, packed, out, add, shifts=()):
    block = lane_digits((1, 128), 1)[0]
    for i in range(4):
        value = vector[i * K : (i + 1) * K, :]
        for q in range(1, 4):
            value = jnp.where(block == q, vector[(4 * q + i) * K : (4 * q + i + 1) * K, :], value)
        packed[i * K : (i + 1) * K, :] = value
    sums = [jnp.zeros((K, 128), f32) for _ in range(4)]
    for column in range(K):
        values = matrix(column)
        for i in range(4):
            sums[i] = sums[i] + values * packed[i * K + column : i * K + column + 1, :]
    for i in range(4):
        for q in range(4):
            part = jnp.where(block == q, sums[i], 0.0)
            for shift in (32, 64) + tuple(shifts):
                part = part + pltpu.roll(part, shift, 1)
            place = slice((4 * q + i) * K, (4 * q + i + 1) * K)
            out[place, :] = out[place, :] + part if add else part


def fold(ref, shifts):
    def step(i, carry):
        place = pl.ds(pl.multiple_of(i * 64, 64), 64)
        value = ref[place, :]
        for shift in shifts:
            value = value + pltpu.roll(value, shift, 1)
        ref[place, :] = value
        return carry

    lax.fori_loop(0, ROWS // 64, step, 0)


def centre_lanes(ids, level_width):
    first = ids * level_width
    row_number = first >> 6
    middle = (first & (row_columns - 1)).astype(f32) + 0.5 * (level_width - 1)
    across = jnp.where((row_number & 1) == 0, middle, row_columns - 1 - middle)
    return across, 4.0 * row_number.astype(f32) + 1.5


def up_kernel(
    tops, basis_hbm, charge_hbm, trans0_hbm, trans1, trans2, trans3, prox1, prox2, prox3,
    et, payload, last_out, first_out, terms, leaf_rows, coef0, coef, flipped, columns, by_column, packed, basis, charge, trans0, sems,
):
    here = lax.axis_index("gx")
    quarter = lax.broadcasted_iota(jnp.int32, (R, 256), 1).astype(f32)

    def moments(tile, carry):
        lanes = pl.ds(pl.multiple_of(tile * 256, 256), 256)
        high, low = split_two(basis[:, lanes])
        right = jnp.concatenate([high, low, high], 1)
        value = charge[:, lanes]
        pieces = [
            split_two(jnp.where((quarter >= 64.0 * i) & (quarter < 64.0 * (i + 1)), value, 0.0))
            for i in range(4)
        ]
        highs = jnp.concatenate([p[0] for p in pieces], 0)
        lows = jnp.concatenate([p[1] for p in pieces], 0)
        left = jnp.concatenate([highs, highs, lows], 1)
        total = lax.dot_general(left, right, (((1,), (1,)), ((), ())), preferred_element_type=f32)
        total = jnp.concatenate([total, jnp.zeros((64, 128 - K), f32)], 1)
        leaf_rows[pl.ds(lane_of_tile(tile), 64, stride=128), :] = total
        return carry

    tiles = basis.shape[1] // 256
    chunk = basis.shape[1] // CHUNKS
    copies = []
    for i in range(CHUNKS):
        lanes = pl.ds(i * chunk, chunk)
        copies.append(pltpu.make_async_copy(basis_hbm.at[:, lanes], basis.at[:, lanes], sems.at[2 * i]))
        copies.append(pltpu.make_async_copy(charge_hbm.at[:, lanes], charge.at[:, lanes], sems.at[2 * i + 1]))
    copies.append(pltpu.make_async_copy(trans0_hbm, trans0, sems.at[2 * CHUNKS]))
    for copy in copies:
        copy.start()
    for i in range(CHUNKS):
        copies[2 * i].wait()
        copies[2 * i + 1].wait()
        lax.fori_loop(i * tiles // CHUNKS, (i + 1) * tiles // CHUNKS, moments, 0, unroll=8)
    copies[2 * CHUNKS].wait()

    def leaf_coefs(r, carry):
        place = pl.ds(pl.multiple_of(r * K, K), K)
        for j0 in range(4):
            rows = leaf_rows[pl.ds(pl.multiple_of((j0 * R + r) * 128, 128), 128), :]
            coef0[j0, place, :] = jnp.transpose(rows)[0:K]
        return carry

    lax.fori_loop(0, R, leaf_coefs, 0, unroll=2)

    def digits_first(q, rows):
        parts = [
            columns[q, pl.ds(rows[0] * a + rows[1] * b + rows[2], 8, stride=rows[3]), :]
            for a in range(4)
            for b in range(4)
        ]
        return jnp.transpose(jnp.concatenate(parts, 0))

    def flip(source, entries):
        for q in range(8):
            columns[q, 0 : source.shape[0], :] = source[:, q * 128 : (q + 1) * 128]
        for q in range(8):
            for entry, rows in entries:
                et[entry, q * 128 : (q + 1) * 128, :] = digits_first(q, rows)

    flip(trans0, [(j0, (4, 16, j0, 64)) for j0 in range(4)])
    flip(trans1, [(4, (1, 4, 0, 16))])
    flip(trans2, [(5, (0, 1, 0, 4))])
    flip(trans3, [(6, (0, 0, 0, 1))])

    def lift_from(entry, vector, out, add):
        for b in range(K):
            by_column[b * K : (b + 1) * K, :] = et[entry, pl.ds(b, K, stride=K), :]
        if entry < 5:
            matvec(lambda b: by_column[b * K : (b + 1) * K, :], vector, out, add)
        else:
            shifts = (8, 16) if entry == 5 else ()
            matvec_packed(lambda b: by_column[b * K : (b + 1) * K, :], vector, packed, out, add, shifts)

    for j0 in range(4):
        lift_from(j0, coef0.at[j0], coef.at[0], j0 > 0)
    lift_from(4, coef.at[0], coef.at[1], False)
    fold(coef.at[1], (32, 64))
    lift_from(5, coef.at[1], coef.at[2], False)
    lift_from(6, coef.at[2], coef.at[3], False)

    j1, j2, c3 = lane_digits((1, 128), 1)
    for level, (prox, ids, rows) in enumerate(
        (
            (prox1, c3 * 16 + j2 * 4 + j1 + here * 128, (1, 4, 0, 16)),
            (prox2, c3 * 4 + j2 + here * 32, (0, 1, 0, 4)),
            (prox3, c3 + here * 8, (0, 0, 0, 1)),
        )
    ):
        if level == 0:
            columns[level, 0:128, :] = jnp.transpose(
                jnp.concatenate([prox[...], jnp.zeros((128 - 3 * K, 128), f32)], 0)
            )
        else:
            columns[level, 0 : prox.shape[0], :] = jnp.concatenate(
                [prox[...], jnp.zeros((prox.shape[0], 128 - 3 * K), f32)], 1
            )
        offsets = digits_first(level, rows)
        across, beside = centre_lanes(ids, 4**level)
        payload[level, 0:ROWS, :] = coef[level]
        payload[level, ROWS : ROWS + K, :] = across + float(4**level) * offsets[0:K]
        payload[level, ROWS + K : ROWS + 2 * K, :] = beside + 4.0 * offsets[K : 2 * K]
        payload[level, ROWS + 2 * K : WIDE, :] = offsets[2 * K : 3 * K]

    def flip_payload(source, width):
        for q in range(0, width, 128):
            size = min(128, width - q)
            block = source[q : q + size, :]
            if size < 128:
                block = jnp.concatenate([block, jnp.zeros((128 - size, 128), f32)], 0)
            flipped[:, q : q + 128] = jnp.transpose(block)

    last_rows = ([31, 63, 95, 127], [7, 15, 23, 31], [4, 5, 6, 7])
    first_rows = ([0, 32, 64, 96], [0, 8, 16, 24], [0, 1, 2, 3])
    last_out[...] = jnp.zeros_like(last_out)
    first_out[...] = jnp.zeros_like(first_out)
    for level in range(3):
        flip_payload(payload.at[level], WIDE)
        for i in range(4):
            target = level * 4 + i
            last_out[target : target + 1, :] = flipped[last_rows[level][i] : last_rows[level][i] + 1, 0:WIDE]
            first_out[target : target + 1, :] = flipped[first_rows[level][i] : first_rows[level][i] + 1, 0:WIDE]
    flip_payload(coef.at[3], ROWS)
    top_ids = lax.broadcasted_iota(jnp.int32, terms.shape, 0)
    total = jnp.zeros(terms.shape, f32)
    for c in range(8):
        total = total + jnp.where(top_ids == tops[here * 8 + c], flipped[c : c + 1, 0:ROWS], 0.0)
    terms[...] = total


def upward_pass(tops, basis, charge, trans0, trans1, trans2, trans3, prox1, prox2, prox3, top_count):
    vmem = pl.BlockSpec(memory_space=pltpu.VMEM)
    leaves = trans0.shape[0]
    return pl.pallas_call(
        up_kernel,
        out_shape=[
            jax.ShapeDtypeStruct((7, K * K, 128), f32),
            jax.ShapeDtypeStruct((3, WIDE, 128), f32),
            jax.ShapeDtypeStruct((EDGE, WIDE), f32),
            jax.ShapeDtypeStruct((EDGE, WIDE), f32),
            jax.ShapeDtypeStruct((top_count, ROWS), f32),
        ],
        in_specs=[pl.BlockSpec(memory_space=pltpu.SMEM)] + [pl.BlockSpec(memory_space=pltpu.HBM)] * 3 + [vmem] * 6,
        out_specs=[vmem] * 5,
        scratch_shapes=[
            pltpu.VMEM((leaves * R, 128), f32),
            pltpu.VMEM((4, ROWS, 128), f32),
            pltpu.VMEM((4, ROWS, 128), f32),
            pltpu.VMEM((128, 640), f32),
            pltpu.VMEM((8, leaves, 128), f32),
            pltpu.VMEM((K * K, 128), f32),
            pltpu.VMEM((4 * K, 128), f32),
            pltpu.VMEM(basis.shape, f32),
            pltpu.VMEM(charge.shape, f32),
            pltpu.VMEM(trans0.shape, f32),
            pltpu.SemaphoreType.DMA((2 * CHUNKS + 1,)),
        ],
        compiler_params=pltpu.CompilerParams(vmem_limit_bytes=54 * 2**20),
        cost_estimate=pl.CostEstimate(
            flops=leaves * 200000, bytes_accessed=leaves * 20000, transcendentals=0
        ),
        name="upward_pass",
    )(tops, basis, charge, trans0, trans1, trans2, trans3, prox1, prox2, prox3)


def pick(ref, hot):
    hot = hot.astype(f32).astype(bf16)
    total = jnp.dot(ref[0], hot, preferred_element_type=f32)
    total = total + jnp.dot(ref[1], hot, preferred_element_type=f32)
    return total + jnp.dot(ref[2], hot, preferred_element_type=f32)


def couple_picked(gathered, green_rows, packed, target, out_ref, add, shifts=None):
    def step(b, carry):
        square = None
        for axis_id in range(3):
            spread = target(axis_id) - gathered[pl.ds(ROWS + axis_id * K + b, 1), :]
            square = spread * spread if square is None else square + spread * spread
        green_rows[pl.ds(pl.multiple_of(b * K, K), K), :] = inv_four_pi * lax.rsqrt(square + soft_square)
        return carry

    lax.fori_loop(0, K, step, 0, unroll=4)
    if shifts is None:
        matvec(lambda b: green_rows[b * K : (b + 1) * K, :], gathered, out_ref, add)
    else:
        matvec_packed(lambda b: green_rows[b * K : (b + 1) * K, :], gathered, packed, out_ref, add, shifts)


def couple_kernel(
    payload, low_halo, high_halo, list1, list2, list3, far, split_rows, gathered, green_rows, columns, packed
):
    here = lax.axis_index("gx")
    j1, j2, c3 = lane_digits((1, 128), 1)

    def split_to(ref, lanes, value):
        parts = split_three(value)
        for i in range(3):
            ref[i, :, lanes] = parts[i].astype(bf16)

    halo = jnp.concatenate([low_halo[...], high_halo[...], jnp.zeros((128 - 2 * EDGE, WIDE), f32)], 0)
    for w in range(0, WIDE, 128):
        size = min(128, WIDE - w)
        block = halo[:, w : w + size]
        if size < 128:
            block = jnp.concatenate([block, jnp.zeros((128, 128 - size), f32)], 1)
        parts = split_three(jnp.transpose(block))
        for i in range(3):
            split_rows[i, w : w + size, 128:256] = parts[i][0:size].astype(bf16)

    def lane_list(ref, rows, base):
        count = ref.shape[1]
        values = jnp.concatenate([(ref[...] - base).astype(f32), jnp.zeros((125, count), f32)], 0)
        if count < 128:
            values = jnp.concatenate([values, jnp.zeros((128, 128 - count), f32)], 1)
        columns[...] = jnp.transpose(values)
        parts = [
            columns[pl.ds(rows[0] * a + rows[1] * b, 8, stride=rows[2]), :] for a in range(4) for b in range(4)
        ]
        return jnp.transpose(jnp.concatenate(parts, 0)).astype(jnp.int32)

    source = lax.broadcasted_iota(jnp.int32, (256, 128), 0)
    edge = source - 128
    s1, s2, s3 = (source >> 5) & 3, (source >> 3) & 3, source & 7

    def source_ids(level, own, own_count, count):
        low = edge - 4 * level
        high = edge - EDGE - 4 * level
        ids = jnp.where(source < own_count, own, -1000)
        ids = jnp.where((low >= 0) & (low < 4), low - 4, ids)
        return jnp.where((high >= 0) & (high < 4), high + count, ids)

    def place_of(level):
        return lambda axis_id: payload[level, ROWS + axis_id * K : ROWS + (axis_id + 1) * K, :]

    picked = lane_list(list3, (0, 0, 1), here * 8)
    wanted = jnp.where(j2 == 0, picked[0:1], jnp.where(j2 == 1, picked[1:2], jnp.where(j2 == 2, picked[2:3], -5000)))
    split_to(split_rows, slice(0, 128), payload[2])
    gathered[...] = pick(split_rows, source_ids(2, s3, 8, 8) == wanted)
    couple_picked(gathered, green_rows, packed, place_of(2), far.at[2], False, (8, 16))

    picked = lane_list(list2, (0, 1, 4), here * 32)
    wanted = jnp.where(j1 == 0, picked[0:1], jnp.where(j1 == 1, picked[1:2], jnp.where(j1 == 2, picked[2:3], -5000)))
    split_to(split_rows, slice(0, 128), payload[1])
    gathered[...] = pick(split_rows, source_ids(1, s3 * 4 + s2, 32, 32) == wanted)
    couple_picked(gathered, green_rows, packed, place_of(1), far.at[1], False)
    fold(far.at[1], (32, 64))

    picked = lane_list(list1, (1, 4, 16), here * 128)
    split_to(split_rows, slice(0, 128), payload[0])
    ids = source_ids(0, s3 * 16 + s2 * 4 + s1, 128, 128)
    for j in range(3):
        gathered[...] = pick(split_rows, ids == picked[j : j + 1])
        couple_picked(gathered, green_rows, packed, place_of(0), far.at[0], j > 0)


def couplings(payload, low_halo, high_halo, list1, list2, list3):
    vmem = pl.BlockSpec(memory_space=pltpu.VMEM)
    return pl.pallas_call(
        couple_kernel,
        out_shape=jax.ShapeDtypeStruct((3, ROWS, 128), f32),
        in_specs=[vmem] * 6,
        out_specs=vmem,
        scratch_shapes=[
            pltpu.VMEM((3, WIDE, 256), bf16),
            pltpu.VMEM((WIDE, 128), f32),
            pltpu.VMEM((K * K, 128), f32),
            pltpu.VMEM((128, 128), f32),
            pltpu.VMEM((4 * K, 128), f32),
        ],
        compiler_params=pltpu.CompilerParams(vmem_limit_bytes=16 * 2**20),
        cost_estimate=pl.CostEstimate(flops=20000000, bytes_accessed=2000000, transcendentals=600000),
        name="couplings",
    )(payload, low_halo, high_halo, list1, list2, list3)


def down_kernel(
    tops, et_hbm, far, coef_top, prox_top, basis_hbm, near_hbm,
    out, split_top, split_place, gathered, green_rows, local, leaf_local, leaf_rows, packed,
    et, basis, near_field, sems,
):
    copies = [
        pltpu.make_async_copy(et_hbm, et, sems.at[0]),
        pltpu.make_async_copy(basis_hbm, basis, sems.at[1]),
        pltpu.make_async_copy(near_hbm, near_field, sems.at[2]),
    ]
    for copy in copies:
        copy.start()
    here = lax.axis_index("gx")
    top_count = prox_top.shape[0]
    j1, j2, c3 = lane_digits((1, 128), 1)

    def descend_from(entry, vector, out_ref, add):
        if entry < 5:
            matvec(lambda a: et[entry, a * K : (a + 1) * K, :], vector, out_ref, add)
        else:
            matvec_packed(lambda a: et[entry, a * K : (a + 1) * K, :], vector, packed, out_ref, add)

    my_top = jnp.zeros((1, 128), jnp.int32)
    for c in range(8):
        my_top = jnp.where(c3 == c, tops[here * 8 + c], my_top)
    def flip_top(block):
        rows, width = block.shape
        if width < 128:
            block = jnp.concatenate([block, jnp.zeros((rows, 128 - width), f32)], 1)
        if rows < 128:
            block = jnp.concatenate([block, jnp.zeros((128 - rows, 128), f32)], 0)
        return jnp.transpose(block)

    def keep(ref, first, q, value):
        parts = split_three(value)
        for i in range(3):
            ref[i, first : first + value.shape[0], q : q + 128] = parts[i].astype(bf16)

    for q in range(0, split_top.shape[2], 128):
        for w in range(0, ROWS, 128):
            keep(split_top, w, q, flip_top(coef_top[q : q + min(128, top_count - q), w : w + 128]))
        offsets = flip_top(prox_top[q : q + min(128, top_count - q), :])
        across, beside = centre_lanes(lax.broadcasted_iota(jnp.int32, (1, 128), 1) + q, 64)
        keep(split_place, 0, q, across + 64.0 * offsets[0:K])
        keep(split_place, K, q, beside + 4.0 * offsets[K : 2 * K])
        keep(split_place, 2 * K, q, offsets[2 * K : 3 * K])
    top_rows = lax.broadcasted_iota(jnp.int32, (split_place.shape[2], 128), 0)
    leaf_local[0, 0 : 3 * K, :] = pick(split_place, top_rows == my_top)
    lane_block = lax.broadcasted_iota(jnp.int32, (1, 128), 1) >> 3
    local[0] = jnp.zeros((ROWS, 128), f32)

    def top_block(block, carry):
        source = block * 16 + lane_block
        wanted = jnp.where(jnp.abs(source - my_top) >= 2, source, -1)
        gathered[0:ROWS, :] = pick(split_top, top_rows == wanted)
        gathered[ROWS:WIDE, :] = pick(split_place, top_rows == wanted)
        couple_picked(
            gathered, green_rows, packed,
            lambda axis_id: leaf_local[0, axis_id * K : (axis_id + 1) * K, :], local.at[0], True,
        )
        return carry

    lax.fori_loop(0, (top_count + 15) // 16, top_block, 0)
    fold(local.at[0], (8, 16, 32, 64))

    copies[0].wait()
    local[1] = far[2]
    descend_from(6, local.at[0], local.at[1], True)
    local[0] = far[1]
    descend_from(5, local.at[1], local.at[0], True)
    local[1] = far[0]
    descend_from(4, local.at[0], local.at[1], True)
    for j0 in range(4):
        descend_from(j0, local.at[1], leaf_local.at[j0], False)

    def leaf_terms(r, carry):
        place = pl.ds(pl.multiple_of(r * K, K), K)
        for j0 in range(4):
            high, low = split_two(leaf_local[j0, place, :])
            high, low = high.astype(f32), low.astype(f32)
            value = jnp.transpose(jnp.concatenate([high, high, low, jnp.zeros_like(low)], 0))
            for a in range(4):
                for b in range(4):
                    leaf_rows[pl.ds((b * 16 + a * 4 + j0) * R + r, 8, stride=64 * R), :] = value[
                        a * 32 + b * 8 : a * 32 + b * 8 + 8
                    ]
        return carry

    lax.fori_loop(0, R, leaf_terms, 0, unroll=2)
    half = lax.broadcasted_iota(jnp.int32, (R, 128), 1) < 64
    copies[1].wait()
    copies[2].wait()

    def potential(tile, carry):
        lanes = pl.ds(pl.multiple_of(tile * 256, 256), 256)
        high, low = split_two(basis[:, lanes])
        left = leaf_rows[pl.ds(pl.multiple_of(tile * 64, 64), 64), 0 : 3 * K].astype(bf16)
        total = jnp.dot(left, jnp.concatenate([high, low, high], 0), preferred_element_type=f32)
        one = jnp.where(half, total[0:16, 0:128], total[16:32, 0:128])
        two = jnp.where(half, total[32:48, 128:256], total[48:64, 128:256])
        out[:, lanes] = near_field[:, lanes] + jnp.concatenate([one, two], 1)
        return carry

    lax.fori_loop(0, basis.shape[1] // 256, potential, 0, unroll=8)


def downward_pass(
    tops, et, far, coef_top, prox_top, basis, near_field
):
    vmem = pl.BlockSpec(memory_space=pltpu.VMEM)
    smem = pl.BlockSpec(memory_space=pltpu.SMEM)
    panels = basis.shape[1]
    hbm = pl.BlockSpec(memory_space=pltpu.HBM)
    top_lanes = (prox_top.shape[0] + 127) // 128 * 128
    return pl.pallas_call(
        down_kernel,
        out_shape=jax.ShapeDtypeStruct((R, panels), f32),
        in_specs=[smem, hbm] + [vmem] * 3 + [hbm] * 2,
        out_specs=vmem,
        scratch_shapes=[
            pltpu.VMEM((3, ROWS, top_lanes), bf16),
            pltpu.VMEM((3, 3 * K, top_lanes), bf16),
            pltpu.VMEM((WIDE, 128), f32),
            pltpu.VMEM((K * K, 128), f32),
            pltpu.VMEM((2, ROWS, 128), f32),
            pltpu.VMEM((4, ROWS, 128), f32),
            pltpu.VMEM((panels // LEAF * R, 128), f32),
            pltpu.VMEM((4 * K, 128), f32),
            pltpu.VMEM(et.shape, f32),
            pltpu.VMEM(basis.shape, f32),
            pltpu.VMEM(near_field.shape, f32),
            pltpu.SemaphoreType.DMA((3,)),
        ],
        compiler_params=pltpu.CompilerParams(vmem_limit_bytes=54 * 2**20),
        cost_estimate=pl.CostEstimate(
            flops=panels * 4000, bytes_accessed=panels * 400, transcendentals=panels * 20
        ),
        name="downward_pass",
    )(
        tops, et, far, coef_top, prox_top, basis, near_field
    )


def body(
    charge, jitter, basis, near, trans0, trans1, trans2, trans3,
    prox1, prox2, prox3, prox_top, list1, list2, list3, top_of,
):
    count = lax.axis_size("gx")
    forward = [(i, i + 1) for i in range(count - 1)]
    backward = [(target, source) for source, target in forward]
    low_leaves, high_leaves = leaf_halos(jitter, charge)
    et, payload, last, first, terms = upward_pass(
        top_of, basis, charge, trans0, trans1, trans2, trans3, prox1.T, prox2, prox3, prox_top.shape[0]
    )
    low_halo = lax.ppermute(last, "gx", forward)
    high_halo = lax.ppermute(first, "gx", backward)
    coef_top = lax.psum(terms, "gx")
    near_field = near_potential(near.T, jitter, charge, low_leaves, high_leaves)
    near_field, low_halo, high_halo = lax.optimization_barrier((near_field, low_halo, high_halo))
    far = couplings(payload, low_halo, high_halo, list1.T, list2.T, list3.T)
    far, coef_top = lax.optimization_barrier((far, coef_top))
    return downward_pass(
        top_of, et, far, coef_top, prox_top, basis, near_field
    )


def solution(mesh):
    placed = (
        P(None, ("groups", "gx")),
        P(None, ("groups", "gx")),
        P(None, ("groups", "gx")),
        P(("groups", "gx"), None),
        P(("groups", "gx"), None),
        P(("groups", "gx"), None),
        P(("groups", "gx"), None),
        P(("groups", "gx"), None),
        P(("groups", "gx"), None),
        P(("groups", "gx"), None),
        P(("groups", "gx"), None),
        P("groups", None),
        P(("groups", "gx"), None),
        P(("groups", "gx"), None),
        P(("groups", "gx"), None),
        P("groups"),
    )
    return jax.shard_map(
        body, mesh=mesh, in_specs=placed, out_specs=P(None, ("groups", "gx")), check_vma=False
    )
```

```python
import jax
import jax.numpy as jnp
from jax import lax
from jax.experimental import pallas as pl
from jax.experimental.pallas import tpu as pltpu
from jax.sharding import PartitionSpec as P

LEAF = 64
K = 32
R = 16
NREACH = 16


inv_four_pi = 0.07957747154594767
soft_square = 0.01
row_columns = 64


def leaf_halos(jitter, charge):
    count = lax.axis_size("gx")
    forward = [(i, i + 1) for i in range(count - 1)]
    backward = [(target, source) for source, target in forward]
    width = NREACH * LEAF
    last = jnp.concatenate([jitter[:, -width:], charge[:, -width:]], axis=0)
    first = jnp.concatenate([jitter[:, :width], charge[:, :width]], axis=0)
    return lax.ppermute(last, "gx", forward), lax.ppermute(first, "gx", backward)


def column_place(column):
    row_number = column >> 6
    middle = column & (row_columns - 1)
    across = jnp.where((row_number & 1) == 0, middle, row_columns - 1 - middle)
    return across.astype(jnp.float32), (4 * row_number).astype(jnp.float32)


GROUP = 16
BATCH = 16
bf16 = jnp.bfloat16
f32 = jnp.float32


def split_two(value):
    high = value.astype(bf16)
    return high, (value - high.astype(f32)).astype(bf16)


def split_three(value):
    first = value.astype(bf16).astype(f32)
    rest = value - first
    second = rest.astype(bf16).astype(f32)
    return first, second, rest - second


def lanes_of(tile):
    return pl.ds(pl.multiple_of(tile * 128, 128), 128)


def near_kernel(
    ids, own_jitter, own_charge, low_halo, high_halo, out, points, feats0, feats1, charges, targets0, targets1, kernels, weights
):
    halo_tiles = low_halo.shape[1] // 128
    own_tiles = own_jitter.shape[1] // 128
    here = lax.axis_index("gx")
    first_id = here * (2 * own_tiles) - NREACH
    high_side = jnp.where(lax.broadcasted_iota(jnp.int32, (1, 128), 1) < LEAF, 0.0, 1.0)
    left_half = lax.broadcasted_iota(jnp.int32, (32, 128), 1).astype(bf16) < 64
    row = lax.broadcasted_iota(jnp.int32, (8, 128), 0)
    is_three = row == 3
    is_four = row == 4
    below_five = row < 5
    one_three = jnp.where(is_three, 1.0, 0.0)
    one_four = jnp.where(is_four, 1.0, 0.0)

    def stage(tile, place, charge):
        number = tile + (here * own_tiles - halo_tiles)
        across, beside = column_place(number >> 1)
        beside = beside + (2 * (number & 1)).astype(f32)
        centre = jnp.where(row == 0, across, jnp.where(row == 1, beside + high_side, 0.0))
        points[:, lanes_of(tile)] = centre + jnp.concatenate([place, jnp.zeros((5, 128), f32)], 0)
        charge = charge * inv_four_pi
        charges[2 * tile] = jnp.concatenate(split_two(charge), 0)
        charges[2 * tile + 1] = jnp.concatenate(split_two(pltpu.roll(charge, 64, 1)), 0)

    def stage_halo(halo, first):
        def step(i, carry):
            stage(first + i, halo[0:3, lanes_of(i)], halo[3:19, lanes_of(i)])
            return carry

        lax.fori_loop(0, halo_tiles, step, 0, unroll=2)

    def stage_own(i, carry):
        stage(halo_tiles + i, own_jitter[:, lanes_of(i)], own_charge[:, lanes_of(i)])
        return carry

    stage_halo(low_halo, 0)
    stage_halo(high_halo, halo_tiles + own_tiles)
    lax.fori_loop(0, own_tiles, stage_own, 0, unroll=16)

    def back(slot):
        total = lax.dot_general(
            kernels[slot], weights[slot], (((1,), (1,)), ((), ())), preferred_element_type=f32
        )
        total = jnp.transpose(total[:LEAF] + total[LEAF:])
        return total[:R] + total[R:]

    def emit(first):
        parts = [back(slot) for slot in range(BATCH)]
        first = jnp.maximum(first, 0)
        for half in range(BATCH // 2):
            place = pl.ds(pl.multiple_of((first + 2 * half) * LEAF, 128), 128)
            out[:, place] = jnp.concatenate([parts[2 * half], parts[2 * half + 1]], 1)

    def fill(group, feats, targets, part, part_count):
        base = group * GROUP
        across, beside = column_place(((first_id + NREACH) >> 2) + group * (GROUP // 4))
        row_sign = jnp.where((((first_id + NREACH + base) >> 8) & 1) == 0, 1.5, -1.5)
        shift = jnp.where(row == 0, across + row_sign, jnp.where(row == 1, beside + 1.5, 0.0))

        def local(tile):
            place = points[:, lanes_of(tile)] - shift
            square = place * place
            return place, jnp.broadcast_to(square[0:1] + square[1:2] + square[2:3], (8, 128))

        def source_rows(i):
            place, square = local(base // 2 + i)
            rows = place * (-2.0) + jnp.where(is_three, square + soft_square, one_four)

            def put(entry, value):
                first, second, third = split_three(value)
                one = jnp.where(below_five, first, pltpu.roll(second, 5, 0))
                two = jnp.where(is_three, second, one)
                three = jnp.where(below_five, third + one_four, pltpu.roll(first, 5, 0))
                feats[entry] = jnp.concatenate([one, two, three, jnp.zeros_like(one)], 0).astype(bf16)

            put(2 * i, rows)
            put(2 * i + 1, pltpu.roll(rows, 64, 1))

        def target_rows(i):
            place, square = local(base // 2 + NREACH // 2 + i)
            first, second, third = split_three(place + jnp.where(is_four, square, one_three))
            one = jnp.where(below_five, first, pltpu.roll(first, 5, 0))
            two = jnp.where(below_five, second + one_three, pltpu.roll(second, 5, 0))
            three = jnp.where(below_five, jnp.where(is_four, third, first), pltpu.roll(third, 5, 0))
            rows = jnp.concatenate([one, two, three, jnp.zeros_like(one)], 0)
            targets[lanes_of(i), :] = jnp.transpose(rows).astype(bf16)

        sources = (GROUP + 2 * NREACH) // 2 // part_count
        for i in range(sources):
            source_rows(part * sources + i)
        own = GROUP // 2 // part_count
        for i in range(own):
            target_rows(part * own + i)

    def front(base, leaf, slot, feats, targets):
        target = targets[pl.ds(pl.multiple_of(leaf * LEAF, LEAF), LEAF), :]
        entry = base + leaf
        for j in range(4):
            sides = []
            for h in range(2):
                one = ids[4 * j + 2 * h, entry] - first_id
                two = (ids[4 * j + 2 * h + 1, entry] - first_id) ^ 1
                sides.append(jnp.where(left_half, feats[one - base], feats[two - base]))
                weights[slot, :, (2 * j + h) * 128 : (2 * j + h + 1) * 128] = jnp.where(
                    left_half, charges[one], charges[two]
                )
            square = jnp.dot(target, jnp.concatenate(sides, 1), preferred_element_type=f32)
            high, low = split_two(lax.rsqrt(square))
            kernels[slot, 0:LEAF, j * 256 : (j + 1) * 256] = high
            kernels[slot, LEAF : 2 * LEAF, j * 256 : (j + 1) * 256] = low

    group_count = own_tiles * 2 // GROUP

    def do_two_groups(i, carry):
        for half in range(2):
            now = (feats0, targets0) if half == 0 else (feats1, targets1)
            later = (feats1, targets1) if half == 0 else (feats0, targets0)
            group = 2 * i + half
            following = jnp.minimum(group + 1, group_count - 1)

            def step(part, inner):
                emit(group * GROUP + BATCH * part - BATCH)
                for slot in range(BATCH):
                    front(group * GROUP, BATCH * part + slot, slot, *now)
                fill(following, *later, part, GROUP // BATCH)
                return inner

            lax.fori_loop(0, GROUP // BATCH, step, 0)
        return carry

    fill(0, feats0, targets0, 0, 1)
    lax.fori_loop(0, group_count // 2, do_two_groups, 0)
    emit(own_tiles * 2 - BATCH)


def near_potential(ids, own_jitter, own_charge, low_halo, high_halo):
    panels = own_jitter.shape[1]
    leaves = (panels + 2 * low_halo.shape[1]) // LEAF
    pairs = panels * 16 * LEAF
    vmem = pl.BlockSpec(memory_space=pltpu.VMEM)
    smem = pl.BlockSpec(memory_space=pltpu.SMEM)
    return pl.pallas_call(
        near_kernel,
        out_shape=jax.ShapeDtypeStruct((R, panels), f32),
        in_specs=[smem, vmem, vmem, vmem, vmem],
        out_specs=vmem,
        scratch_shapes=[
            pltpu.VMEM((8, leaves * LEAF), f32),
            pltpu.VMEM((GROUP + 2 * NREACH, 32, 128), bf16),
            pltpu.VMEM((GROUP + 2 * NREACH, 32, 128), bf16),
            pltpu.VMEM((leaves, 2 * R, 128), bf16),
            pltpu.VMEM((GROUP * LEAF, 32), bf16),
            pltpu.VMEM((GROUP * LEAF, 32), bf16),
            pltpu.VMEM((BATCH, 2 * LEAF, 16 * LEAF), bf16),
            pltpu.VMEM((BATCH, 2 * R, 16 * LEAF), bf16),
        ],
        compiler_params=pltpu.CompilerParams(vmem_limit_bytes=16 * 2**20),
        cost_estimate=pl.CostEstimate(
            flops=pairs * 192, bytes_accessed=panels * 160, transcendentals=pairs
        ),
        name="near_potential",
    )(ids, own_jitter, own_charge, low_halo, high_halo)


EDGE = 16
CHUNKS = 4
ROWS = R * K
WIDE = ROWS + 3 * K


def lane_digits(shape, dim):
    index = lax.broadcasted_iota(jnp.int32, shape, dim)
    return index >> 5, (index >> 3) & 3, index & 7


def lane_of_tile(tile):
    return (tile & 3) * 32 + ((tile >> 2) & 3) * 8 + (tile >> 4)


def matvec(matrix, vector, out, add, for_rows=4):

    def step(block, carry):
        start = pl.multiple_of(block * for_rows * K, for_rows * K)
        sums = [jnp.zeros((K, 128), f32) for _ in range(for_rows)]
        for column in range(K):
            values = matrix(column)
            for i in range(for_rows):
                sums[i] = sums[i] + values * vector[pl.ds(start + i * K + column, 1), :]
        for i in range(for_rows):
            place = pl.ds(start + i * K, K)
            out[place, :] = out[place, :] + sums[i] if add else sums[i]
        return carry

    lax.fori_loop(0, R // for_rows, step, 0)


def matvec_packed(matrix, vector, packed, out, add, shifts=()):
    block = lane_digits((1, 128), 1)[0]
    for i in range(4):
        value = vector[i * K : (i + 1) * K, :]
        for q in range(1, 4):
            value = jnp.where(block == q, vector[(4 * q + i) * K : (4 * q + i + 1) * K, :], value)
        packed[i * K : (i + 1) * K, :] = value
    sums = [jnp.zeros((K, 128), f32) for _ in range(4)]
    for column in range(K):
        values = matrix(column)
        for i in range(4):
            sums[i] = sums[i] + values * packed[i * K + column : i * K + column + 1, :]
    for i in range(4):
        for q in range(4):
            part = jnp.where(block == q, sums[i], 0.0)
            for shift in (32, 64) + tuple(shifts):
                part = part + pltpu.roll(part, shift, 1)
            place = slice((4 * q + i) * K, (4 * q + i + 1) * K)
            out[place, :] = out[place, :] + part if add else part


def fold(ref, shifts):
    def step(i, carry):
        place = pl.ds(pl.multiple_of(i * 64, 64), 64)
        value = ref[place, :]
        for shift in shifts:
            value = value + pltpu.roll(value, shift, 1)
        ref[place, :] = value
        return carry

    lax.fori_loop(0, ROWS // 64, step, 0)


def centre_lanes(ids, level_width):
    first = ids * level_width
    row_number = first >> 6
    middle = (first & (row_columns - 1)).astype(f32) + 0.5 * (level_width - 1)
    across = jnp.where((row_number & 1) == 0, middle, row_columns - 1 - middle)
    return across, 4.0 * row_number.astype(f32) + 1.5


def up_kernel(
    tops, basis_hbm, charge_hbm, trans0_hbm, trans1, trans2, trans3, prox1, prox2, prox3,
    et, payload, last_out, first_out, terms, leaf_rows, coef0, coef, flipped, columns, by_column, packed, basis, charge, trans0, sems,
):
    here = lax.axis_index("gx")
    quarter = lax.broadcasted_iota(jnp.int32, (R, 256), 1).astype(f32)

    def moments(tile, carry):
        lanes = pl.ds(pl.multiple_of(tile * 256, 256), 256)
        high, low = split_two(basis[:, lanes])
        right = jnp.concatenate([high, low, high], 1)
        value = charge[:, lanes]
        pieces = [
            split_two(jnp.where((quarter >= 64.0 * i) & (quarter < 64.0 * (i + 1)), value, 0.0))
            for i in range(4)
        ]
        highs = jnp.concatenate([p[0] for p in pieces], 0)
        lows = jnp.concatenate([p[1] for p in pieces], 0)
        left = jnp.concatenate([highs, highs, lows], 1)
        total = lax.dot_general(left, right, (((1,), (1,)), ((), ())), preferred_element_type=f32)
        total = jnp.concatenate([total, jnp.zeros((64, 128 - K), f32)], 1)
        leaf_rows[pl.ds(lane_of_tile(tile), 64, stride=128), :] = total
        return carry

    tiles = basis.shape[1] // 256
    chunk = basis.shape[1] // CHUNKS
    copies = []
    for i in range(CHUNKS):
        lanes = pl.ds(i * chunk, chunk)
        copies.append(pltpu.make_async_copy(basis_hbm.at[:, lanes], basis.at[:, lanes], sems.at[2 * i]))
        copies.append(pltpu.make_async_copy(charge_hbm.at[:, lanes], charge.at[:, lanes], sems.at[2 * i + 1]))
    copies.append(pltpu.make_async_copy(trans0_hbm, trans0, sems.at[2 * CHUNKS]))
    for copy in copies:
        copy.start()
    for i in range(CHUNKS):
        copies[2 * i].wait()
        copies[2 * i + 1].wait()
        lax.fori_loop(i * tiles // CHUNKS, (i + 1) * tiles // CHUNKS, moments, 0, unroll=8)
    copies[2 * CHUNKS].wait()

    def leaf_coefs(r, carry):
        place = pl.ds(pl.multiple_of(r * K, K), K)
        for j0 in range(4):
            rows = leaf_rows[pl.ds(pl.multiple_of((j0 * R + r) * 128, 128), 128), :]
            coef0[j0, place, :] = jnp.transpose(rows)[0:K]
        return carry

    lax.fori_loop(0, R, leaf_coefs, 0, unroll=4)

    def digits_first(q, rows):
        parts = [
            columns[q, pl.ds(rows[0] * a + rows[1] * b + rows[2], 8, stride=rows[3]), :]
            for a in range(4)
            for b in range(4)
        ]
        return jnp.transpose(jnp.concatenate(parts, 0))

    def flip(source, entries):
        for q in range(8):
            columns[q, 0 : source.shape[0], :] = source[:, q * 128 : (q + 1) * 128]
        for q in range(8):
            for entry, rows in entries:
                et[entry, q * 128 : (q + 1) * 128, :] = digits_first(q, rows)

    flip(trans0, [(j0, (4, 16, j0, 64)) for j0 in range(4)])
    flip(trans1, [(4, (1, 4, 0, 16))])
    flip(trans2, [(5, (0, 1, 0, 4))])
    flip(trans3, [(6, (0, 0, 0, 1))])

    def lift_from(entry, vector, out, add):
        for b in range(K):
            by_column[b * K : (b + 1) * K, :] = et[entry, pl.ds(b, K, stride=K), :]
        if entry < 5:
            matvec(lambda b: by_column[b * K : (b + 1) * K, :], vector, out, add)
        else:
            shifts = (8, 16) if entry == 5 else ()
            matvec_packed(lambda b: by_column[b * K : (b + 1) * K, :], vector, packed, out, add, shifts)

    for j0 in range(4):
        lift_from(j0, coef0.at[j0], coef.at[0], j0 > 0)
    lift_from(4, coef.at[0], coef.at[1], False)
    fold(coef.at[1], (32, 64))
    lift_from(5, coef.at[1], coef.at[2], False)
    lift_from(6, coef.at[2], coef.at[3], False)

    j1, j2, c3 = lane_digits((1, 128), 1)
    for level, (prox, ids, rows) in enumerate(
        (
            (prox1, c3 * 16 + j2 * 4 + j1 + here * 128, (1, 4, 0, 16)),
            (prox2, c3 * 4 + j2 + here * 32, (0, 1, 0, 4)),
            (prox3, c3 + here * 8, (0, 0, 0, 1)),
        )
    ):
        if level == 0:
            columns[level, 0:128, :] = jnp.transpose(
                jnp.concatenate([prox[...], jnp.zeros((128 - 3 * K, 128), f32)], 0)
            )
        else:
            columns[level, 0 : prox.shape[0], :] = jnp.concatenate(
                [prox[...], jnp.zeros((prox.shape[0], 128 - 3 * K), f32)], 1
            )
        offsets = digits_first(level, rows)
        across, beside = centre_lanes(ids, 4**level)
        payload[level, 0:ROWS, :] = coef[level]
        payload[level, ROWS : ROWS + K, :] = across + float(4**level) * offsets[0:K]
        payload[level, ROWS + K : ROWS + 2 * K, :] = beside + 4.0 * offsets[K : 2 * K]
        payload[level, ROWS + 2 * K : WIDE, :] = offsets[2 * K : 3 * K]

    def flip_payload(source, width):
        for q in range(0, width, 128):
            size = min(128, width - q)
            block = source[q : q + size, :]
            if size < 128:
                block = jnp.concatenate([block, jnp.zeros((128 - size, 128), f32)], 0)
            flipped[:, q : q + 128] = jnp.transpose(block)

    last_rows = ([31, 63, 95, 127], [7, 15, 23, 31], [4, 5, 6, 7])
    first_rows = ([0, 32, 64, 96], [0, 8, 16, 24], [0, 1, 2, 3])
    last_out[...] = jnp.zeros_like(last_out)
    first_out[...] = jnp.zeros_like(first_out)
    for level in range(3):
        flip_payload(payload.at[level], WIDE)
        for i in range(4):
            target = level * 4 + i
            last_out[target : target + 1, :] = flipped[last_rows[level][i] : last_rows[level][i] + 1, 0:WIDE]
            first_out[target : target + 1, :] = flipped[first_rows[level][i] : first_rows[level][i] + 1, 0:WIDE]
    flip_payload(coef.at[3], ROWS)
    top_ids = lax.broadcasted_iota(jnp.int32, terms.shape, 0)
    total = jnp.zeros(terms.shape, f32)
    for c in range(8):
        total = total + jnp.where(top_ids == tops[here * 8 + c], flipped[c : c + 1, 0:ROWS], 0.0)
    terms[...] = total


def upward_pass(tops, basis, charge, trans0, trans1, trans2, trans3, prox1, prox2, prox3, top_count):
    vmem = pl.BlockSpec(memory_space=pltpu.VMEM)
    leaves = trans0.shape[0]
    return pl.pallas_call(
        up_kernel,
        out_shape=[
            jax.ShapeDtypeStruct((7, K * K, 128), f32),
            jax.ShapeDtypeStruct((3, WIDE, 128), f32),
            jax.ShapeDtypeStruct((EDGE, WIDE), f32),
            jax.ShapeDtypeStruct((EDGE, WIDE), f32),
            jax.ShapeDtypeStruct((top_count, ROWS), f32),
        ],
        in_specs=[pl.BlockSpec(memory_space=pltpu.SMEM)] + [pl.BlockSpec(memory_space=pltpu.HBM)] * 3 + [vmem] * 6,
        out_specs=[vmem] * 5,
        scratch_shapes=[
            pltpu.VMEM((leaves * R, 128), f32),
            pltpu.VMEM((4, ROWS, 128), f32),
            pltpu.VMEM((4, ROWS, 128), f32),
            pltpu.VMEM((128, 640), f32),
            pltpu.VMEM((8, leaves, 128), f32),
            pltpu.VMEM((K * K, 128), f32),
            pltpu.VMEM((4 * K, 128), f32),
            pltpu.VMEM(basis.shape, f32),
            pltpu.VMEM(charge.shape, f32),
            pltpu.VMEM(trans0.shape, f32),
            pltpu.SemaphoreType.DMA((2 * CHUNKS + 1,)),
        ],
        compiler_params=pltpu.CompilerParams(vmem_limit_bytes=54 * 2**20),
        cost_estimate=pl.CostEstimate(
            flops=leaves * 200000, bytes_accessed=leaves * 20000, transcendentals=0
        ),
        name="upward_pass",
    )(tops, basis, charge, trans0, trans1, trans2, trans3, prox1, prox2, prox3)


def pick(ref, hot):
    hot = hot.astype(f32).astype(bf16)
    total = jnp.dot(ref[0], hot, preferred_element_type=f32)
    total = total + jnp.dot(ref[1], hot, preferred_element_type=f32)
    return total + jnp.dot(ref[2], hot, preferred_element_type=f32)


def couple_picked(gathered, green_rows, packed, target, out_ref, add, shifts=None):
    def step(b, carry):
        square = None
        for axis_id in range(3):
            spread = target(axis_id) - gathered[pl.ds(ROWS + axis_id * K + b, 1), :]
            square = spread * spread if square is None else square + spread * spread
        green_rows[pl.ds(pl.multiple_of(b * K, K), K), :] = inv_four_pi * lax.rsqrt(square + soft_square)
        return carry

    lax.fori_loop(0, K, step, 0, unroll=16)
    if shifts is None:
        matvec(lambda b: green_rows[b * K : (b + 1) * K, :], gathered, out_ref, add)
    else:
        matvec_packed(lambda b: green_rows[b * K : (b + 1) * K, :], gathered, packed, out_ref, add, shifts)


def couple_kernel(
    payload, low_halo, high_halo, list1, list2, list3, far, split_rows, gathered, green_rows, columns, packed
):
    here = lax.axis_index("gx")
    j1, j2, c3 = lane_digits((1, 128), 1)

    def split_to(ref, lanes, value):
        parts = split_three(value)
        for i in range(3):
            ref[i, :, lanes] = parts[i].astype(bf16)

    halo = jnp.concatenate([low_halo[...], high_halo[...], jnp.zeros((128 - 2 * EDGE, WIDE), f32)], 0)
    for w in range(0, WIDE, 128):
        size = min(128, WIDE - w)
        block = halo[:, w : w + size]
        if size < 128:
            block = jnp.concatenate([block, jnp.zeros((128, 128 - size), f32)], 1)
        parts = split_three(jnp.transpose(block))
        for i in range(3):
            split_rows[i, w : w + size, 128:256] = parts[i][0:size].astype(bf16)

    def lane_list(ref, rows, base):
        count = ref.shape[1]
        values = jnp.concatenate([(ref[...] - base).astype(f32), jnp.zeros((125, count), f32)], 0)
        if count < 128:
            values = jnp.concatenate([values, jnp.zeros((128, 128 - count), f32)], 1)
        columns[...] = jnp.transpose(values)
        parts = [
            columns[pl.ds(rows[0] * a + rows[1] * b, 8, stride=rows[2]), :] for a in range(4) for b in range(4)
        ]
        return jnp.transpose(jnp.concatenate(parts, 0)).astype(jnp.int32)

    source = lax.broadcasted_iota(jnp.int32, (256, 128), 0)
    edge = source - 128
    s1, s2, s3 = (source >> 5) & 3, (source >> 3) & 3, source & 7

    def source_ids(level, own, own_count, count):
        low = edge - 4 * level
        high = edge - EDGE - 4 * level
        ids = jnp.where(source < own_count, own, -1000)
        ids = jnp.where((low >= 0) & (low < 4), low - 4, ids)
        return jnp.where((high >= 0) & (high < 4), high + count, ids)

    def place_of(level):
        return lambda axis_id: payload[level, ROWS + axis_id * K : ROWS + (axis_id + 1) * K, :]

    picked = lane_list(list3, (0, 0, 1), here * 8)
    wanted = jnp.where(j2 == 0, picked[0:1], jnp.where(j2 == 1, picked[1:2], jnp.where(j2 == 2, picked[2:3], -5000)))
    split_to(split_rows, slice(0, 128), payload[2])
    gathered[...] = pick(split_rows, source_ids(2, s3, 8, 8) == wanted)
    couple_picked(gathered, green_rows, packed, place_of(2), far.at[2], False, (8, 16))

    picked = lane_list(list2, (0, 1, 4), here * 32)
    wanted = jnp.where(j1 == 0, picked[0:1], jnp.where(j1 == 1, picked[1:2], jnp.where(j1 == 2, picked[2:3], -5000)))
    split_to(split_rows, slice(0, 128), payload[1])
    gathered[...] = pick(split_rows, source_ids(1, s3 * 4 + s2, 32, 32) == wanted)
    couple_picked(gathered, green_rows, packed, place_of(1), far.at[1], False)
    fold(far.at[1], (32, 64))

    picked = lane_list(list1, (1, 4, 16), here * 128)
    split_to(split_rows, slice(0, 128), payload[0])
    ids = source_ids(0, s3 * 16 + s2 * 4 + s1, 128, 128)
    for j in range(3):
        gathered[...] = pick(split_rows, ids == picked[j : j + 1])
        couple_picked(gathered, green_rows, packed, place_of(0), far.at[0], j > 0)


def couplings(payload, low_halo, high_halo, list1, list2, list3):
    vmem = pl.BlockSpec(memory_space=pltpu.VMEM)
    return pl.pallas_call(
        couple_kernel,
        out_shape=jax.ShapeDtypeStruct((3, ROWS, 128), f32),
        in_specs=[vmem] * 6,
        out_specs=vmem,
        scratch_shapes=[
            pltpu.VMEM((3, WIDE, 256), bf16),
            pltpu.VMEM((WIDE, 128), f32),
            pltpu.VMEM((K * K, 128), f32),
            pltpu.VMEM((128, 128), f32),
            pltpu.VMEM((4 * K, 128), f32),
        ],
        compiler_params=pltpu.CompilerParams(vmem_limit_bytes=16 * 2**20),
        cost_estimate=pl.CostEstimate(flops=20000000, bytes_accessed=2000000, transcendentals=600000),
        name="couplings",
    )(payload, low_halo, high_halo, list1, list2, list3)


def down_kernel(
    tops, et_hbm, far, coef_top, prox_top, basis_hbm, near_hbm,
    out, split_top, split_place, gathered, green_rows, local, leaf_local, leaf_rows, packed,
    et, basis, near_field, sems,
):
    copies = [
        pltpu.make_async_copy(et_hbm, et, sems.at[0]),
        pltpu.make_async_copy(basis_hbm, basis, sems.at[1]),
        pltpu.make_async_copy(near_hbm, near_field, sems.at[2]),
    ]
    for copy in copies:
        copy.start()
    here = lax.axis_index("gx")
    top_count = prox_top.shape[0]
    j1, j2, c3 = lane_digits((1, 128), 1)

    def descend_from(entry, vector, out_ref, add):
        if entry < 5:
            matvec(lambda a: et[entry, a * K : (a + 1) * K, :], vector, out_ref, add)
        else:
            matvec_packed(lambda a: et[entry, a * K : (a + 1) * K, :], vector, packed, out_ref, add)

    my_top = jnp.zeros((1, 128), jnp.int32)
    for c in range(8):
        my_top = jnp.where(c3 == c, tops[here * 8 + c], my_top)
    def flip_top(block):
        rows, width = block.shape
        if width < 128:
            block = jnp.concatenate([block, jnp.zeros((rows, 128 - width), f32)], 1)
        if rows < 128:
            block = jnp.concatenate([block, jnp.zeros((128 - rows, 128), f32)], 0)
        return jnp.transpose(block)

    def keep(ref, first, q, value):
        parts = split_three(value)
        for i in range(3):
            ref[i, first : first + value.shape[0], q : q + 128] = parts[i].astype(bf16)

    for q in range(0, split_top.shape[2], 128):
        for w in range(0, ROWS, 128):
            keep(split_top, w, q, flip_top(coef_top[q : q + min(128, top_count - q), w : w + 128]))
        offsets = flip_top(prox_top[q : q + min(128, top_count - q), :])
        across, beside = centre_lanes(lax.broadcasted_iota(jnp.int32, (1, 128), 1) + q, 64)
        keep(split_place, 0, q, across + 64.0 * offsets[0:K])
        keep(split_place, K, q, beside + 4.0 * offsets[K : 2 * K])
        keep(split_place, 2 * K, q, offsets[2 * K : 3 * K])
    top_rows = lax.broadcasted_iota(jnp.int32, (split_place.shape[2], 128), 0)
    leaf_local[0, 0 : 3 * K, :] = pick(split_place, top_rows == my_top)
    lane_block = lax.broadcasted_iota(jnp.int32, (1, 128), 1) >> 3
    local[0] = jnp.zeros((ROWS, 128), f32)

    def top_block(block, carry):
        source = block * 16 + lane_block
        wanted = jnp.where(jnp.abs(source - my_top) >= 2, source, -1)
        gathered[0:ROWS, :] = pick(split_top, top_rows == wanted)
        gathered[ROWS:WIDE, :] = pick(split_place, top_rows == wanted)
        couple_picked(
            gathered, green_rows, packed,
            lambda axis_id: leaf_local[0, axis_id * K : (axis_id + 1) * K, :], local.at[0], True,
        )
        return carry

    lax.fori_loop(0, (top_count + 15) // 16, top_block, 0)
    fold(local.at[0], (8, 16, 32, 64))

    copies[0].wait()
    local[1] = far[2]
    descend_from(6, local.at[0], local.at[1], True)
    local[0] = far[1]
    descend_from(5, local.at[1], local.at[0], True)
    local[1] = far[0]
    descend_from(4, local.at[0], local.at[1], True)
    for j0 in range(4):
        descend_from(j0, local.at[1], leaf_local.at[j0], False)

    def leaf_terms(r, carry):
        place = pl.ds(pl.multiple_of(r * K, K), K)
        for j0 in range(4):
            high, low = split_two(leaf_local[j0, place, :])
            high, low = high.astype(f32), low.astype(f32)
            value = jnp.transpose(jnp.concatenate([high, high, low, jnp.zeros_like(low)], 0))
            for a in range(4):
                for b in range(4):
                    leaf_rows[pl.ds((b * 16 + a * 4 + j0) * R + r, 8, stride=64 * R), :] = value[
                        a * 32 + b * 8 : a * 32 + b * 8 + 8
                    ]
        return carry

    lax.fori_loop(0, R, leaf_terms, 0, unroll=2)
    half = lax.broadcasted_iota(jnp.int32, (R, 128), 1) < 64
    copies[1].wait()
    copies[2].wait()

    def potential(tile, carry):
        lanes = pl.ds(pl.multiple_of(tile * 256, 256), 256)
        high, low = split_two(basis[:, lanes])
        left = leaf_rows[pl.ds(pl.multiple_of(tile * 64, 64), 64), 0 : 3 * K].astype(bf16)
        total = jnp.dot(left, jnp.concatenate([high, low, high], 0), preferred_element_type=f32)
        one = jnp.where(half, total[0:16, 0:128], total[16:32, 0:128])
        two = jnp.where(half, total[32:48, 128:256], total[48:64, 128:256])
        out[:, lanes] = near_field[:, lanes] + jnp.concatenate([one, two], 1)
        return carry

    lax.fori_loop(0, basis.shape[1] // 256, potential, 0, unroll=8)


def downward_pass(
    tops, et, far, coef_top, prox_top, basis, near_field
):
    vmem = pl.BlockSpec(memory_space=pltpu.VMEM)
    smem = pl.BlockSpec(memory_space=pltpu.SMEM)
    panels = basis.shape[1]
    hbm = pl.BlockSpec(memory_space=pltpu.HBM)
    top_lanes = (prox_top.shape[0] + 127) // 128 * 128
    return pl.pallas_call(
        down_kernel,
        out_shape=jax.ShapeDtypeStruct((R, panels), f32),
        in_specs=[smem, hbm] + [vmem] * 3 + [hbm] * 2,
        out_specs=vmem,
        scratch_shapes=[
            pltpu.VMEM((3, ROWS, top_lanes), bf16),
            pltpu.VMEM((3, 3 * K, top_lanes), bf16),
            pltpu.VMEM((WIDE, 128), f32),
            pltpu.VMEM((K * K, 128), f32),
            pltpu.VMEM((2, ROWS, 128), f32),
            pltpu.VMEM((4, ROWS, 128), f32),
            pltpu.VMEM((panels // LEAF * R, 128), f32),
            pltpu.VMEM((4 * K, 128), f32),
            pltpu.VMEM(et.shape, f32),
            pltpu.VMEM(basis.shape, f32),
            pltpu.VMEM(near_field.shape, f32),
            pltpu.SemaphoreType.DMA((3,)),
        ],
        compiler_params=pltpu.CompilerParams(vmem_limit_bytes=54 * 2**20),
        cost_estimate=pl.CostEstimate(
            flops=panels * 4000, bytes_accessed=panels * 400, transcendentals=panels * 20
        ),
        name="downward_pass",
    )(
        tops, et, far, coef_top, prox_top, basis, near_field
    )


def body(
    charge, jitter, basis, near, trans0, trans1, trans2, trans3,
    prox1, prox2, prox3, prox_top, list1, list2, list3, top_of,
):
    count = lax.axis_size("gx")
    forward = [(i, i + 1) for i in range(count - 1)]
    backward = [(target, source) for source, target in forward]
    low_leaves, high_leaves = leaf_halos(jitter, charge)
    et, payload, last, first, terms = upward_pass(
        top_of, basis, charge, trans0, trans1, trans2, trans3, prox1.T, prox2, prox3, prox_top.shape[0]
    )
    low_halo = lax.ppermute(last, "gx", forward)
    high_halo = lax.ppermute(first, "gx", backward)
    coef_top = lax.psum(terms, "gx")
    near_field = near_potential(near.T, jitter, charge, low_leaves, high_leaves)
    near_field, low_halo, high_halo = lax.optimization_barrier((near_field, low_halo, high_halo))
    far = couplings(payload, low_halo, high_halo, list1.T, list2.T, list3.T)
    far, coef_top = lax.optimization_barrier((far, coef_top))
    return downward_pass(
        top_of, et, far, coef_top, prox_top, basis, near_field
    )


def solution(mesh):
    placed = (
        P(None, ("groups", "gx")),
        P(None, ("groups", "gx")),
        P(None, ("groups", "gx")),
        P(("groups", "gx"), None),
        P(("groups", "gx"), None),
        P(("groups", "gx"), None),
        P(("groups", "gx"), None),
        P(("groups", "gx"), None),
        P(("groups", "gx"), None),
        P(("groups", "gx"), None),
        P(("groups", "gx"), None),
        P("groups", None),
        P(("groups", "gx"), None),
        P(("groups", "gx"), None),
        P(("groups", "gx"), None),
        P("groups"),
    )
    return jax.shard_map(
        body, mesh=mesh, in_specs=placed, out_specs=P(None, ("groups", "gx")), check_vma=False
    )
```

```python
import jax
import jax.numpy as jnp
from jax import lax
from jax.experimental import pallas as pl
from jax.experimental.pallas import tpu as pltpu
from jax.sharding import PartitionSpec as P

LEAF = 64
K = 32
R = 16
NREACH = 16


inv_four_pi = 0.07957747154594767
soft_square = 0.01
row_columns = 64


def leaf_halos(jitter, charge):
    count = lax.axis_size("gx")
    forward = [(i, i + 1) for i in range(count - 1)]
    backward = [(target, source) for source, target in forward]
    width = NREACH * LEAF
    last = jnp.concatenate([jitter[:, -width:], charge[:, -width:]], axis=0)
    first = jnp.concatenate([jitter[:, :width], charge[:, :width]], axis=0)
    return lax.ppermute(last, "gx", forward), lax.ppermute(first, "gx", backward)


def column_place(column):
    row_number = column >> 6
    middle = column & (row_columns - 1)
    across = jnp.where((row_number & 1) == 0, middle, row_columns - 1 - middle)
    return across.astype(jnp.float32), (4 * row_number).astype(jnp.float32)


GROUP = 16
BATCH = 16
bf16 = jnp.bfloat16
f32 = jnp.float32


def split_two(value):
    high = value.astype(bf16)
    return high, (value - high.astype(f32)).astype(bf16)


def split_three(value):
    first = value.astype(bf16).astype(f32)
    rest = value - first
    second = rest.astype(bf16).astype(f32)
    return first, second, rest - second


def lanes_of(tile):
    return pl.ds(pl.multiple_of(tile * 128, 128), 128)


def near_kernel(
    ids, own_jitter, own_charge, low_halo, high_halo, out, points, feats0, feats1, charges, targets0, targets1, kernels, weights
):
    halo_tiles = low_halo.shape[1] // 128
    own_tiles = own_jitter.shape[1] // 128
    here = lax.axis_index("gx")
    first_id = here * (2 * own_tiles) - NREACH
    high_side = jnp.where(lax.broadcasted_iota(jnp.int32, (1, 128), 1) < LEAF, 0.0, 1.0)
    left_half = lax.broadcasted_iota(jnp.int32, (32, 128), 1).astype(bf16) < 64
    row = lax.broadcasted_iota(jnp.int32, (8, 128), 0)
    is_three = row == 3
    is_four = row == 4
    below_five = row < 5
    one_three = jnp.where(is_three, 1.0, 0.0)
    one_four = jnp.where(is_four, 1.0, 0.0)

    def stage(tile, place, charge):
        number = tile + (here * own_tiles - halo_tiles)
        across, beside = column_place(number >> 1)
        beside = beside + (2 * (number & 1)).astype(f32)
        centre = jnp.where(row == 0, across, jnp.where(row == 1, beside + high_side, 0.0))
        points[:, lanes_of(tile)] = centre + jnp.concatenate([place, jnp.zeros((5, 128), f32)], 0)
        charge = charge * inv_four_pi
        charges[2 * tile] = jnp.concatenate(split_two(charge), 0)
        charges[2 * tile + 1] = jnp.concatenate(split_two(pltpu.roll(charge, 64, 1)), 0)

    def stage_halo(halo, first):
        def step(i, carry):
            stage(first + i, halo[0:3, lanes_of(i)], halo[3:19, lanes_of(i)])
            return carry

        lax.fori_loop(0, halo_tiles, step, 0, unroll=2)

    def stage_own(i, carry):
        stage(halo_tiles + i, own_jitter[:, lanes_of(i)], own_charge[:, lanes_of(i)])
        return carry

    stage_halo(low_halo, 0)
    stage_halo(high_halo, halo_tiles + own_tiles)
    lax.fori_loop(0, own_tiles, stage_own, 0, unroll=16)

    def back(slot):
        total = lax.dot_general(
            kernels[slot], weights[slot], (((1,), (1,)), ((), ())), preferred_element_type=f32
        )
        total = jnp.transpose(total[:LEAF] + total[LEAF:])
        return total[:R] + total[R:]

    def emit(first):
        parts = [back(slot) for slot in range(BATCH)]
        first = jnp.maximum(first, 0)
        for half in range(BATCH // 2):
            place = pl.ds(pl.multiple_of((first + 2 * half) * LEAF, 128), 128)
            out[:, place] = jnp.concatenate([parts[2 * half], parts[2 * half + 1]], 1)

    def fill(group, feats, targets, part, part_count):
        base = group * GROUP
        across, beside = column_place(((first_id + NREACH) >> 2) + group * (GROUP // 4))
        row_sign = jnp.where((((first_id + NREACH + base) >> 8) & 1) == 0, 1.5, -1.5)
        shift = jnp.where(row == 0, across + row_sign, jnp.where(row == 1, beside + 1.5, 0.0))

        def local(tile):
            place = points[:, lanes_of(tile)] - shift
            square = place * place
            return place, jnp.broadcast_to(square[0:1] + square[1:2] + square[2:3], (8, 128))

        def source_rows(i):
            place, square = local(base // 2 + i)
            rows = place * (-2.0) + jnp.where(is_three, square + soft_square, one_four)

            def put(entry, value):
                first, second, third = split_three(value)
                one = jnp.where(below_five, first, pltpu.roll(second, 5, 0))
                two = jnp.where(is_three, second, one)
                three = jnp.where(below_five, third + one_four, pltpu.roll(first, 5, 0))
                feats[entry] = jnp.concatenate([one, two, three, jnp.zeros_like(one)], 0).astype(bf16)

            put(2 * i, rows)
            put(2 * i + 1, pltpu.roll(rows, 64, 1))

        def target_rows(i):
            place, square = local(base // 2 + NREACH // 2 + i)
            first, second, third = split_three(place + jnp.where(is_four, square, one_three))
            one = jnp.where(below_five, first, pltpu.roll(first, 5, 0))
            two = jnp.where(below_five, second + one_three, pltpu.roll(second, 5, 0))
            three = jnp.where(below_five, jnp.where(is_four, third, first), pltpu.roll(third, 5, 0))
            rows = jnp.concatenate([one, two, three, jnp.zeros_like(one)], 0)
            targets[lanes_of(i), :] = jnp.transpose(rows).astype(bf16)

        sources = (GROUP + 2 * NREACH) // 2 // part_count
        for i in range(sources):
            source_rows(part * sources + i)
        own = GROUP // 2 // part_count
        for i in range(own):
            target_rows(part * own + i)

    def front(base, leaf, slot, feats, targets):
        target = targets[pl.ds(pl.multiple_of(leaf * LEAF, LEAF), LEAF), :]
        entry = base + leaf
        for j in range(4):
            sides = []
            for h in range(2):
                one = ids[4 * j + 2 * h, entry] - first_id
                two = (ids[4 * j + 2 * h + 1, entry] - first_id) ^ 1
                sides.append(jnp.where(left_half, feats[one - base], feats[two - base]))
                weights[slot, :, (2 * j + h) * 128 : (2 * j + h + 1) * 128] = jnp.where(
                    left_half, charges[one], charges[two]
                )
            square = jnp.dot(target, jnp.concatenate(sides, 1), preferred_element_type=f32)
            high, low = split_two(lax.rsqrt(square))
            kernels[slot, 0:LEAF, j * 256 : (j + 1) * 256] = high
            kernels[slot, LEAF : 2 * LEAF, j * 256 : (j + 1) * 256] = low

    group_count = own_tiles * 2 // GROUP

    def do_two_groups(i, carry):
        for half in range(2):
            now = (feats0, targets0) if half == 0 else (feats1, targets1)
            later = (feats1, targets1) if half == 0 else (feats0, targets0)
            group = 2 * i + half
            following = jnp.minimum(group + 1, group_count - 1)

            def step(part, inner):
                emit(group * GROUP + BATCH * part - BATCH)
                for slot in range(BATCH):
                    front(group * GROUP, BATCH * part + slot, slot, *now)
                fill(following, *later, part, GROUP // BATCH)
                return inner

            lax.fori_loop(0, GROUP // BATCH, step, 0)
        return carry

    fill(0, feats0, targets0, 0, 1)
    lax.fori_loop(0, group_count // 2, do_two_groups, 0)
    emit(own_tiles * 2 - BATCH)


def near_potential(ids, own_jitter, own_charge, low_halo, high_halo):
    panels = own_jitter.shape[1]
    leaves = (panels + 2 * low_halo.shape[1]) // LEAF
    pairs = panels * 16 * LEAF
    vmem = pl.BlockSpec(memory_space=pltpu.VMEM)
    smem = pl.BlockSpec(memory_space=pltpu.SMEM)
    return pl.pallas_call(
        near_kernel,
        out_shape=jax.ShapeDtypeStruct((R, panels), f32),
        in_specs=[smem, vmem, vmem, vmem, vmem],
        out_specs=vmem,
        scratch_shapes=[
            pltpu.VMEM((8, leaves * LEAF), f32),
            pltpu.VMEM((GROUP + 2 * NREACH, 32, 128), bf16),
            pltpu.VMEM((GROUP + 2 * NREACH, 32, 128), bf16),
            pltpu.VMEM((leaves, 2 * R, 128), bf16),
            pltpu.VMEM((GROUP * LEAF, 32), bf16),
            pltpu.VMEM((GROUP * LEAF, 32), bf16),
            pltpu.VMEM((BATCH, 2 * LEAF, 16 * LEAF), bf16),
            pltpu.VMEM((BATCH, 2 * R, 16 * LEAF), bf16),
        ],
        compiler_params=pltpu.CompilerParams(vmem_limit_bytes=16 * 2**20),
        cost_estimate=pl.CostEstimate(
            flops=pairs * 192, bytes_accessed=panels * 160, transcendentals=pairs
        ),
        name="near_potential",
    )(ids, own_jitter, own_charge, low_halo, high_halo)


EDGE = 16
CHUNKS = 4
ROWS = R * K
WIDE = ROWS + 3 * K


def lane_digits(shape, dim):
    index = lax.broadcasted_iota(jnp.int32, shape, dim)
    return index >> 5, (index >> 3) & 3, index & 7


def lane_of_tile(tile):
    return (tile & 3) * 32 + ((tile >> 2) & 3) * 8 + (tile >> 4)


def matvec(matrix, vector, out, add, for_rows=4):

    def step(block, carry):
        start = pl.multiple_of(block * for_rows * K, for_rows * K)
        sums = [jnp.zeros((K, 128), f32) for _ in range(for_rows)]
        for column in range(K):
            values = matrix(column)
            for i in range(for_rows):
                sums[i] = sums[i] + values * vector[pl.ds(start + i * K + column, 1), :]
        for i in range(for_rows):
            place = pl.ds(start + i * K, K)
            out[place, :] = out[place, :] + sums[i] if add else sums[i]
        return carry

    lax.fori_loop(0, R // for_rows, step, 0)


def matvec_packed(matrix, vector, packed, out, add, shifts=()):
    block = lane_digits((1, 128), 1)[0]
    for i in range(4):
        value = vector[i * K : (i + 1) * K, :]
        for q in range(1, 4):
            value = jnp.where(block == q, vector[(4 * q + i) * K : (4 * q + i + 1) * K, :], value)
        packed[i * K : (i + 1) * K, :] = value
    sums = [jnp.zeros((K, 128), f32) for _ in range(4)]
    for column in range(K):
        values = matrix(column)
        for i in range(4):
            sums[i] = sums[i] + values * packed[i * K + column : i * K + column + 1, :]
    for i in range(4):
        for q in range(4):
            part = jnp.where(block == q, sums[i], 0.0)
            for shift in (32, 64) + tuple(shifts):
                part = part + pltpu.roll(part, shift, 1)
            place = slice((4 * q + i) * K, (4 * q + i + 1) * K)
            out[place, :] = out[place, :] + part if add else part


def fold(ref, shifts):
    def step(i, carry):
        place = pl.ds(pl.multiple_of(i * 64, 64), 64)
        value = ref[place, :]
        for shift in shifts:
            value = value + pltpu.roll(value, shift, 1)
        ref[place, :] = value
        return carry

    lax.fori_loop(0, ROWS // 64, step, 0)


def centre_lanes(ids, level_width):
    first = ids * level_width
    row_number = first >> 6
    middle = (first & (row_columns - 1)).astype(f32) + 0.5 * (level_width - 1)
    across = jnp.where((row_number & 1) == 0, middle, row_columns - 1 - middle)
    return across, 4.0 * row_number.astype(f32) + 1.5


def up_kernel(
    tops, basis_hbm, charge_hbm, trans0_hbm, trans1, trans2, trans3, prox1, prox2, prox3,
    et_hbm, payload, last_out, first_out, terms, leaf_rows, coef0, coef, flipped, columns, by_column, packed, basis, charge, trans0, et, sems,
):
    here = lax.axis_index("gx")
    quarter = lax.broadcasted_iota(jnp.int32, (R, 256), 1).astype(f32)

    def moments(tile, carry):
        lanes = pl.ds(pl.multiple_of(tile * 256, 256), 256)
        high, low = split_two(basis[:, lanes])
        right = jnp.concatenate([high, low, high], 1)
        value = charge[:, lanes]
        pieces = [
            split_two(jnp.where((quarter >= 64.0 * i) & (quarter < 64.0 * (i + 1)), value, 0.0))
            for i in range(4)
        ]
        highs = jnp.concatenate([p[0] for p in pieces], 0)
        lows = jnp.concatenate([p[1] for p in pieces], 0)
        left = jnp.concatenate([highs, highs, lows], 1)
        total = lax.dot_general(left, right, (((1,), (1,)), ((), ())), preferred_element_type=f32)
        total = jnp.concatenate([total, jnp.zeros((64, 128 - K), f32)], 1)
        leaf_rows[pl.ds(lane_of_tile(tile), 64, stride=128), :] = total
        return carry

    tiles = basis.shape[1] // 256
    chunk = basis.shape[1] // CHUNKS
    copies = []
    for i in range(CHUNKS):
        lanes = pl.ds(i * chunk, chunk)
        copies.append(pltpu.make_async_copy(basis_hbm.at[:, lanes], basis.at[:, lanes], sems.at[2 * i]))
        copies.append(pltpu.make_async_copy(charge_hbm.at[:, lanes], charge.at[:, lanes], sems.at[2 * i + 1]))
    copies.append(pltpu.make_async_copy(trans0_hbm, trans0, sems.at[2 * CHUNKS]))
    for copy in copies:
        copy.start()
    for i in range(CHUNKS):
        copies[2 * i].wait()
        copies[2 * i + 1].wait()
        lax.fori_loop(i * tiles // CHUNKS, (i + 1) * tiles // CHUNKS, moments, 0, unroll=8)
    copies[2 * CHUNKS].wait()

    def leaf_coefs(r, carry):
        place = pl.ds(pl.multiple_of(r * K, K), K)
        for j0 in range(4):
            rows = leaf_rows[pl.ds(pl.multiple_of((j0 * R + r) * 128, 128), 128), :]
            coef0[j0, place, :] = jnp.transpose(rows)[0:K]
        return carry

    lax.fori_loop(0, R, leaf_coefs, 0, unroll=4)

    def digits_first(q, rows):
        parts = [
            columns[q, pl.ds(rows[0] * a + rows[1] * b + rows[2], 8, stride=rows[3]), :]
            for a in range(4)
            for b in range(4)
        ]
        return jnp.transpose(jnp.concatenate(parts, 0))

    def flip(source, entries):
        for q in range(8):
            columns[q, 0 : source.shape[0], :] = source[:, q * 128 : (q + 1) * 128]
        for q in range(8):
            for entry, rows in entries:
                et[entry, q * 128 : (q + 1) * 128, :] = digits_first(q, rows)

    flip(trans0, [(j0, (4, 16, j0, 64)) for j0 in range(4)])
    flip(trans1, [(4, (1, 4, 0, 16))])
    flip(trans2, [(5, (0, 1, 0, 4))])
    flip(trans3, [(6, (0, 0, 0, 1))])
    give = pltpu.make_async_copy(et, et_hbm, sems.at[2 * CHUNKS + 1])
    give.start()

    def lift_from(entry, vector, out, add):
        if entry < 5:
            for b in range(K):
                by_column[b * K : (b + 1) * K, :] = et[entry, pl.ds(b, K, stride=K), :]
            matvec(lambda b: by_column[b * K : (b + 1) * K, :], vector, out, add)
        else:
            shifts = (8, 16) if entry == 5 else ()
            matvec_packed(lambda b: et[entry, pl.ds(b, K, stride=K), :], vector, packed, out, add, shifts)

    for j0 in range(4):
        lift_from(j0, coef0.at[j0], coef.at[0], j0 > 0)
    lift_from(4, coef.at[0], coef.at[1], False)
    fold(coef.at[1], (32, 64))
    lift_from(5, coef.at[1], coef.at[2], False)
    lift_from(6, coef.at[2], coef.at[3], False)

    j1, j2, c3 = lane_digits((1, 128), 1)
    for level, (prox, ids, rows) in enumerate(
        (
            (prox1, c3 * 16 + j2 * 4 + j1 + here * 128, (1, 4, 0, 16)),
            (prox2, c3 * 4 + j2 + here * 32, (0, 1, 0, 4)),
            (prox3, c3 + here * 8, (0, 0, 0, 1)),
        )
    ):
        if level == 0:
            columns[level, 0:128, :] = jnp.transpose(
                jnp.concatenate([prox[...], jnp.zeros((128 - 3 * K, 128), f32)], 0)
            )
        else:
            columns[level, 0 : prox.shape[0], :] = jnp.concatenate(
                [prox[...], jnp.zeros((prox.shape[0], 128 - 3 * K), f32)], 1
            )
        offsets = digits_first(level, rows)
        across, beside = centre_lanes(ids, 4**level)
        payload[level, 0:ROWS, :] = coef[level]
        payload[level, ROWS : ROWS + K, :] = across + float(4**level) * offsets[0:K]
        payload[level, ROWS + K : ROWS + 2 * K, :] = beside + 4.0 * offsets[K : 2 * K]
        payload[level, ROWS + 2 * K : WIDE, :] = offsets[2 * K : 3 * K]

    def flip_payload(source, width):
        for q in range(0, width, 128):
            size = min(128, width - q)
            block = source[q : q + size, :]
            if size < 128:
                block = jnp.concatenate([block, jnp.zeros((128 - size, 128), f32)], 0)
            flipped[:, q : q + 128] = jnp.transpose(block)

    last_rows = ([31, 63, 95, 127], [7, 15, 23, 31], [4, 5, 6, 7])
    first_rows = ([0, 32, 64, 96], [0, 8, 16, 24], [0, 1, 2, 3])
    last_out[...] = jnp.zeros_like(last_out)
    first_out[...] = jnp.zeros_like(first_out)
    for level in range(3):
        flip_payload(payload.at[level], WIDE)
        for i in range(4):
            target = level * 4 + i
            last_out[target : target + 1, :] = flipped[last_rows[level][i] : last_rows[level][i] + 1, 0:WIDE]
            first_out[target : target + 1, :] = flipped[first_rows[level][i] : first_rows[level][i] + 1, 0:WIDE]
    flip_payload(coef.at[3], ROWS)
    top_ids = lax.broadcasted_iota(jnp.int32, terms.shape, 0)
    total = jnp.zeros(terms.shape, f32)
    for c in range(8):
        total = total + jnp.where(top_ids == tops[here * 8 + c], flipped[c : c + 1, 0:ROWS], 0.0)
    terms[...] = total
    give.wait()


def upward_pass(tops, basis, charge, trans0, trans1, trans2, trans3, prox1, prox2, prox3, top_count):
    vmem = pl.BlockSpec(memory_space=pltpu.VMEM)
    leaves = trans0.shape[0]
    return pl.pallas_call(
        up_kernel,
        out_shape=[
            jax.ShapeDtypeStruct((7, K * K, 128), f32),
            jax.ShapeDtypeStruct((3, WIDE, 128), f32),
            jax.ShapeDtypeStruct((EDGE, WIDE), f32),
            jax.ShapeDtypeStruct((EDGE, WIDE), f32),
            jax.ShapeDtypeStruct((top_count, ROWS), f32),
        ],
        in_specs=[pl.BlockSpec(memory_space=pltpu.SMEM)] + [pl.BlockSpec(memory_space=pltpu.HBM)] * 3 + [vmem] * 6,
        out_specs=[pl.BlockSpec(memory_space=pltpu.HBM)] + [vmem] * 4,
        scratch_shapes=[
            pltpu.VMEM((leaves * R, 128), f32),
            pltpu.VMEM((4, ROWS, 128), f32),
            pltpu.VMEM((4, ROWS, 128), f32),
            pltpu.VMEM((128, 640), f32),
            pltpu.VMEM((8, leaves, 128), f32),
            pltpu.VMEM((K * K, 128), f32),
            pltpu.VMEM((4 * K, 128), f32),
            pltpu.VMEM(basis.shape, f32),
            pltpu.VMEM(charge.shape, f32),
            pltpu.VMEM(trans0.shape, f32),
            pltpu.VMEM((7, K * K, 128), f32),
            pltpu.SemaphoreType.DMA((2 * CHUNKS + 2,)),
        ],
        compiler_params=pltpu.CompilerParams(vmem_limit_bytes=54 * 2**20),
        cost_estimate=pl.CostEstimate(
            flops=leaves * 200000, bytes_accessed=leaves * 20000, transcendentals=0
        ),
        name="upward_pass",
    )(tops, basis, charge, trans0, trans1, trans2, trans3, prox1, prox2, prox3)


def pick(ref, hot):
    hot = hot.astype(f32).astype(bf16)
    total = jnp.dot(ref[0], hot, preferred_element_type=f32)
    total = total + jnp.dot(ref[1], hot, preferred_element_type=f32)
    return total + jnp.dot(ref[2], hot, preferred_element_type=f32)


def couple_picked(gathered, green_rows, packed, target, out_ref, add, shifts=None):
    def step(b, carry):
        square = None
        for axis_id in range(3):
            spread = target(axis_id) - gathered[pl.ds(ROWS + axis_id * K + b, 1), :]
            square = spread * spread if square is None else square + spread * spread
        green_rows[pl.ds(pl.multiple_of(b * K, K), K), :] = inv_four_pi * lax.rsqrt(square + soft_square)
        return carry

    lax.fori_loop(0, K, step, 0, unroll=16)
    if shifts is None:
        matvec(lambda b: green_rows[b * K : (b + 1) * K, :], gathered, out_ref, add)
    else:
        matvec_packed(lambda b: green_rows[b * K : (b + 1) * K, :], gathered, packed, out_ref, add, shifts)


def couple_kernel(
    payload, low_halo, high_halo, list1, list2, list3, far, split_rows, gathered, green_rows, columns, packed
):
    here = lax.axis_index("gx")
    j1, j2, c3 = lane_digits((1, 128), 1)

    def split_to(ref, lanes, value):
        parts = split_three(value)
        for i in range(3):
            ref[i, :, lanes] = parts[i].astype(bf16)

    halo = jnp.concatenate([low_halo[...], high_halo[...], jnp.zeros((128 - 2 * EDGE, WIDE), f32)], 0)
    for w in range(0, WIDE, 128):
        size = min(128, WIDE - w)
        block = halo[:, w : w + size]
        if size < 128:
            block = jnp.concatenate([block, jnp.zeros((128, 128 - size), f32)], 1)
        parts = split_three(jnp.transpose(block))
        for i in range(3):
            split_rows[i, w : w + size, 128:256] = parts[i][0:size].astype(bf16)

    def lane_list(ref, rows, base):
        count = ref.shape[1]
        values = jnp.concatenate([(ref[...] - base).astype(f32), jnp.zeros((125, count), f32)], 0)
        if count < 128:
            values = jnp.concatenate([values, jnp.zeros((128, 128 - count), f32)], 1)
        columns[...] = jnp.transpose(values)
        parts = [
            columns[pl.ds(rows[0] * a + rows[1] * b, 8, stride=rows[2]), :] for a in range(4) for b in range(4)
        ]
        return jnp.transpose(jnp.concatenate(parts, 0)).astype(jnp.int32)

    source = lax.broadcasted_iota(jnp.int32, (256, 128), 0)
    edge = source - 128
    s1, s2, s3 = (source >> 5) & 3, (source >> 3) & 3, source & 7

    def source_ids(level, own, own_count, count):
        low = edge - 4 * level
        high = edge - EDGE - 4 * level
        ids = jnp.where(source < own_count, own, -1000)
        ids = jnp.where((low >= 0) & (low < 4), low - 4, ids)
        return jnp.where((high >= 0) & (high < 4), high + count, ids)

    def place_of(level):
        return lambda axis_id: payload[level, ROWS + axis_id * K : ROWS + (axis_id + 1) * K, :]

    picked = lane_list(list3, (0, 0, 1), here * 8)
    wanted = jnp.where(j2 == 0, picked[0:1], jnp.where(j2 == 1, picked[1:2], jnp.where(j2 == 2, picked[2:3], -5000)))
    split_to(split_rows, slice(0, 128), payload[2])
    gathered[...] = pick(split_rows, source_ids(2, s3, 8, 8) == wanted)
    couple_picked(gathered, green_rows, packed, place_of(2), far.at[2], False, (8, 16))

    picked = lane_list(list2, (0, 1, 4), here * 32)
    wanted = jnp.where(j1 == 0, picked[0:1], jnp.where(j1 == 1, picked[1:2], jnp.where(j1 == 2, picked[2:3], -5000)))
    split_to(split_rows, slice(0, 128), payload[1])
    gathered[...] = pick(split_rows, source_ids(1, s3 * 4 + s2, 32, 32) == wanted)
    couple_picked(gathered, green_rows, packed, place_of(1), far.at[1], False)
    fold(far.at[1], (32, 64))

    picked = lane_list(list1, (1, 4, 16), here * 128)
    split_to(split_rows, slice(0, 128), payload[0])
    ids = source_ids(0, s3 * 16 + s2 * 4 + s1, 128, 128)
    for j in range(3):
        gathered[...] = pick(split_rows, ids == picked[j : j + 1])
        couple_picked(gathered, green_rows, packed, place_of(0), far.at[0], j > 0)


def couplings(payload, low_halo, high_halo, list1, list2, list3):
    vmem = pl.BlockSpec(memory_space=pltpu.VMEM)
    return pl.pallas_call(
        couple_kernel,
        out_shape=jax.ShapeDtypeStruct((3, ROWS, 128), f32),
        in_specs=[vmem] * 6,
        out_specs=vmem,
        scratch_shapes=[
            pltpu.VMEM((3, WIDE, 256), bf16),
            pltpu.VMEM((WIDE, 128), f32),
            pltpu.VMEM((K * K, 128), f32),
            pltpu.VMEM((128, 128), f32),
            pltpu.VMEM((4 * K, 128), f32),
        ],
        compiler_params=pltpu.CompilerParams(vmem_limit_bytes=16 * 2**20),
        cost_estimate=pl.CostEstimate(flops=20000000, bytes_accessed=2000000, transcendentals=600000),
        name="couplings",
    )(payload, low_halo, high_halo, list1, list2, list3)


def down_kernel(
    tops, et_hbm, far, coef_top, prox_top, basis_hbm, near_hbm,
    out, split_top, split_place, gathered, green_rows, local, leaf_local, leaf_rows, packed,
    et, basis, near_field, sems,
):
    copies = [
        pltpu.make_async_copy(et_hbm, et, sems.at[0]),
        pltpu.make_async_copy(basis_hbm, basis, sems.at[1]),
        pltpu.make_async_copy(near_hbm, near_field, sems.at[2]),
    ]
    for copy in copies:
        copy.start()
    here = lax.axis_index("gx")
    top_count = prox_top.shape[0]
    j1, j2, c3 = lane_digits((1, 128), 1)

    def descend_from(entry, vector, out_ref, add):
        if entry < 5:
            matvec(lambda a: et[entry, a * K : (a + 1) * K, :], vector, out_ref, add)
        else:
            matvec_packed(lambda a: et[entry, a * K : (a + 1) * K, :], vector, packed, out_ref, add)

    my_top = jnp.zeros((1, 128), jnp.int32)
    for c in range(8):
        my_top = jnp.where(c3 == c, tops[here * 8 + c], my_top)
    def flip_top(block):
        rows, width = block.shape
        if width < 128:
            block = jnp.concatenate([block, jnp.zeros((rows, 128 - width), f32)], 1)
        if rows < 128:
            block = jnp.concatenate([block, jnp.zeros((128 - rows, 128), f32)], 0)
        return jnp.transpose(block)

    def keep(ref, first, q, value):
        parts = split_three(value)
        for i in range(3):
            ref[i, first : first + value.shape[0], q : q + 128] = parts[i].astype(bf16)

    for q in range(0, split_top.shape[2], 128):
        for w in range(0, ROWS, 128):
            keep(split_top, w, q, flip_top(coef_top[q : q + min(128, top_count - q), w : w + 128]))
        offsets = flip_top(prox_top[q : q + min(128, top_count - q), :])
        across, beside = centre_lanes(lax.broadcasted_iota(jnp.int32, (1, 128), 1) + q, 64)
        keep(split_place, 0, q, across + 64.0 * offsets[0:K])
        keep(split_place, K, q, beside + 4.0 * offsets[K : 2 * K])
        keep(split_place, 2 * K, q, offsets[2 * K : 3 * K])
    top_rows = lax.broadcasted_iota(jnp.int32, (split_place.shape[2], 128), 0)
    leaf_local[0, 0 : 3 * K, :] = pick(split_place, top_rows == my_top)
    lane_block = lax.broadcasted_iota(jnp.int32, (1, 128), 1) >> 3
    local[0] = jnp.zeros((ROWS, 128), f32)

    def top_block(block, carry):
        source = block * 16 + lane_block
        wanted = jnp.where(jnp.abs(source - my_top) >= 2, source, -1)
        gathered[0:ROWS, :] = pick(split_top, top_rows == wanted)
        gathered[ROWS:WIDE, :] = pick(split_place, top_rows == wanted)
        couple_picked(
            gathered, green_rows, packed,
            lambda axis_id: leaf_local[0, axis_id * K : (axis_id + 1) * K, :], local.at[0], True,
        )
        return carry

    lax.fori_loop(0, (top_count + 15) // 16, top_block, 0)
    fold(local.at[0], (8, 16, 32, 64))

    copies[0].wait()
    local[1] = far[2]
    descend_from(6, local.at[0], local.at[1], True)
    local[0] = far[1]
    descend_from(5, local.at[1], local.at[0], True)
    local[1] = far[0]
    descend_from(4, local.at[0], local.at[1], True)
    for j0 in range(4):
        descend_from(j0, local.at[1], leaf_local.at[j0], False)

    def leaf_terms(r, carry):
        place = pl.ds(pl.multiple_of(r * K, K), K)
        for j0 in range(4):
            high, low = split_two(leaf_local[j0, place, :])
            high, low = high.astype(f32), low.astype(f32)
            value = jnp.transpose(jnp.concatenate([high, high, low, jnp.zeros_like(low)], 0))
            for a in range(4):
                for b in range(4):
                    leaf_rows[pl.ds((b * 16 + a * 4 + j0) * R + r, 8, stride=64 * R), :] = value[
                        a * 32 + b * 8 : a * 32 + b * 8 + 8
                    ]
        return carry

    lax.fori_loop(0, R, leaf_terms, 0, unroll=2)
    half = lax.broadcasted_iota(jnp.int32, (R, 128), 1) < 64
    copies[1].wait()
    copies[2].wait()

    def potential(tile, carry):
        lanes = pl.ds(pl.multiple_of(tile * 256, 256), 256)
        high, low = split_two(basis[:, lanes])
        left = leaf_rows[pl.ds(pl.multiple_of(tile * 64, 64), 64), 0 : 3 * K].astype(bf16)
        total = jnp.dot(left, jnp.concatenate([high, low, high], 0), preferred_element_type=f32)
        one = jnp.where(half, total[0:16, 0:128], total[16:32, 0:128])
        two = jnp.where(half, total[32:48, 128:256], total[48:64, 128:256])
        out[:, lanes] = near_field[:, lanes] + jnp.concatenate([one, two], 1)
        return carry

    lax.fori_loop(0, basis.shape[1] // 256, potential, 0, unroll=8)


def downward_pass(
    tops, et, far, coef_top, prox_top, basis, near_field
):
    vmem = pl.BlockSpec(memory_space=pltpu.VMEM)
    smem = pl.BlockSpec(memory_space=pltpu.SMEM)
    panels = basis.shape[1]
    hbm = pl.BlockSpec(memory_space=pltpu.HBM)
    top_lanes = (prox_top.shape[0] + 127) // 128 * 128
    return pl.pallas_call(
        down_kernel,
        out_shape=jax.ShapeDtypeStruct((R, panels), f32),
        in_specs=[smem, hbm] + [vmem] * 3 + [hbm] * 2,
        out_specs=vmem,
        scratch_shapes=[
            pltpu.VMEM((3, ROWS, top_lanes), bf16),
            pltpu.VMEM((3, 3 * K, top_lanes), bf16),
            pltpu.VMEM((WIDE, 128), f32),
            pltpu.VMEM((K * K, 128), f32),
            pltpu.VMEM((2, ROWS, 128), f32),
            pltpu.VMEM((4, ROWS, 128), f32),
            pltpu.VMEM((panels // LEAF * R, 128), f32),
            pltpu.VMEM((4 * K, 128), f32),
            pltpu.VMEM(et.shape, f32),
            pltpu.VMEM(basis.shape, f32),
            pltpu.VMEM(near_field.shape, f32),
            pltpu.SemaphoreType.DMA((3,)),
        ],
        compiler_params=pltpu.CompilerParams(vmem_limit_bytes=54 * 2**20),
        cost_estimate=pl.CostEstimate(
            flops=panels * 4000, bytes_accessed=panels * 400, transcendentals=panels * 20
        ),
        name="downward_pass",
    )(
        tops, et, far, coef_top, prox_top, basis, near_field
    )


def body(
    charge, jitter, basis, near, trans0, trans1, trans2, trans3,
    prox1, prox2, prox3, prox_top, list1, list2, list3, top_of,
):
    count = lax.axis_size("gx")
    forward = [(i, i + 1) for i in range(count - 1)]
    backward = [(target, source) for source, target in forward]
    low_leaves, high_leaves = leaf_halos(jitter, charge)
    et, payload, last, first, terms = upward_pass(
        top_of, basis, charge, trans0, trans1, trans2, trans3, prox1.T, prox2, prox3, prox_top.shape[0]
    )
    low_halo = lax.ppermute(last, "gx", forward)
    high_halo = lax.ppermute(first, "gx", backward)
    coef_top = lax.psum(terms, "gx")
    near_field = near_potential(near.T, jitter, charge, low_leaves, high_leaves)
    near_field, low_halo, high_halo = lax.optimization_barrier((near_field, low_halo, high_halo))
    far = couplings(payload, low_halo, high_halo, list1.T, list2.T, list3.T)
    far, coef_top = lax.optimization_barrier((far, coef_top))
    return downward_pass(
        top_of, et, far, coef_top, prox_top, basis, near_field
    )


def solution(mesh):
    placed = (
        P(None, ("groups", "gx")),
        P(None, ("groups", "gx")),
        P(None, ("groups", "gx")),
        P(("groups", "gx"), None),
        P(("groups", "gx"), None),
        P(("groups", "gx"), None),
        P(("groups", "gx"), None),
        P(("groups", "gx"), None),
        P(("groups", "gx"), None),
        P(("groups", "gx"), None),
        P(("groups", "gx"), None),
        P("groups", None),
        P(("groups", "gx"), None),
        P(("groups", "gx"), None),
        P(("groups", "gx"), None),
        P("groups"),
    )
    return jax.shard_map(
        body, mesh=mesh, in_specs=placed, out_specs=P(None, ("groups", "gx")), check_vma=False
    )
```
